32 devices in a mesh: dp: 4 (over x, core), fsdp: 8 (over z, y).
Axes of the slice: x: 2, y: 2, z: 4, core: 2. Of those that a mesh axis runs over, the one named last changes fastest.
Arguments:
- tokens: bfloat16 [65536, 768], P(('dp', 'fsdp')), may hold values from -6 to 6
- masked: int32 [65536], P(('dp', 'fsdp')), may hold values 0 or 1
- replace_ids: int32 [65536], P(('dp', 'fsdp')), may hold values from 0 to 1023
- in_weight: bfloat16 [768, 1536], P(('dp', 'fsdp')), may hold values from -0.21875 to 0.21875
- depth_weight: bfloat16 [9, 768], P(None, ('dp', 'fsdp')), may hold values from -2 to 2
- point_weight: bfloat16 [768, 384], P(('dp', 'fsdp')), may hold values from -0.21875 to 0.21875
- kernel_weight: bfloat16 [384, 54], P('fsdp'), may hold values from -0.3125 to 0.3125
- out_weight: bfloat16 [768, 768], P(('dp', 'fsdp')), may hold values from -0.875 to 0.875
- gain_one: bfloat16 [768], P(('dp', 'fsdp')), may hold values from 0.099609375 to 1.8984375
- shift_one: bfloat16 [768], P(('dp', 'fsdp')), may hold values from -3 to 3
- ffn_in: bfloat16 [2, 384, 1536], P(None, None, ('dp', 'fsdp')), may hold values from -0.3125 to 0.3125
- feedforward_output: bfloat16 [2, 1536, 384], P(None, ('dp', 'fsdp')), may hold values from -0.15625 to 0.15625
- gain_two: bfloat16 [768], P(('dp', 'fsdp')), may hold values from 0.099609375 to 1.8984375
- shift_two: bfloat16 [768], P(('dp', 'fsdp')), may hold values from -3 to 3
- cotangent: bfloat16 [65536, 768], P(('dp', 'fsdp')), may hold values from -6 to 6
Outputs:
- layer_out: bfloat16 [65536, 768], P(('dp', 'fsdp'))
- grad_tokens: float32 [65536, 768], P(('dp', 'fsdp'))
- grad_in_weight: float32 [768, 1536], P(('dp', 'fsdp'))
- grad_depth_weight: float32 [9, 768], P(None, ('dp', 'fsdp'))
- grad_point_weight: float32 [768, 384], P(('dp', 'fsdp'))
- grad_kernel_weight: float32 [384, 54], P('fsdp')
- grad_out_weight: float32 [768, 768], P(('dp', 'fsdp'))
- grad_gain_one: float32 [768], P(('dp', 'fsdp'))
- grad_shift_one: float32 [768], P(('dp', 'fsdp'))
- grad_ffn_in: float32 [2, 384, 1536], P(None, None, ('dp', 'fsdp'))
- grad_ffn_out: float32 [2, 1536, 384], P(None, ('dp', 'fsdp'))
- grad_gain_two: float32 [768], P(('dp', 'fsdp'))
- grad_shift_two: float32 [768], P(('dp', 'fsdp'))
The draws below stay inside these ranges and needn't reach their ends.
Inputs may be any that keep to these rules, and one draw needn't show every extreme that they name: 1 marks a masked token. `replace_ids`: a position within the same sequence.
All inputs are finite; a program needn't handle non-finite values. No bound on the sum of `masked` on one device may be relied on, other than what follows from the above.
Results may differ from the reference program's by a relative error of at most 0.014.
Values may be sent and summed in bfloat16 or wider, within the bound.
No kernel may reach another device: no remote copies, remote signals or barrier semaphores. Data moves between devices by JAX's collectives and lax.ppermute only.
A program may use at most 256 MiB of HBM per device.

```python
import math
import jax
import jax.numpy as jnp
from jax import lax

MODEL_DIM = 768
HEADS = 6
HEAD = 64
ATT = 384
KER = 9
GROUPS = 2
DG = 384
FFG = 1536
SEQUENCE_TOKENS = 1024
TOKENS = 65536


def plant(entries, key, low, high):
    longest = entries.shape.index(max(entries.shape))
    spots = []
    for shift in (0, 1):
        where = [jax.random.randint(jax.random.fold_in(key, axis), (), 0, length) for axis, length in enumerate(entries.shape)]
        where[longest] = (where[longest] + shift) % entries.shape[longest]
        spots.append(tuple(where))
    return entries.at[spots[0]].set(low).at[spots[1]].set(high)


def with_spikes(values, key, source, target, blocks, factor):
    owner, partner = [(jnp.arange(values.shape[position]) // (values.shape[position] // blocks)).reshape([-1 if axis == position else 1 for axis in range(values.ndim)]) for position in (source, target)]
    chosen = jax.random.permutation(key, blocks)[partner]
    strong = (owner == chosen) | (owner == (partner + blocks // 2) % blocks)
    return jnp.where(strong, factor * values, values)


def steps_of(rng, shape, shards, least, high):
    def one(position, blocks):
        steps = jax.random.uniform(jax.random.fold_in(jax.random.fold_in(rng, 6), position), (blocks,), jnp.float32, least / len(shards), high / len(shards))
        return jnp.repeat(jnp.exp(steps), shape[position] // blocks).reshape((-1,) + (1,) * (len(shape) - position - 1))

    level = one(*shards[0])
    for cut in shards[1:]:
        level = level * one(*cut)
    return level


def scatter_about(rng, extent, scale, reach, shards=(), held_as=jnp.bfloat16):
    values = jax.random.normal(rng, extent, jnp.float32) * scale
    if len(shards) > 0:
        values = steps_of(rng, extent, shards, -0.22, 0.18) * values
    return jnp.clip(values, min=-reach, max=reach).astype(held_as)


def noise_with(stream_key, shape, scale, bound, split, heavy, kind=jnp.bfloat16):
    array = scale * jax.random.normal(stream_key, shape, jnp.float32)
    if split:
        array = array * steps_of(stream_key, shape, split, -0.22, 0.18)
    return jnp.clip(with_spikes(array, jax.random.fold_in(stream_key, 3), *heavy), -bound, bound).astype(kind)


def setup_inputs(seed: int = 0) -> dict:
    key_list = jax.random.split(jax.random.key(seed), 16)
    tokens = noise_with(key_list[0], (TOKENS, MODEL_DIM), 1.0, 6.0, ((0, 32),), (0, 1, 32, 2.75))
    masked = plant((jax.random.randint(key_list[1], (TOKENS,), 0, 20) < 3).astype(jnp.int32), jax.random.fold_in(key_list[1], 1), 0, 1)
    replace_ids = plant(jax.random.randint(key_list[2], (TOKENS,), 0, SEQUENCE_TOKENS), jax.random.fold_in(key_list[2], 1), 0, SEQUENCE_TOKENS - 1).astype(jnp.int32)
    in_weight = scatter_about(key_list[3], (MODEL_DIM, 4 * ATT), MODEL_DIM ** -0.5, 0.21875, ((0, 32),))
    depth_weight = scatter_about(key_list[4], (KER, MODEL_DIM), KER ** -0.5, 2.0, ((1, 32),))
    point_weight = scatter_about(key_list[5], (MODEL_DIM, ATT), MODEL_DIM ** -0.5, 0.21875, ((0, 32),))
    kernel_weight = scatter_about(key_list[6], (ATT, HEADS * KER), ATT ** -0.5, 0.3125, ((0, 8),))
    out_weight = scatter_about(key_list[7], (MODEL_DIM, MODEL_DIM), (MODEL_DIM // 16) ** -0.5, 0.875, ((0, 32),))
    gain_one = jnp.clip(1.0 + 0.18 * jax.random.normal(key_list[8], (MODEL_DIM,), jnp.float32), 0.099609375, 1.8984375).astype(jnp.bfloat16)
    shift_one = scatter_about(key_list[9], (MODEL_DIM,), 0.2, 3.0, ((0, 32),))
    ffn_in = scatter_about(key_list[10], (GROUPS, DG, FFG), DG ** -0.5, 0.3125, ((2, 32),))
    feedforward_output = scatter_about(key_list[11], (GROUPS, FFG, DG), FFG ** -0.5, 0.15625, ((1, 32),))
    gain_two = jnp.clip(1.0 + 0.18 * jax.random.normal(key_list[12], (MODEL_DIM,), jnp.float32), 0.099609375, 1.8984375).astype(jnp.bfloat16)
    shift_two = scatter_about(key_list[13], (MODEL_DIM,), 0.2, 3.0, ((0, 32),))
    cotangent = noise_with(key_list[14], (TOKENS, MODEL_DIM), 1.0, 6.0, ((0, 32),), (0, 1, 32, 2.75))
    return {"tokens": tokens, "masked": masked, "replace_ids": replace_ids, "in_weight": in_weight, "depth_weight": depth_weight, "point_weight": point_weight, "kernel_weight": kernel_weight, "out_weight": out_weight, "gain_one": gain_one, "shift_one": shift_one, "ffn_in": ffn_in, "feedforward_output": feedforward_output, "gain_two": gain_two, "shift_two": shift_two, "cotangent": cotangent}


@jax.custom_vjp
def low(v):
    return lax.optimization_barrier(v.astype(jnp.bfloat16)).astype(jnp.float32)

@jax.custom_vjp
def low_back(v):
    return v

def low_keep(v):
    return (low(v), None)

def low_pass(kept, grad):
    return (grad,)

def back_keep(v):
    return (v, None)

def back_low(kept, grad):
    return (low(grad),)
low.defvjp(low_keep, low_pass)
low_back.defvjp(back_keep, back_low)

def matmul(left, right):
    return jnp.dot(left, right, precision=lax.Precision.HIGHEST)

def round_both(values):
    return low_back(low(values))

def norm_rows(field_in, gain_vec, shift_vec):
    mean_rows = lax.optimization_barrier(jnp.mean(field_in, -1, keepdims=True))
    centred = field_in - mean_rows
    variance = lax.optimization_barrier(jnp.mean(centred * centred, -1, keepdims=True))
    return centred * lax.rsqrt(variance + 1e-12) * gain_vec + shift_vec

def depthwise(field_in, tap_weights):
    kernel_len = tap_weights.shape[0]
    half_span = kernel_len // 2
    length_rows = field_in.shape[-2]
    pads = ((0, 0),) * (field_in.ndim - 2) + ((half_span, half_span), (0, 0))
    padded = jnp.pad(field_in, pads)
    summed = jnp.zeros_like(field_in)
    for offset in range(kernel_len):
        summed = summed + tap_weights[offset] * padded[..., offset:offset + length_rows, :]
    return summed

def dynamic_conv(logits, values, head_count):
    kernels = jax.nn.softmax(logits.reshape(logits.shape[:-1] + (head_count, -1)), axis=-1)
    kernel_len = kernels.shape[-1]
    half_span = kernel_len // 2
    length_rows = values.shape[-2]
    split_heads = values.reshape(values.shape[:-1] + (head_count, -1))
    pads = ((0, 0),) * (split_heads.ndim - 3) + ((half_span, half_span), (0, 0), (0, 0))
    padded = jnp.pad(split_heads, pads)
    summed = jnp.zeros_like(split_heads)
    for offset in range(kernel_len):
        summed = summed + kernels[..., offset:offset + 1] * padded[..., offset:offset + length_rows, :, :]
    return summed.reshape(values.shape)

def attend(queries, key_rows, value_rows):
    query_heads = queries.reshape(SEQUENCE_TOKENS, HEADS, HEAD)
    key_heads = key_rows.reshape(SEQUENCE_TOKENS, HEADS, HEAD)
    value_heads = value_rows.reshape(SEQUENCE_TOKENS, HEADS, HEAD)
    raw_scores = jnp.einsum('qhd,khd->hqk', query_heads, key_heads, precision=lax.Precision.HIGHEST)
    scores = low_back(raw_scores * (1.0 / math.sqrt(HEAD)))
    soft = jax.nn.softmax(scores, axis=-1)
    mixed_heads = jnp.einsum('hqk,khd->qhd', low(soft), value_heads, precision=lax.Precision.HIGHEST)
    return mixed_heads.reshape(SEQUENCE_TOKENS, ATT)

def layer_rows(token_rows, mask_row, pick_row, in_weight, depth_weight, point_weight, kernel_weight, out_weight, gain_one, shift_one, ffn_in, feedforward_output, gain_two, shift_two):
    chosen = jnp.take(token_rows, pick_row, axis=0)
    inputs = jnp.where((mask_row == 1)[:, None], chosen, token_rows)
    projected = round_both(matmul(inputs, in_weight))
    queries = projected[:, :ATT]
    key_rows = projected[:, ATT:2 * ATT]
    value_rows = projected[:, 2 * ATT:3 * ATT]
    conv_values = projected[:, 3 * ATT:]
    spread = low(depthwise(inputs, depth_weight))
    conv_keys = round_both(matmul(spread, point_weight))
    kernel_logits = low_back(matmul(low(conv_keys * queries), kernel_weight))
    conv_out = dynamic_conv(kernel_logits, conv_values, HEADS)
    attended = attend(queries, key_rows, value_rows)
    context = round_both(jnp.concatenate([attended, conv_out], -1))
    first = norm_rows(low_back(matmul(context, out_weight)) + inputs, gain_one, shift_one)
    grouped = low(first).reshape(SEQUENCE_TOKENS, GROUPS, DG)
    inner = low_back(jnp.einsum('ngc,gcf->ngf', grouped, ffn_in, precision=lax.Precision.HIGHEST))
    active_hidden = low(jax.nn.gelu(inner, approximate=False))
    outer_hidden = low_back(jnp.einsum('tza,zah->tzh', active_hidden, feedforward_output, precision=lax.Precision.HIGHEST)).reshape(SEQUENCE_TOKENS, MODEL_DIM)
    return norm_rows(outer_hidden + first, gain_two, shift_two)

def reference(tokens, masked, replace_ids, in_weight, depth_weight, point_weight, kernel_weight, out_weight, gain_one, shift_one, ffn_in, feedforward_output, gain_two, shift_two, cotangent):
    params = tuple((weight_arg.astype(jnp.float32) for weight_arg in (in_weight, depth_weight, point_weight, kernel_weight, out_weight, gain_one, shift_one, ffn_in, feedforward_output, gain_two, shift_two)))
    mask_rows = masked.reshape(-1, SEQUENCE_TOKENS)
    pick_rows = replace_ids.reshape(-1, SEQUENCE_TOKENS)

    def forward(token_rows, *weights):

        def one_sequence(sequence):
            return layer_rows(sequence[0], sequence[1], sequence[2], *weights)
        return lax.map(jax.checkpoint(one_sequence), (token_rows, mask_rows, pick_rows))
    result, pullback = jax.vjp(forward, tokens.astype(jnp.float32).reshape(-1, SEQUENCE_TOKENS, MODEL_DIM), *params)
    gradients = pullback(cotangent.astype(jnp.float32).reshape(-1, SEQUENCE_TOKENS, MODEL_DIM))
    grad_scale = 1.0 / math.sqrt(TOKENS)
    return (result.reshape(TOKENS, MODEL_DIM).astype(jnp.bfloat16), gradients[0].reshape(TOKENS, MODEL_DIM), gradients[1] * grad_scale, gradients[2] * grad_scale, gradients[3] * grad_scale, gradients[4] * grad_scale, gradients[5] * grad_scale, gradients[6] * grad_scale, gradients[7] * grad_scale, gradients[8] * grad_scale, gradients[9] * grad_scale, gradients[10] * grad_scale, gradients[11] * grad_scale)
```

```python
from functools import partial
import math

import jax
import jax.numpy as jnp
from jax import lax
from jax.experimental import pallas as pl
from jax.experimental.pallas import tpu as pltpu
from jax.sharding import PartitionSpec as P

BF = jnp.bfloat16
F32 = jnp.float32
HEADS = 6
HEAD = 64
SEQ = 1024
KER = 9
ATT = HEADS * HEAD
WIDTH = 768
VMEM_MAX = 60 * 1024 * 1024


def mm(a, b):
    return jnp.dot(a, b, preferred_element_type=F32)


def mm_nt(a, b):
    return lax.dot_general(a, b, (((1,), (1,)), ((), ())), preferred_element_type=F32)


def mm_tn(a, b):
    return lax.dot_general(a, b, (((0,), (0,)), ((), ())), preferred_element_type=F32)


def params(count):
    return pltpu.CompilerParams(
        dimension_semantics=("arbitrary",) * count, vmem_limit_bytes=VMEM_MAX
    )


def whole(shape):
    zeros = (0,) * len(shape)
    return pl.BlockSpec(shape, lambda *_: zeros, pipeline_mode=pl.Buffered(1))


def whole_out(shape):
    zeros = (0,) * len(shape)
    return pl.BlockSpec(shape, lambda *_: zeros)


def lane_groups(x, combine):
    for step in (64, 32, 16, 8):
        x = combine(x, pltpu.roll(x, step, 1))
    return x


def tap_spread(block):
    rows = lax.broadcasted_iota(jnp.int32, (128, KER * 128), 0)
    cols = lax.broadcasted_iota(jnp.int32, (128, KER * 128), 1)
    want = (cols // 128) * 8 + block * 2 + (cols % 128) // HEAD
    return (rows == want).astype(F32).astype(BF)


CH = 256
HALO = CH + 16


def enter_kernel(
    pick_ref, tok_ref, w_in_ref, w_depth_ref, w_point_ref, w_kern_ref,
    inp_ref, proj_ref, spread_ref, ck_ref, kern_ref, conv_ref,
    x_pad, cv_pad,
):
    x_pad[0:8, :] = jnp.zeros((8, WIDTH), F32)
    x_pad[SEQ + 8 : SEQ + 16, :] = jnp.zeros((8, WIDTH), F32)
    cv_pad[0:8, :] = jnp.zeros((8, ATT), F32)
    cv_pad[SEQ + 8 : SEQ + 16, :] = jnp.zeros((8, ATT), F32)

    def load(i, carry):
        r = pl.multiple_of(i * CH, CH)
        pick = pick_ref[pl.ds(r, CH), :]
        cols = lax.broadcasted_iota(jnp.int32, (CH, SEQ), 1)
        hot = (cols == pick).astype(F32).astype(BF)
        rows = mm(hot, tok_ref[...])
        x_pad[pl.ds(r + 8, CH), :] = rows
        low = rows.astype(BF)
        inp_ref[pl.ds(r, CH), :] = low
        proj = mm(low, w_in_ref[...])
        proj_low = proj.astype(BF)
        proj_ref[pl.ds(r, CH), :] = proj_low
        cv_pad[pl.ds(r + 8, CH), :] = proj_low[:, 3 * ATT :].astype(F32)
        return carry

    lax.fori_loop(0, SEQ // CH, load, 0)

    def conv(i, carry):
        r = pl.multiple_of(i * CH, CH)
        for b in range(WIDTH // 128):
            lanes = slice(b * 128, (b + 1) * 128)
            xs = x_pad[pl.ds(r, HALO), lanes]
            shifted = [xs] + [pltpu.roll(xs, HALO - s, 0) for s in (1, 2, 3)]
            tap = lambda j: w_depth_ref[j : j + 1, lanes]
            low_part = sum(tap(s) * shifted[s] for s in range(4))
            mid_part = sum(tap(4 + s) * shifted[s] for s in range(4))
            high_part = tap(8) * xs
            low_part = pltpu.roll(low_part, HALO - 4, 0)
            high_part = pltpu.roll(high_part, HALO - 4, 0)
            total = low_part[0:CH] + mid_part[8 : 8 + CH] + high_part[8 : 8 + CH]
            spread_ref[pl.ds(r, CH), lanes] = total.astype(BF)
        ck = mm(spread_ref[pl.ds(r, CH), :], w_point_ref[...]).astype(BF)
        ck_ref[pl.ds(r, CH), :] = ck
        q = proj_ref[pl.ds(r, CH), 0:ATT].astype(F32)
        mixed = (ck.astype(F32) * q).astype(BF)
        logits = mm(mixed, w_kern_ref[...])
        lane = lax.broadcasted_iota(jnp.int32, (CH, 128), 1)
        logits = jnp.where(lane < KER * 8, logits, -1e30)
        top = lane_groups(logits, jnp.maximum)
        e = jnp.exp(logits - top)
        kern = e / lane_groups(e, jnp.add)
        kern_ref[pl.ds(r, CH), :] = kern
        kern_low = kern.astype(BF)
        for b in range(ATT // 128):
            lanes = slice(b * 128, (b + 1) * 128)
            wide = mm(kern_low, tap_spread(b))
            cs = cv_pad[pl.ds(r, HALO), lanes]
            total = jnp.zeros((CH, 128), F32)
            for j in range(KER):
                moved = cs if j == 4 else pltpu.roll(cs, (HALO - (j - 4)) % HALO, 0)
                total = total + wide[:, j * 128 : (j + 1) * 128] * moved[8 : 8 + CH]
            conv_ref[pl.ds(r, CH), lanes] = total.astype(BF)
        return carry

    lax.fori_loop(0, SEQ // CH, conv, 0)


def enter(pick, tokens, w_in, w_depth, w_point, w_kern):
    rows = tokens.shape[0]
    block = lambda n: pl.BlockSpec((SEQ, n), lambda s: (s, 0))
    return pl.pallas_call(
        enter_kernel,
        grid=(rows // SEQ,),
        in_specs=[
            block(1), block(WIDTH), whole((WIDTH, 4 * ATT)), whole((KER, WIDTH)),
            whole((WIDTH, ATT)), whole((ATT, 128)),
        ],
        out_specs=[block(WIDTH), block(4 * ATT), block(WIDTH), block(ATT), block(128), block(ATT)],
        out_shape=[
            jax.ShapeDtypeStruct((rows, WIDTH), BF),
            jax.ShapeDtypeStruct((rows, 4 * ATT), BF),
            jax.ShapeDtypeStruct((rows, WIDTH), BF),
            jax.ShapeDtypeStruct((rows, ATT), BF),
            jax.ShapeDtypeStruct((rows, 128), F32),
            jax.ShapeDtypeStruct((rows, ATT), BF),
        ],
        scratch_shapes=[pltpu.VMEM((SEQ + 16, WIDTH), F32), pltpu.VMEM((SEQ + 16, ATT), F32)],
        compiler_params=params(1),
        name="enter",
    )(pick, tokens, w_in, w_depth, w_point, w_kern)


def own_lanes(rows, head):
    lane = lax.broadcasted_iota(jnp.int32, (rows, 128), 1)
    return (lane // HEAD) == head


def attend_kernel(q_ref, k_ref, v_ref, p_ref, o_ref, inv_ref):
    k = k_ref[...]
    for head in (0, 1):
        mine = own_lanes(SEQ, head)
        v = jnp.where(mine, v_ref[...].astype(F32), 1.0).astype(BF)

        def part(i, carry):
            r = pl.multiple_of(i * CH, CH)
            mine_q = own_lanes(CH, head)
            q = jnp.where(mine_q, q_ref[pl.ds(r, CH), :].astype(F32) * (HEAD**-0.5), 0.0).astype(BF)
            s = mm_nt(q, k)
            p = jnp.exp(s - jnp.max(s, -1, keepdims=True)).astype(BF)
            p_ref[0, head, pl.ds(r, CH), :] = p
            o = mm(p, v)
            total = jnp.where(mine_q, pltpu.roll(o, HEAD, 1), o)
            inv = 1.0 / total
            res = o * inv
            if head == 0:
                o_ref[pl.ds(r, CH), :] = res.astype(BF)
                inv_ref[pl.ds(r, CH), :] = inv
            else:
                o_ref[pl.ds(r, CH), :] = jnp.where(
                    mine_q, res, o_ref[pl.ds(r, CH), :].astype(F32)
                ).astype(BF)
                inv_ref[pl.ds(r, CH), :] = jnp.where(mine_q, inv, inv_ref[pl.ds(r, CH), :])
            return carry

        lax.fori_loop(0, SEQ // CH, part, 0)


def attend(proj):
    rows = proj.shape[0]
    pairs = HEADS // 2
    col = lambda base: pl.BlockSpec((SEQ, 128), lambda s, p: (s, base + p))
    return pl.pallas_call(
        attend_kernel,
        grid=(rows // SEQ, pairs),
        in_specs=[col(0), col(pairs), col(2 * pairs)],
        out_specs=[pl.BlockSpec((1, 2, SEQ, SEQ), lambda s, p: (s, p, 0, 0)), col(0), col(0)],
        out_shape=[
            jax.ShapeDtypeStruct((rows // SEQ, HEADS, SEQ, SEQ), BF),
            jax.ShapeDtypeStruct((rows, ATT), BF),
            jax.ShapeDtypeStruct((rows, ATT), F32),
        ],
        compiler_params=params(2),
        name="attend",
    )(proj, proj, proj)


ERF_P = 0.3275911 / math.sqrt(2.0)
ERF_A = (0.254829592, -0.284496736, 1.421413741, -1.453152027, 1.061405429)
PHI = 1.0 / math.sqrt(2.0 * math.pi)


def gelu_both(u):
    mag = jnp.abs(u)
    t = 1.0 / (1.0 + ERF_P * mag)
    poly = ERF_A[4]
    for a in ERF_A[3::-1]:
        poly = poly * t + a
    e = jnp.exp(-0.5 * (u * u))
    tail = (0.5 * t) * poly * e
    cdf = jnp.where(u > 0, 1.0 - tail, tail)
    return u * cdf, cdf + (PHI * u) * e


def norm_parts(z):
    mean = jnp.mean(z, -1, keepdims=True)
    centred = z - mean
    var = jnp.mean(centred * centred, -1, keepdims=True)
    r = lax.rsqrt(var + 1e-12)
    return centred * r, r


def norm_back(c, xh, r, gain):
    gc = c * gain
    return r * (gc - jnp.mean(gc, -1, keepdims=True) - xh * jnp.mean(gc * xh, -1, keepdims=True))


def fold_rows(x):
    return jnp.sum(x.reshape(-1, 8, x.shape[-1]), 0)


MID = 256
FF = 1536
FC = 512


def middle_kernel(
    att_ref, conv_ref, inp_ref, cot_ref, w_out_ref, w_up_ref, w_down_ref, vec_ref,
    out_ref, dctx_ref, dfirst_ref, dout_ref, dup_ref, ddown_ref, dvec_ref,
    acc_out, acc_up, acc_down, acc_vec, act_ref, slope_ref,
):
    step = pl.program_id(0)
    last = pl.num_programs(0) - 1

    @pl.when(step == 0)
    def _():
        acc_out[...] = jnp.zeros_like(acc_out)
        acc_up[...] = jnp.zeros_like(acc_up)
        acc_down[...] = jnp.zeros_like(acc_down)
        acc_vec[...] = jnp.zeros_like(acc_vec)

    ctx = jnp.concatenate([att_ref[...], conv_ref[...]], -1)
    g_one, s_one = vec_ref[0:1, :], vec_ref[1:2, :]
    g_two, s_two = vec_ref[2:3, :], vec_ref[3:4, :]
    first_in = mm(ctx, w_out_ref[...]) + inp_ref[...].astype(F32)
    xh_one, r_one = norm_parts(first_in)
    first = xh_one * g_one + s_one
    first_low = first.astype(BF)
    outs = []
    for g in (0, 1):
        cols = slice(g * ATT, (g + 1) * ATT)
        total = None
        for f in range(FF // FC):
            hid = slice(f * FC, (f + 1) * FC)
            inner = mm_nt(first_low[:, cols], w_up_ref[g, hid, :])
            act, slope = gelu_both(inner)
            act = act.astype(BF)
            act_ref[g, :, hid] = act
            slope_ref[g, :, hid] = slope.astype(slope_ref.dtype)
            part = mm(act, w_down_ref[g, hid, :])
            total = part if total is None else total + part
        outs.append(total)
    xh_two, r_two = norm_parts(jnp.concatenate(outs, -1) + first)
    out_ref[...] = (xh_two * g_two + s_two).astype(BF)
    c = cot_ref[...].astype(F32)
    acc_vec[2] += fold_rows(c * xh_two)
    acc_vec[3] += fold_rows(c)
    d_second = norm_back(c, xh_two, r_two, g_two)
    d_outer = d_second.astype(BF)
    d_outer_t = d_second.T.astype(BF)
    first_t = first.T.astype(BF)
    backs = []
    for g in (0, 1):
        cols = slice(g * ATT, (g + 1) * ATT)
        total = None
        for f in range(FF // FC):
            hid = slice(f * FC, (f + 1) * FC)
            d_act = mm_nt(d_outer[:, cols], w_down_ref[g, hid, :])
            d_inner = (d_act * slope_ref[g, :, hid].astype(F32)).astype(BF)
            acc_down[g, :, hid] += mm(d_outer_t[cols, :], act_ref[g, :, hid])
            acc_up[g, :, hid] += mm(first_t[cols, :], d_inner)
            part = mm(d_inner, w_up_ref[g, hid, :])
            total = part if total is None else total + part
        backs.append(total)
    d_first = jnp.concatenate(backs, -1) + d_second
    acc_vec[0] += fold_rows(d_first * xh_one)
    acc_vec[1] += fold_rows(d_first)
    d_first_in = norm_back(d_first, xh_one, r_one, g_one)
    dfirst_ref[...] = d_first_in
    d_dense = d_first_in.astype(BF)
    acc_out[...] += mm_tn(ctx, d_dense)
    dctx_ref[...] = mm_nt(d_dense, w_out_ref[...]).astype(BF)

    @pl.when(step == last)
    def _():
        dout_ref[...] = acc_out[...].astype(dout_ref.dtype)
        for g in (0, 1):
            dup_ref[g] = acc_up[g].T.astype(dup_ref.dtype)
            ddown_ref[g] = acc_down[g].T.astype(ddown_ref.dtype)
        dvec_ref[...] = jnp.sum(acc_vec[...], 1)


def middle(att, conv, inputs, cot, w_out, w_up, w_down, vecs, grad_type=BF):
    rows = att.shape[0]
    block = lambda n: pl.BlockSpec((MID, n), lambda s: (s, 0))
    return pl.pallas_call(
        middle_kernel,
        grid=(rows // MID,),
        in_specs=[
            block(ATT), block(ATT), block(WIDTH), block(WIDTH),
            whole((WIDTH, WIDTH)), whole((2, FF, ATT)), whole((2, FF, ATT)), whole((4, WIDTH)),
        ],
        out_specs=[
            block(WIDTH), block(WIDTH), block(WIDTH), whole_out((WIDTH, WIDTH)),
            whole_out((2, FF, ATT)), whole_out((2, FF, ATT)), whole_out((4, WIDTH)),
        ],
        out_shape=[
            jax.ShapeDtypeStruct((rows, WIDTH), BF),
            jax.ShapeDtypeStruct((rows, WIDTH), BF),
            jax.ShapeDtypeStruct((rows, WIDTH), F32),
            jax.ShapeDtypeStruct((WIDTH, WIDTH), grad_type),
            jax.ShapeDtypeStruct((2, FF, ATT), grad_type),
            jax.ShapeDtypeStruct((2, FF, ATT), grad_type),
            jax.ShapeDtypeStruct((4, WIDTH), F32),
        ],
        scratch_shapes=[
            pltpu.VMEM((WIDTH, WIDTH), F32),
            pltpu.VMEM((2, ATT, FF), F32),
            pltpu.VMEM((2, ATT, FF), F32),
            pltpu.VMEM((4, 8, WIDTH), F32),
            pltpu.VMEM((2, MID, FF), BF),
            pltpu.VMEM((2, MID, FF), F32),
        ],
        compiler_params=params(1),
        name="middle",
    )(att, conv, inputs, cot, w_out, w_up, w_down, vecs)


def conv_back_kernel(
    dconv_ref, kern_ref, q_ref, cv_ref, ck_ref, spread_ref, inp_ref, w_depth_ref, w_point_ref, w_kern_ref,
    dq_ref, dcv_ref, din_ref, dpoint_ref, dkern_ref, ddepth_ref,
    x_pad, cv_pad, dc_pad, kl_pad, ds_pad, acc_point, acc_kern, acc_depth,
):
    step = pl.program_id(0)
    last = pl.num_programs(0) - 1
    zero = lambda n: jnp.zeros((8, n), F32)
    for ref, n in ((x_pad, WIDTH), (cv_pad, ATT), (dc_pad, ATT), (kl_pad, 128), (ds_pad, WIDTH)):
        ref[0:8, :] = zero(n)
        ref[SEQ + 8 : SEQ + 16, :] = zero(n)

    @pl.when(step == 0)
    def _():
        acc_point[...] = jnp.zeros_like(acc_point)
        acc_kern[...] = jnp.zeros_like(acc_kern)
        acc_depth[...] = jnp.zeros_like(acc_depth)

    def fill(i, carry):
        r = pl.multiple_of(i * CH, CH)
        rows = pl.ds(r, CH)
        there = pl.ds(r + 8, CH)
        x_pad[there, :] = inp_ref[rows, :].astype(F32)
        cv_pad[there, :] = cv_ref[rows, :].astype(F32)
        dc_pad[there, :] = dconv_ref[rows, :].astype(F32)
        kl_pad[there, :] = kern_ref[rows, :]
        return carry

    lax.fori_loop(0, SEQ // CH, fill, 0)

    def back(i, carry):
        r = pl.multiple_of(i * CH, CH)
        rows = pl.ds(r, CH)
        d_kern = jnp.zeros((CH, 128), F32)
        kl = kl_pad[pl.ds(r, HALO), :].astype(BF)
        for b in range(ATT // 128):
            lanes = slice(b * 128, (b + 1) * 128)
            spreader = tap_spread(b)
            cs = cv_pad[pl.ds(r, HALO), lanes]
            dc = dc_pad[pl.ds(r + 8, CH), lanes]
            prods = []
            for j in range(KER):
                moved = cs if j == 4 else pltpu.roll(cs, (HALO - (j - 4)) % HALO, 0)
                prods.append((dc * moved[8 : 8 + CH]).astype(BF))
            d_kern = d_kern + mm_nt(jnp.concatenate(prods, -1), spreader)
            wide = mm(kl, spreader)
            dch = dc_pad[pl.ds(r, HALO), lanes]
            total = jnp.zeros((CH, 128), F32)
            for j in range(KER):
                term = wide[:, j * 128 : (j + 1) * 128] * dch
                moved = term if j == 4 else pltpu.roll(term, (HALO + (j - 4)) % HALO, 0)
                total = total + moved[8 : 8 + CH]
            dcv_ref[rows, lanes] = total.astype(BF)
        kern = kern_ref[rows, :]
        dot_rows = lane_groups(kern * d_kern, jnp.add)
        d_logits = (kern * (d_kern - dot_rows)).astype(BF)
        q = q_ref[rows, :].astype(F32)
        ck = ck_ref[rows, :].astype(F32)
        mixed = (ck * q).astype(BF)
        acc_kern[...] += mm_tn(mixed, d_logits)
        d_mixed = mm_nt(d_logits, w_kern_ref[...])
        dq_ref[rows, :] = d_mixed * ck
        d_ck = (d_mixed * q).astype(BF)
        acc_point[...] += mm_tn(spread_ref[rows, :], d_ck)
        ds_pad[pl.ds(r + 8, CH), :] = mm_nt(d_ck, w_point_ref[...])
        return carry

    lax.fori_loop(0, SEQ // CH, back, 0)

    def depth(i, carry):
        r = pl.multiple_of(i * CH, CH)
        rows = pl.ds(r, CH)
        for b in range(WIDTH // 128):
            lanes = slice(b * 128, (b + 1) * 128)
            dsh = ds_pad[pl.ds(r, HALO), lanes]
            tap = lambda j: w_depth_ref[j : j + 1, lanes]
            shifted = [dsh] + [pltpu.roll(dsh, s, 0) for s in (1, 2, 3)]
            low_part = sum(tap(s) * shifted[s] for s in range(4))
            mid_part = sum(tap(4 + s) * shifted[s] for s in range(4))
            high_part = tap(8) * dsh
            low_part = pltpu.roll(low_part, HALO - 4, 0)
            high_part = pltpu.roll(high_part, 4, 0)
            din_ref[rows, lanes] = (low_part + mid_part + high_part)[8 : 8 + CH]
            xs = x_pad[pl.ds(r + 8, CH), lanes]
            far_low = [pltpu.roll(shifted[s], HALO - 4, 0) for s in range(4)]
            far_high = pltpu.roll(dsh, 4, 0)
            for j in range(KER):
                src = far_low[j] if j < 4 else (shifted[j - 4] if j < 8 else far_high)
                acc_depth[j, :, lanes] += fold_rows(src[8 : 8 + CH] * xs)
        return carry

    lax.fori_loop(0, SEQ // CH, depth, 0)

    @pl.when(step == last)
    def _():
        dpoint_ref[...] = acc_point[...].astype(dpoint_ref.dtype)
        dkern_ref[...] = acc_kern[...]
        ddepth_ref[...] = jnp.sum(acc_depth[...], 1)


def conv_back(dctx, kern, proj, ck, spread, inputs, w_depth, w_point, w_kern, grad_type=BF):
    rows = inputs.shape[0]
    block = lambda n: pl.BlockSpec((SEQ, n), lambda s: (s, 0))
    at = lambda c: pl.BlockSpec((SEQ, ATT), lambda s: (s, c))
    return pl.pallas_call(
        conv_back_kernel,
        grid=(rows // SEQ,),
        in_specs=[
            at(1), block(128), at(0), at(3), block(ATT), block(WIDTH), block(WIDTH),
            whole((KER, WIDTH)), whole((WIDTH, ATT)), whole((ATT, 128)),
        ],
        out_specs=[
            block(ATT), block(ATT), block(WIDTH), whole_out((WIDTH, ATT)), whole_out((ATT, 128)),
            whole_out((KER, WIDTH)),
        ],
        out_shape=[
            jax.ShapeDtypeStruct((rows, ATT), F32),
            jax.ShapeDtypeStruct((rows, ATT), BF),
            jax.ShapeDtypeStruct((rows, WIDTH), F32),
            jax.ShapeDtypeStruct((WIDTH, ATT), grad_type),
            jax.ShapeDtypeStruct((ATT, 128), F32),
            jax.ShapeDtypeStruct((KER, WIDTH), F32),
        ],
        scratch_shapes=[
            pltpu.VMEM((SEQ + 16, WIDTH), F32),
            pltpu.VMEM((SEQ + 16, ATT), F32),
            pltpu.VMEM((SEQ + 16, ATT), F32),
            pltpu.VMEM((SEQ + 16, 128), F32),
            pltpu.VMEM((SEQ + 16, WIDTH), F32),
            pltpu.VMEM((WIDTH, ATT), F32),
            pltpu.VMEM((ATT, 128), F32),
            pltpu.VMEM((KER, 8, WIDTH), F32),
        ],
        compiler_params=params(1),
        name="conv_back",
    )(dctx, kern, proj, proj, ck, spread, inputs, w_depth, w_point, w_kern)


def attend_back_kernel(
    q_ref, k_ref, v_ref, p_ref, o_ref, inv_ref, datt_ref, dqc_ref, dq_ref, dk_ref, dv_ref, acc_k, acc_v
):
    scale = HEAD**-0.5
    acc_k[...] = jnp.zeros_like(acc_k)
    acc_v[...] = jnp.zeros_like(acc_v)
    v = v_ref[...]

    def part(i, carry):
        r = pl.multiple_of(i * CH, CH)
        rows = pl.ds(r, CH)
        d_att = datt_ref[rows, :].astype(F32) * inv_ref[rows, :]
        o = o_ref[rows, :].astype(F32)
        dq = dqc_ref[rows, :]
        for head in (0, 1):
            mine = own_lanes(CH, head)
            da = jnp.where(mine, d_att, 0.0)
            dot_rows = jnp.sum(da * o, -1, keepdims=True)
            da = da.astype(BF)
            p = p_ref[0, head, rows, :]
            ds = mm_nt(da, v)
            ds = (p.astype(F32) * (ds - dot_rows)).astype(BF)
            k_own = jnp.where(own_lanes(SEQ, head), k_ref[...].astype(F32) * scale, 0.0).astype(BF)
            dq = dq + mm(ds, k_own)
            q_own = jnp.where(mine, q_ref[rows, :].astype(F32) * scale, 0.0)
            acc_k[...] += mm_tn(ds, q_own.astype(BF))
            acc_v[...] += mm_tn(p, da)
        dq_ref[rows, :] = dq.astype(BF)
        return carry

    lax.fori_loop(0, SEQ // CH, part, 0)
    dk_ref[...] = acc_k[...].astype(BF)
    dv_ref[...] = acc_v[...].astype(BF)


def attend_back(proj, probs, att, inv, dctx, dq_conv):
    rows = proj.shape[0]
    pairs = HEADS // 2
    col = lambda base: pl.BlockSpec((SEQ, 128), lambda s, p: (s, base + p))
    return pl.pallas_call(
        attend_back_kernel,
        grid=(rows // SEQ, pairs),
        in_specs=[
            col(0), col(pairs), col(2 * pairs),
            pl.BlockSpec((1, 2, SEQ, SEQ), lambda s, p: (s, p, 0, 0)),
            col(0), col(0), col(0), col(0),
        ],
        out_specs=[col(0)] * 3,
        out_shape=[jax.ShapeDtypeStruct((rows, ATT), BF)] * 3,
        scratch_shapes=[pltpu.VMEM((SEQ, 128), F32), pltpu.VMEM((SEQ, 128), F32)],
        compiler_params=params(2),
        name="attend_back",
    )(proj, proj, proj, probs, att, inv, dctx, dq_conv)


def weight_kernel(inp_ref, dq_ref, dk_ref, dv_ref, dcv_ref, din_ref, acc):
    step = pl.program_id(0)
    last = pl.num_programs(0) - 1
    inp_t = inp_ref[...].astype(F32).T.astype(BF)
    for i, ref in enumerate((dq_ref, dk_ref, dv_ref, dcv_ref)):
        cols = slice(i * ATT, (i + 1) * ATT)
        part = mm(inp_t, ref[...])

        @pl.when(step == 0)
        def _():
            acc[:, cols] = part

        @pl.when(step > 0)
        def _():
            acc[:, cols] += part

    @pl.when(step == last)
    def _():
        din_ref[...] = acc[...].astype(din_ref.dtype)


def weight_grad(inputs, dq, dk, dv, dcv, grad_type=BF):
    rows = inputs.shape[0]
    block = lambda n: pl.BlockSpec((512, n), lambda s: (s, 0))
    return pl.pallas_call(
        weight_kernel,
        grid=(rows // 512,),
        in_specs=[block(WIDTH)] + [block(ATT)] * 4,
        out_specs=whole_out((WIDTH, 4 * ATT)),
        out_shape=jax.ShapeDtypeStruct((WIDTH, 4 * ATT), grad_type),
        scratch_shapes=[pltpu.VMEM((WIDTH, 4 * ATT), F32)],
        compiler_params=params(1),
        name="weight_grad",
    )(inputs, dq, dk, dv, dcv)


def leave_kernel(
    dq_ref, dk_ref, dv_ref, dcv_ref, conv_ref, first_ref, mask_ref, to_ref, w_in_ref, out_ref, moved
):
    def make(i, carry):
        rows = pl.ds(pl.multiple_of(i * CH, CH), CH)
        total = conv_ref[rows, :] + first_ref[rows, :]
        for n, ref in enumerate((dq_ref, dk_ref, dv_ref, dcv_ref)):
            total = total + mm_nt(ref[rows, :], w_in_ref[:, n * ATT : (n + 1) * ATT])
        moved[rows, :] = total.astype(BF)
        out_ref[rows, :] = jnp.where(mask_ref[rows, :] == 1, 0.0, total)
        return carry

    lax.fori_loop(0, SEQ // CH, make, 0)

    def scatter(i, carry):
        r = pl.multiple_of(i * CH, CH)
        rows = pl.ds(r, CH)
        target = lax.broadcasted_iota(jnp.int32, (CH, SEQ), 0) + r
        hot = (target == to_ref[0]).astype(F32).astype(BF)
        out_ref[rows, :] += mm(hot, moved[...])
        return carry

    lax.fori_loop(0, SEQ // CH, scatter, 0)


def leave(dq, dk, dv, dcv, d_conv_in, d_first_in, mask_col, to_row, w_in):
    rows = dq.shape[0]
    block = lambda n: pl.BlockSpec((SEQ, n), lambda s: (s, 0))
    return pl.pallas_call(
        leave_kernel,
        grid=(rows // SEQ,),
        in_specs=[block(ATT)] * 4
        + [block(WIDTH)] * 2
        + [block(1), pl.BlockSpec((1, 1, SEQ), lambda s: (s, 0, 0)), whole((WIDTH, 4 * ATT))],
        out_specs=block(WIDTH),
        out_shape=jax.ShapeDtypeStruct((rows, WIDTH), F32),
        scratch_shapes=[pltpu.VMEM((SEQ, WIDTH), BF)],
        compiler_params=params(1),
        name="leave",
    )(dq, dk, dv, dcv, d_conv_in, d_first_in, mask_col, to_row, w_in)


def pack_taps(kernel_full):
    by_tap = kernel_full.reshape(ATT, HEADS, KER).transpose(0, 2, 1)
    return jnp.pad(by_tap, ((0, 0), (0, 16 - KER), (0, 8 - HEADS))).reshape(ATT, 128)


def unpack_taps(packed):
    return packed.reshape(ATT, 16, 8)[:, :KER, :HEADS].transpose(0, 2, 1).reshape(ATT, HEADS * KER)


AXES = ("dp", "fsdp")
LANES = 384


def as_rows(x):
    flat = x.reshape(-1)
    return jnp.pad(flat, (0, -flat.size % LANES)).reshape(-1, LANES)


def per_device(
    tokens,
    masked,
    replace_ids,
    in_weight,
    depth_weight,
    point_weight,
    kernel_weight,
    out_weight,
    gain_one,
    shift_one,
    ffn_in,
    feedforward_output,
    gain_two,
    shift_two,
    cotangent,
):
    rows = tokens.shape[0]
    seqs = rows // SEQ
    dp, fsdp = lax.axis_size("dp"), lax.axis_size("fsdp")
    devices = dp * fsdp
    own = in_weight.shape[0]
    hit = masked == 1
    here = jnp.arange(rows, dtype=jnp.int32) % SEQ
    pick = jnp.where(hit, replace_ids, here)[:, None]
    to_row = jnp.where(hit, replace_ids, -1).reshape(seqs, 1, SEQ)

    vec_own = jnp.stack([gain_one, shift_one, gain_two, shift_two])
    small = as_rows(
        jnp.concatenate([depth_weight.reshape(-1), vec_own.reshape(-1), kernel_weight.reshape(-1)])
    )
    head_own = jnp.concatenate([in_weight.reshape(-1, LANES), point_weight, small])
    head = lax.all_gather(head_own, AXES, axis=0)
    mid_own = jnp.concatenate(
        [
            out_weight.reshape(-1, LANES),
            ffn_in.transpose(0, 2, 1).reshape(-1, LANES),
            feedforward_output.reshape(-1, LANES),
        ]
    )
    mid = lax.all_gather(mid_own, AXES, axis=0)
    w_in = head[:, : 4 * own].reshape(WIDTH, 4 * ATT)
    w_point = head[:, 4 * own : 5 * own].reshape(WIDTH, ATT)
    small_all = head[:, 5 * own :].reshape(devices, -1)
    n_depth, n_vec = KER * own, 4 * own
    w_depth = small_all[:, :n_depth].reshape(devices, KER, own).transpose(1, 0, 2).reshape(KER, WIDTH)
    vecs = small_all[:, n_depth : n_depth + n_vec].reshape(devices, 4, own).transpose(1, 0, 2)
    vecs = vecs.reshape(4, WIDTH).astype(F32)
    w_depth = w_depth.astype(F32)
    kern_full = small_all[:fsdp, n_depth + n_vec :][:, : kernel_weight.size].reshape(ATT, HEADS * KER)
    w_kern = pack_taps(kern_full)
    hid = ffn_in.shape[2]
    w_out = mid[:, : 2 * own].reshape(WIDTH, WIDTH)
    up = mid[:, 2 * own : 2 * own + 2 * hid].reshape(devices, 2, hid, ATT)
    w_up_t = up.transpose(1, 0, 2, 3).reshape(2, FF, ATT)
    down = mid[:, 2 * own + 2 * hid :].reshape(devices, 2, hid, ATT)
    w_down = down.transpose(1, 0, 2, 3).reshape(2, FF, ATT)

    inputs, proj, spread, ck, kern, conv = enter(pick, tokens, w_in, w_depth, w_point, w_kern)
    probs, att, inv = attend(proj)
    out, dctx, d_first_in, d_out, d_up_t, d_down, d_vecs = middle(
        att, conv, inputs, cotangent, w_out, w_up_t, w_down, vecs
    )
    split = lambda g: g.reshape(2, devices, hid, ATT).transpose(1, 0, 2, 3).reshape(devices, -1, LANES)
    mid_grads = jnp.concatenate(
        [d_out.reshape(devices, -1, LANES), split(d_up_t), split(d_down)], 1
    )
    mid_sum = lax.psum_scatter(mid_grads, AXES, scatter_dimension=0, tiled=True)[0]
    dq_conv, dcv, d_conv_in, d_point, d_kern, d_depth = conv_back(
        dctx, kern, proj, ck, spread, inputs, w_depth, w_point, w_kern
    )
    dq, dk, dv = attend_back(proj, probs, att, inv, dctx, dq_conv)
    d_in = weight_grad(inputs, dq, dk, dv, dcv)
    by_owner = lambda g: g.reshape(-1, devices, own).transpose(1, 0, 2).reshape(devices, -1)
    kern_by = jnp.tile(unpack_taps(d_kern).reshape(fsdp, -1), (dp, 1))
    small_grad = jnp.concatenate([by_owner(d_depth), by_owner(d_vecs), kern_by], 1).astype(BF)
    small_grad = jnp.pad(small_grad, ((0, 0), (0, -small_grad.shape[1] % LANES)))
    tail = jnp.concatenate(
        [
            d_in.reshape(devices, -1, LANES),
            d_point.reshape(devices, -1, LANES),
            small_grad.reshape(devices, -1, LANES),
        ],
        1,
    )
    tail_sum = lax.psum_scatter(tail, AXES, scatter_dimension=0, tiled=True)[0]
    d_tokens = leave(dq, dk, dv, dcv, d_conv_in, d_first_in, masked[:, None], to_row, w_in)

    scale = 1.0 / math.sqrt(rows * devices)
    mid_sum = mid_sum.astype(F32) * scale
    tail_sum = tail_sum.astype(F32) * scale
    small_sum = tail_sum[5 * own :].reshape(-1)
    vec_sum = small_sum[n_depth : n_depth + n_vec].reshape(4, own)
    kern_sum = small_sum[n_depth + n_vec :][: kernel_weight.size].reshape(kernel_weight.shape)
    return (
        out,
        d_tokens,
        tail_sum[: 4 * own].reshape(own, 4 * ATT),
        small_sum[:n_depth].reshape(KER, own),
        tail_sum[4 * own : 5 * own],
        kern_sum,
        mid_sum[: 2 * own].reshape(own, WIDTH),
        vec_sum[0],
        vec_sum[1],
        mid_sum[2 * own : 2 * own + 2 * hid].reshape(2, hid, ATT).transpose(0, 2, 1),
        mid_sum[2 * own + 2 * hid :].reshape(2, hid, ATT),
        vec_sum[2],
        vec_sum[3],
    )


def solution(mesh):
    return jax.shard_map(
        per_device,
        mesh=mesh,
        in_specs=(
            P(("dp", "fsdp"), None),
            P(("dp", "fsdp")),
            P(("dp", "fsdp")),
            P(("dp", "fsdp"), None),
            P(None, ("dp", "fsdp")),
            P(("dp", "fsdp"), None),
            P("fsdp", None),
            P(("dp", "fsdp"), None),
            P(("dp", "fsdp")),
            P(("dp", "fsdp")),
            P(None, None, ("dp", "fsdp")),
            P(None, ("dp", "fsdp"), None),
            P(("dp", "fsdp")),
            P(("dp", "fsdp")),
            P(("dp", "fsdp"), None),
        ),
        out_specs=(
            P(("dp", "fsdp"), None),
            P(("dp", "fsdp"), None),
            P(("dp", "fsdp"), None),
            P(None, ("dp", "fsdp")),
            P(("dp", "fsdp"), None),
            P("fsdp", None),
            P(("dp", "fsdp"), None),
            P(("dp", "fsdp")),
            P(("dp", "fsdp")),
            P(None, None, ("dp", "fsdp")),
            P(None, ("dp", "fsdp"), None),
            P(("dp", "fsdp")),
            P(("dp", "fsdp")),
        ),
        check_vma=False,
    )
```

```python
from functools import partial
import math

import jax
import jax.numpy as jnp
from jax import lax
from jax.experimental import pallas as pl
from jax.experimental.pallas import tpu as pltpu
from jax.sharding import PartitionSpec as P

BF = jnp.bfloat16
F32 = jnp.float32
HEADS = 6
HEAD = 64
SEQ = 1024
KER = 9
ATT = HEADS * HEAD
WIDTH = 768
VMEM_MAX = 60 * 1024 * 1024


def mm(a, b):
    return jnp.dot(a, b, preferred_element_type=F32)


def mm_nt(a, b):
    return lax.dot_general(a, b, (((1,), (1,)), ((), ())), preferred_element_type=F32)


def mm_tn(a, b):
    return lax.dot_general(a, b, (((0,), (0,)), ((), ())), preferred_element_type=F32)


def params(count):
    return pltpu.CompilerParams(
        dimension_semantics=("arbitrary",) * count, vmem_limit_bytes=VMEM_MAX
    )


def cost(flops, moved):
    return pl.CostEstimate(flops=int(flops), bytes_accessed=int(moved), transcendentals=0)


def whole(shape):
    zeros = (0,) * len(shape)
    return pl.BlockSpec(shape, lambda *_: zeros, pipeline_mode=pl.Buffered(1))


def whole_out(shape):
    zeros = (0,) * len(shape)
    return pl.BlockSpec(shape, lambda *_: zeros)


AXES = ("dp", "fsdp")
LANES = 384


def as_rows(x, multiple=1):
    flat = x.reshape(-1)
    return jnp.pad(flat, (0, -flat.size % (LANES * multiple))).reshape(-1, LANES)


def hop(x, axis, mask):
    return lax.ppermute(x, axis, [(i, i ^ mask) for i in range(lax.axis_size(axis))])


PLACE = {"x": ("dp", 2, 2), "core": ("dp", 1, 2), "z": ("fsdp", 2, 4), "y": ("fsdp", 1, 2)}


def seat(name):
    axis, unit, count = PLACE[name]
    return (lax.axis_index(axis) // unit) % count


def fold_kernel(count, parts, mine_ref, *refs):
    ins, outs = refs[:parts], refs[parts:]
    for k in range(count):
        b = mine_ref[0] ^ k
        total = ins[0][:, b].astype(F32)
        for ref in ins[1:]:
            total = total + ref[:, b].astype(F32)
        outs[k][...] = total.astype(BF)


def fold(arrays, name, before, after):
    count = PLACE[name][2]
    rows = arrays[0].shape[-2]
    views = [a.reshape(before, count, after, rows, LANES) for a in arrays]
    cut = 2 if after % 2 == 0 else 1
    in_block = pl.BlockSpec((before, count, after // cut, rows, LANES), lambda i, m: (0, 0, i, 0, 0))
    out_block = pl.BlockSpec((before, after // cut, rows, LANES), lambda i, m: (0, i, 0, 0))
    return pl.pallas_call(
        partial(fold_kernel, count, len(arrays)),
        grid_spec=pltpu.PrefetchScalarGridSpec(
            num_scalar_prefetch=1,
            grid=(cut,),
            in_specs=[in_block] * len(arrays),
            out_specs=[out_block] * count,
        ),
        out_shape=[jax.ShapeDtypeStruct((before, after, rows, LANES), BF)] * count,
        compiler_params=params(1),
        cost_estimate=cost(0, 4 * arrays[0].size * len(arrays)),
        name="fold",
    )(seat(name).astype(jnp.int32).reshape(1), *views)


def spread_out(pieces, name):
    axis, unit, count = PLACE[name]
    return [pieces[0]] + [hop(pieces[k], axis, unit * k) for k in range(1, count)]


def fold_step(arrays, left, name):
    at = [n for n, _ in left].index(name)
    before = math.prod(c for _, c in left[:at])
    after = math.prod(c for _, c in left[at + 1 :])
    return fold(arrays, name, before, after), left[:at] + left[at + 1 :]


SPAN = [("x", 2), ("z", 4), ("y", 2)]


def tie(first, second):
    first, second = lax.optimization_barrier((first, second))
    return first, second


def pair_slabs(own, own_small):
    n = own.shape[1]
    packed = jnp.concatenate([own.reshape(-1, LANES), own_small])
    other = hop(packed, "fsdp", 1)
    even = seat("y") == 0
    first, second = jnp.where(even, packed, other), jnp.where(even, other, packed)
    cut = lambda a: a[: 5 * n].reshape(5, n, LANES)
    big = jnp.concatenate([cut(first), cut(second)], 1).reshape(-1, LANES)
    slab = jnp.concatenate([big, first[5 * n :], second[5 * n :]])
    slabs = [slab] + [hop(slab, "fsdp", 2 * k) for k in (1, 2, 3)]
    slabs = slabs + [hop(s, "dp", 2) for s in slabs]
    slabs = slabs + [hop(s, "dp", 1) for s in slabs]
    return slabs


SLAB_BITS = [((s // 8) + 2 * ((s // 4) % 2)) * 4 + s % 4 for s in range(16)]


def lane_groups(x, combine):
    for step in (64, 32, 16, 8):
        x = combine(x, pltpu.roll(x, step, 1))
    return x


def tap_spread(block):
    rows = lax.broadcasted_iota(jnp.int32, (128, KER * 128), 0)
    cols = lax.broadcasted_iota(jnp.int32, (128, KER * 128), 1)
    want = (cols // 128) * 8 + block * 2 + (cols % 128) // HEAD
    return (rows == want).astype(F32).astype(BF)


CH = 256
HALO = CH + 16


def enter_kernel(
    pick_ref, tok_ref, w_in_ref, w_depth_ref, w_point_ref, w_kern_ref,
    inp_ref, proj_ref, spread_ref, ck_ref, kern_ref, conv_ref,
    x_pad, cv_pad,
):
    x_pad[0:8, :] = jnp.zeros((8, WIDTH), F32)
    x_pad[SEQ + 8 : SEQ + 16, :] = jnp.zeros((8, WIDTH), F32)
    cv_pad[0:8, :] = jnp.zeros((8, ATT), F32)
    cv_pad[SEQ + 8 : SEQ + 16, :] = jnp.zeros((8, ATT), F32)

    def load(i, carry):
        r = pl.multiple_of(i * CH, CH)
        pick = pick_ref[pl.ds(r, CH), :]
        cols = lax.broadcasted_iota(jnp.int32, (CH, SEQ), 1)
        hot = (cols == pick).astype(F32).astype(BF)
        rows = mm(hot, tok_ref[...])
        x_pad[pl.ds(r + 8, CH), :] = rows
        low = rows.astype(BF)
        inp_ref[pl.ds(r, CH), :] = low
        proj = mm(low, w_in_ref[...])
        proj_low = proj.astype(BF)
        proj_ref[pl.ds(r, CH), :] = proj_low
        cv_pad[pl.ds(r + 8, CH), :] = proj_low[:, 3 * ATT :].astype(F32)
        return carry

    lax.fori_loop(0, SEQ // CH, load, 0)

    def conv(i, carry):
        r = pl.multiple_of(i * CH, CH)
        for b in range(WIDTH // 128):
            lanes = slice(b * 128, (b + 1) * 128)
            xs = x_pad[pl.ds(r, HALO), lanes]
            shifted = [xs] + [pltpu.roll(xs, HALO - s, 0) for s in (1, 2, 3)]
            tap = lambda j: w_depth_ref[j : j + 1, lanes]
            low_part = sum(tap(s) * shifted[s] for s in range(4))
            mid_part = sum(tap(4 + s) * shifted[s] for s in range(4))
            high_part = tap(8) * xs
            low_part = pltpu.roll(low_part, HALO - 4, 0)
            high_part = pltpu.roll(high_part, HALO - 4, 0)
            total = low_part[0:CH] + mid_part[8 : 8 + CH] + high_part[8 : 8 + CH]
            spread_ref[pl.ds(r, CH), lanes] = total.astype(BF)
        ck = mm(spread_ref[pl.ds(r, CH), :], w_point_ref[...]).astype(BF)
        ck_ref[pl.ds(r, CH), :] = ck
        q = proj_ref[pl.ds(r, CH), 0:ATT].astype(F32)
        mixed = (ck.astype(F32) * q).astype(BF)
        logits = mm(mixed, w_kern_ref[...])
        lane = lax.broadcasted_iota(jnp.int32, (CH, 128), 1)
        logits = jnp.where(lane < KER * 8, logits, -1e30)
        top = lane_groups(logits, jnp.maximum)
        e = jnp.exp(logits - top)
        kern = e / lane_groups(e, jnp.add)
        kern_ref[pl.ds(r, CH), :] = kern
        kern_low = kern.astype(BF)
        for b in range(ATT // 128):
            lanes = slice(b * 128, (b + 1) * 128)
            wide = mm(kern_low, tap_spread(b))
            cs = cv_pad[pl.ds(r, HALO), lanes]
            total = jnp.zeros((CH, 128), F32)
            for j in range(KER):
                moved = cs if j == 4 else pltpu.roll(cs, (HALO - (j - 4)) % HALO, 0)
                total = total + wide[:, j * 128 : (j + 1) * 128] * moved[8 : 8 + CH]
            conv_ref[pl.ds(r, CH), lanes] = total.astype(BF)
        return carry

    lax.fori_loop(0, SEQ // CH, conv, 0)


def enter_slabs_kernel(
    place_ref, pick_ref, tok_ref, w_depth_ref, w_kern_ref, *refs
):
    slabs, outs = refs[:16], refs[16:]
    results, w_in_ref, w_point_ref, scratch, sems = outs[:6], outs[6], outs[7], outs[8:10], outs[10]

    @pl.when(pl.program_id(0) == 0)
    def _():
        copies = []
        for s, slab in enumerate(slabs):
            spot = pl.ds(pl.multiple_of((place_ref[0] ^ SLAB_BITS[s]) * 48, 16), 48)
            for b in range(5):
                to = w_in_ref.at[spot, b * ATT : (b + 1) * ATT] if b < 4 else w_point_ref.at[spot, :]
                copies.append(pltpu.make_async_copy(slab.at[b * 48 : (b + 1) * 48, :], to, sems.at[s, b]))
        for copy in copies:
            copy.start()
        for copy in copies:
            copy.wait()

    enter_kernel(pick_ref, tok_ref, w_in_ref, w_depth_ref, w_point_ref, w_kern_ref, *results, *scratch)


def enter_outs(rows):
    block = lambda n: pl.BlockSpec((SEQ, n), lambda s: (s, 0))
    widths = ((WIDTH, BF), (4 * ATT, BF), (WIDTH, BF), (ATT, BF), (128, F32), (ATT, BF))
    return [block(n) for n, _ in widths], [jax.ShapeDtypeStruct((rows, n), t) for n, t in widths]


ENTER_COST = cost(25e9, 20e6)


def enter_slabs(pick, tokens, w_depth, w_kern, slabs):
    rows = tokens.shape[0]
    block = lambda n: pl.BlockSpec((SEQ, n), lambda s: (s, 0))
    place = (lax.axis_index("dp") * 8 + lax.axis_index("fsdp")) // 2
    specs, shapes = enter_outs(rows)
    return pl.pallas_call(
        enter_slabs_kernel,
        grid=(rows // SEQ,),
        in_specs=[
            pl.BlockSpec(memory_space=pltpu.SMEM), block(1), block(WIDTH), whole((KER, WIDTH)),
            whole((ATT, 128)),
        ]
        + [pl.BlockSpec(memory_space=pl.ANY)] * 16,
        out_specs=specs + [whole_out((WIDTH, 4 * ATT)), whole_out((WIDTH, ATT))],
        out_shape=shapes
        + [jax.ShapeDtypeStruct((WIDTH, 4 * ATT), BF), jax.ShapeDtypeStruct((WIDTH, ATT), BF)],
        scratch_shapes=[
            pltpu.VMEM((SEQ + 16, WIDTH), F32),
            pltpu.VMEM((SEQ + 16, ATT), F32),
            pltpu.SemaphoreType.DMA((16, 5)),
        ],
        compiler_params=params(1),
        cost_estimate=ENTER_COST,
        name="enter",
    )(place.astype(jnp.int32).reshape(1), pick, tokens, w_depth, w_kern, *slabs)


def enter(pick, tokens, w_in, w_depth, w_point, w_kern):
    rows = tokens.shape[0]
    block = lambda n: pl.BlockSpec((SEQ, n), lambda s: (s, 0))
    return pl.pallas_call(
        enter_kernel,
        grid=(rows // SEQ,),
        in_specs=[
            block(1), block(WIDTH), whole((WIDTH, 4 * ATT)), whole((KER, WIDTH)),
            whole((WIDTH, ATT)), whole((ATT, 128)),
        ],
        out_specs=[block(WIDTH), block(4 * ATT), block(WIDTH), block(ATT), block(128), block(ATT)],
        out_shape=[
            jax.ShapeDtypeStruct((rows, WIDTH), BF),
            jax.ShapeDtypeStruct((rows, 4 * ATT), BF),
            jax.ShapeDtypeStruct((rows, WIDTH), BF),
            jax.ShapeDtypeStruct((rows, ATT), BF),
            jax.ShapeDtypeStruct((rows, 128), F32),
            jax.ShapeDtypeStruct((rows, ATT), BF),
        ],
        scratch_shapes=[pltpu.VMEM((SEQ + 16, WIDTH), F32), pltpu.VMEM((SEQ + 16, ATT), F32)],
        compiler_params=params(1),
        cost_estimate=ENTER_COST,
        name="enter",
    )(pick, tokens, w_in, w_depth, w_point, w_kern)


def own_lanes(rows, head):
    lane = lax.broadcasted_iota(jnp.int32, (rows, 128), 1)
    return (lane // HEAD) == head


def attend_kernel(q_ref, k_ref, v_ref, p_ref, o_ref, inv_ref):
    k = k_ref[...]
    for head in (0, 1):
        mine = own_lanes(SEQ, head)
        v = jnp.where(mine, v_ref[...].astype(F32), 1.0).astype(BF)

        def part(i, carry):
            r = pl.multiple_of(i * CH, CH)
            mine_q = own_lanes(CH, head)
            q = jnp.where(mine_q, q_ref[pl.ds(r, CH), :].astype(F32) * (HEAD**-0.5), 0.0).astype(BF)
            s = mm_nt(q, k)
            p = jnp.exp(s - jnp.max(s, -1, keepdims=True)).astype(BF)
            p_ref[0, head, pl.ds(r, CH), :] = p
            o = mm(p, v)
            total = jnp.where(mine_q, pltpu.roll(o, HEAD, 1), o)
            inv = 1.0 / total
            res = o * inv
            if head == 0:
                o_ref[pl.ds(r, CH), :] = res.astype(BF)
                inv_ref[pl.ds(r, CH), :] = inv
            else:
                o_ref[pl.ds(r, CH), :] = jnp.where(
                    mine_q, res, o_ref[pl.ds(r, CH), :].astype(F32)
                ).astype(BF)
                inv_ref[pl.ds(r, CH), :] = jnp.where(mine_q, inv, inv_ref[pl.ds(r, CH), :])
            return carry

        lax.fori_loop(0, SEQ // CH, part, 0)


def attend(proj):
    rows = proj.shape[0]
    pairs = HEADS // 2
    col = lambda base: pl.BlockSpec((SEQ, 128), lambda s, p: (s, base + p))
    return pl.pallas_call(
        attend_kernel,
        grid=(rows // SEQ, pairs),
        in_specs=[col(0), col(pairs), col(2 * pairs)],
        out_specs=[pl.BlockSpec((1, 2, SEQ, SEQ), lambda s, p: (s, p, 0, 0)), col(0), col(0)],
        out_shape=[
            jax.ShapeDtypeStruct((rows // SEQ, HEADS, SEQ, SEQ), BF),
            jax.ShapeDtypeStruct((rows, ATT), BF),
            jax.ShapeDtypeStruct((rows, ATT), F32),
        ],
        compiler_params=params(2),
        cost_estimate=cost(25e9, 35e6),
        name="attend",
    )(proj, proj, proj)


ERF_P = 0.3275911 / math.sqrt(2.0)
ERF_A = (0.254829592, -0.284496736, 1.421413741, -1.453152027, 1.061405429)
PHI = 1.0 / math.sqrt(2.0 * math.pi)


def gelu_both(u):
    mag = jnp.abs(u)
    t = 1.0 / (1.0 + ERF_P * mag)
    poly = ERF_A[4]
    for a in ERF_A[3::-1]:
        poly = poly * t + a
    e = jnp.exp(-0.5 * (u * u))
    tail = (0.5 * t) * poly * e
    cdf = jnp.where(u > 0, 1.0 - tail, tail)
    return u * cdf, cdf + (PHI * u) * e


def norm_parts(z):
    mean = jnp.mean(z, -1, keepdims=True)
    centred = z - mean
    var = jnp.mean(centred * centred, -1, keepdims=True)
    r = lax.rsqrt(var + 1e-12)
    return centred * r, r


def norm_back(c, xh, r, gain):
    gc = c * gain
    return r * (gc - jnp.mean(gc, -1, keepdims=True) - xh * jnp.mean(gc * xh, -1, keepdims=True))


def fold_rows(x):
    return jnp.sum(x.reshape(-1, 8, x.shape[-1]), 0)


MID = 256
FF = 1536
FC = 512


def middle_kernel(
    att_ref, conv_ref, inp_ref, cot_ref, w_out_ref, w_up_ref, w_down_ref, vec_ref,
    out_ref, dctx_ref, dfirst_ref, dvec_ref, *refs
):
    grad_refs = refs[:-7]
    acc_out, acc_up, acc_down, acc_vec, act_ref, slope_ref, flip_ref = refs[-7:]
    step = pl.program_id(0)
    last = pl.num_programs(0) - 1

    @pl.when(step == 0)
    def _():
        acc_out[...] = jnp.zeros_like(acc_out)
        acc_up[...] = jnp.zeros_like(acc_up)
        acc_down[...] = jnp.zeros_like(acc_down)
        acc_vec[...] = jnp.zeros_like(acc_vec)

    ctx = jnp.concatenate([att_ref[...], conv_ref[...]], -1)
    g_one, s_one = vec_ref[0:1, :], vec_ref[1:2, :]
    g_two, s_two = vec_ref[2:3, :], vec_ref[3:4, :]
    first_in = mm(ctx, w_out_ref[...]) + inp_ref[...].astype(F32)
    xh_one, r_one = norm_parts(first_in)
    first = xh_one * g_one + s_one
    first_low = first.astype(BF)
    outs = []
    for g in (0, 1):
        cols = slice(g * ATT, (g + 1) * ATT)
        total = None
        for f in range(FF // FC):
            hid = slice(f * FC, (f + 1) * FC)
            inner = mm_nt(first_low[:, cols], w_up_ref[g, hid, :])
            act, slope = gelu_both(inner)
            act = act.astype(BF)
            act_ref[g, :, hid] = act
            slope_ref[g, :, hid] = slope.astype(slope_ref.dtype)
            part = mm(act, w_down_ref[g, hid, :])
            total = part if total is None else total + part
        outs.append(total)
    xh_two, r_two = norm_parts(jnp.concatenate(outs, -1) + first)
    out_ref[...] = (xh_two * g_two + s_two).astype(BF)
    c = cot_ref[...].astype(F32)
    acc_vec[2] += fold_rows(c * xh_two)
    acc_vec[3] += fold_rows(c)
    d_second = norm_back(c, xh_two, r_two, g_two)
    d_outer = d_second.astype(BF)
    d_outer_t = d_second.T.astype(BF)
    first_t = first.T.astype(BF)
    backs = []
    for g in (0, 1):
        cols = slice(g * ATT, (g + 1) * ATT)
        total = None
        for f in range(FF // FC):
            hid = slice(f * FC, (f + 1) * FC)
            d_act = mm_nt(d_outer[:, cols], w_down_ref[g, hid, :])
            d_inner = (d_act * slope_ref[g, :, hid].astype(F32)).astype(BF)
            acc_down[g, :, hid] += mm(d_outer_t[cols, :], act_ref[g, :, hid])
            acc_up[g, :, hid] += mm(first_t[cols, :], d_inner)
            part = mm(d_inner, w_up_ref[g, hid, :])
            total = part if total is None else total + part
        backs.append(total)
    d_first = jnp.concatenate(backs, -1) + d_second
    acc_vec[0] += fold_rows(d_first * xh_one)
    acc_vec[1] += fold_rows(d_first)
    d_first_in = norm_back(d_first, xh_one, r_one, g_one)
    dfirst_ref[...] = d_first_in
    d_dense = d_first_in.astype(BF)
    acc_out[...] += mm_tn(ctx, d_dense)
    dctx_ref[...] = mm_nt(d_dense, w_out_ref[...]).astype(BF)

    @pl.when(step == last)
    def _():
        dvec_ref[...] = jnp.sum(acc_vec[...], 1)
        if len(grad_refs) == 3:
            dout_ref, dup_ref, ddown_ref = grad_refs
            dout_ref[...] = acc_out[...].astype(BF)
            for g in (0, 1):
                dup_ref[g] = acc_up[g].T.astype(BF)
                ddown_ref[g] = acc_down[g].T.astype(BF)
            return
        for g in (0, 1):
            flip_ref[0, g] = acc_up[g].T.astype(BF)
            flip_ref[1, g] = acc_down[g].T.astype(BF)
        packed = grad_refs[0]

        def emit(i, carry):
            o = acc_out[pl.ds(pl.multiple_of(i * 24, 8), 24), :]
            packed[i, 0:48, :] = jnp.concatenate([o[:, :ATT], o[:, ATT:]], 0).astype(BF)
            hidden = pl.ds(pl.multiple_of(i * 48, 16), 48)
            for n in range(4):
                packed[i, 48 * n + 48 : 48 * n + 96, :] = flip_ref[n // 2, n % 2, hidden, :]
            return carry

        lax.fori_loop(0, 32, emit, 0)


def middle(att, conv, inputs, cot, w_out, w_up, w_down, vecs, packed):
    rows = att.shape[0]
    block = lambda n: pl.BlockSpec((MID, n), lambda s: (s, 0))
    grad_shapes = [(32, 240, LANES)] if packed else [(WIDTH, WIDTH), (2, FF, ATT), (2, FF, ATT)]
    return pl.pallas_call(
        middle_kernel,
        grid=(rows // MID,),
        in_specs=[
            block(ATT), block(ATT), block(WIDTH), block(WIDTH),
            whole((WIDTH, WIDTH)), whole((2, FF, ATT)), whole((2, FF, ATT)), whole((4, WIDTH)),
        ],
        out_specs=[block(WIDTH), block(WIDTH), block(WIDTH), whole_out((4, WIDTH))]
        + [whole_out(s) for s in grad_shapes],
        out_shape=[
            jax.ShapeDtypeStruct((rows, WIDTH), BF),
            jax.ShapeDtypeStruct((rows, WIDTH), BF),
            jax.ShapeDtypeStruct((rows, WIDTH), F32),
            jax.ShapeDtypeStruct((4, WIDTH), F32),
        ]
        + [jax.ShapeDtypeStruct(s, BF) for s in grad_shapes],
        scratch_shapes=[
            pltpu.VMEM((WIDTH, WIDTH), F32),
            pltpu.VMEM((2, ATT, FF), F32),
            pltpu.VMEM((2, ATT, FF), F32),
            pltpu.VMEM((4, 8, WIDTH), F32),
            pltpu.VMEM((2, MID, FF), BF),
            pltpu.VMEM((2, MID, FF), F32),
            pltpu.VMEM((2, 2, FF, ATT), BF),
        ],
        compiler_params=params(1),
        cost_estimate=cost(60e9, 40e6),
        name="middle",
    )(att, conv, inputs, cot, w_out, w_up, w_down, vecs)


def conv_back_kernel(
    dconv_ref, kern_ref, q_ref, cv_ref, ck_ref, spread_ref, inp_ref, w_depth_ref, w_point_ref, w_kern_ref,
    dq_ref, dcv_ref, din_ref, dpoint_ref, dkern_ref, ddepth_ref,
    x_pad, cv_pad, dc_pad, kl_pad, ds_pad, acc_point, acc_kern, acc_depth,
):
    step = pl.program_id(0)
    last = pl.num_programs(0) - 1
    zero = lambda n: jnp.zeros((8, n), F32)
    for ref, n in ((x_pad, WIDTH), (cv_pad, ATT), (dc_pad, ATT), (kl_pad, 128), (ds_pad, WIDTH)):
        ref[0:8, :] = zero(n)
        ref[SEQ + 8 : SEQ + 16, :] = zero(n)

    @pl.when(step == 0)
    def _():
        acc_point[...] = jnp.zeros_like(acc_point)
        acc_kern[...] = jnp.zeros_like(acc_kern)
        acc_depth[...] = jnp.zeros_like(acc_depth)

    def fill(i, carry):
        r = pl.multiple_of(i * CH, CH)
        rows = pl.ds(r, CH)
        there = pl.ds(r + 8, CH)
        x_pad[there, :] = inp_ref[rows, :].astype(F32)
        cv_pad[there, :] = cv_ref[rows, :].astype(F32)
        dc_pad[there, :] = dconv_ref[rows, :].astype(F32)
        kl_pad[there, :] = kern_ref[rows, :]
        return carry

    lax.fori_loop(0, SEQ // CH, fill, 0)

    def back(i, carry):
        r = pl.multiple_of(i * CH, CH)
        rows = pl.ds(r, CH)
        d_kern = jnp.zeros((CH, 128), F32)
        kl = kl_pad[pl.ds(r, HALO), :].astype(BF)
        for b in range(ATT // 128):
            lanes = slice(b * 128, (b + 1) * 128)
            spreader = tap_spread(b)
            cs = cv_pad[pl.ds(r, HALO), lanes]
            dc = dc_pad[pl.ds(r + 8, CH), lanes]
            prods = []
            for j in range(KER):
                moved = cs if j == 4 else pltpu.roll(cs, (HALO - (j - 4)) % HALO, 0)
                prods.append((dc * moved[8 : 8 + CH]).astype(BF))
            d_kern = d_kern + mm_nt(jnp.concatenate(prods, -1), spreader)
            wide = mm(kl, spreader)
            dch = dc_pad[pl.ds(r, HALO), lanes]
            total = jnp.zeros((CH, 128), F32)
            for j in range(KER):
                term = wide[:, j * 128 : (j + 1) * 128] * dch
                moved = term if j == 4 else pltpu.roll(term, (HALO + (j - 4)) % HALO, 0)
                total = total + moved[8 : 8 + CH]
            dcv_ref[rows, lanes] = total.astype(BF)
        kern = kern_ref[rows, :]
        dot_rows = lane_groups(kern * d_kern, jnp.add)
        d_logits = (kern * (d_kern - dot_rows)).astype(BF)
        q = q_ref[rows, :].astype(F32)
        ck = ck_ref[rows, :].astype(F32)
        mixed = (ck * q).astype(BF)
        acc_kern[...] += mm_tn(mixed, d_logits)
        d_mixed = mm_nt(d_logits, w_kern_ref[...])
        dq_ref[rows, :] = d_mixed * ck
        d_ck = (d_mixed * q).astype(BF)
        acc_point[...] += mm_tn(spread_ref[rows, :], d_ck)
        ds_pad[pl.ds(r + 8, CH), :] = mm_nt(d_ck, w_point_ref[...])
        return carry

    lax.fori_loop(0, SEQ // CH, back, 0)

    def depth(i, carry):
        r = pl.multiple_of(i * CH, CH)
        rows = pl.ds(r, CH)
        for b in range(WIDTH // 128):
            lanes = slice(b * 128, (b + 1) * 128)
            dsh = ds_pad[pl.ds(r, HALO), lanes]
            tap = lambda j: w_depth_ref[j : j + 1, lanes]
            shifted = [dsh] + [pltpu.roll(dsh, s, 0) for s in (1, 2, 3)]
            low_part = sum(tap(s) * shifted[s] for s in range(4))
            mid_part = sum(tap(4 + s) * shifted[s] for s in range(4))
            high_part = tap(8) * dsh
            low_part = pltpu.roll(low_part, HALO - 4, 0)
            high_part = pltpu.roll(high_part, 4, 0)
            din_ref[rows, lanes] = (low_part + mid_part + high_part)[8 : 8 + CH]
            xs = x_pad[pl.ds(r + 8, CH), lanes]
            far_low = [pltpu.roll(shifted[s], HALO - 4, 0) for s in range(4)]
            far_high = pltpu.roll(dsh, 4, 0)
            for j in range(KER):
                src = far_low[j] if j < 4 else (shifted[j - 4] if j < 8 else far_high)
                acc_depth[j, :, lanes] += fold_rows(src[8 : 8 + CH] * xs)
        return carry

    lax.fori_loop(0, SEQ // CH, depth, 0)

    @pl.when(step == last)
    def _():
        dpoint_ref[...] = acc_point[...]
        dkern_ref[...] = acc_kern[...]
        ddepth_ref[...] = jnp.sum(acc_depth[...], 1)


def conv_back(dctx, kern, proj, ck, spread, inputs, w_depth, w_point, w_kern):
    rows = inputs.shape[0]
    block = lambda n: pl.BlockSpec((SEQ, n), lambda s: (s, 0))
    at = lambda c: pl.BlockSpec((SEQ, ATT), lambda s: (s, c))
    return pl.pallas_call(
        conv_back_kernel,
        grid=(rows // SEQ,),
        in_specs=[
            at(1), block(128), at(0), at(3), block(ATT), block(WIDTH), block(WIDTH),
            whole((KER, WIDTH)), whole((WIDTH, ATT)), whole((ATT, 128)),
        ],
        out_specs=[
            block(ATT), block(ATT), block(WIDTH), whole_out((WIDTH, ATT)), whole_out((ATT, 128)),
            whole_out((KER, WIDTH)),
        ],
        out_shape=[
            jax.ShapeDtypeStruct((rows, ATT), F32),
            jax.ShapeDtypeStruct((rows, ATT), BF),
            jax.ShapeDtypeStruct((rows, WIDTH), F32),
            jax.ShapeDtypeStruct((WIDTH, ATT), F32),
            jax.ShapeDtypeStruct((ATT, 128), F32),
            jax.ShapeDtypeStruct((KER, WIDTH), F32),
        ],
        scratch_shapes=[
            pltpu.VMEM((SEQ + 16, WIDTH), F32),
            pltpu.VMEM((SEQ + 16, ATT), F32),
            pltpu.VMEM((SEQ + 16, ATT), F32),
            pltpu.VMEM((SEQ + 16, 128), F32),
            pltpu.VMEM((SEQ + 16, WIDTH), F32),
            pltpu.VMEM((WIDTH, ATT), F32),
            pltpu.VMEM((ATT, 128), F32),
            pltpu.VMEM((KER, 8, WIDTH), F32),
        ],
        compiler_params=params(1),
        cost_estimate=cost(25e9, 30e6),
        name="conv_back",
    )(dctx, kern, proj, proj, ck, spread, inputs, w_depth, w_point, w_kern)


def attend_back_kernel(
    q_ref, k_ref, v_ref, p_ref, o_ref, inv_ref, datt_ref, dqc_ref, dq_ref, dk_ref, dv_ref, acc_k, acc_v
):
    scale = HEAD**-0.5
    acc_k[...] = jnp.zeros_like(acc_k)
    acc_v[...] = jnp.zeros_like(acc_v)
    v = v_ref[...]

    def part(i, carry):
        r = pl.multiple_of(i * CH, CH)
        rows = pl.ds(r, CH)
        d_att = datt_ref[rows, :].astype(F32) * inv_ref[rows, :]
        o = o_ref[rows, :].astype(F32)
        dq = dqc_ref[rows, :]
        for head in (0, 1):
            mine = own_lanes(CH, head)
            da = jnp.where(mine, d_att, 0.0)
            dot_rows = jnp.sum(da * o, -1, keepdims=True)
            da = da.astype(BF)
            p = p_ref[0, head, rows, :]
            ds = mm_nt(da, v)
            ds = (p.astype(F32) * (ds - dot_rows)).astype(BF)
            k_own = jnp.where(own_lanes(SEQ, head), k_ref[...].astype(F32) * scale, 0.0).astype(BF)
            dq = dq + mm(ds, k_own)
            q_own = jnp.where(mine, q_ref[rows, :].astype(F32) * scale, 0.0)
            acc_k[...] += mm_tn(ds, q_own.astype(BF))
            acc_v[...] += mm_tn(p, da)
        dq_ref[rows, :] = dq.astype(BF)
        return carry

    lax.fori_loop(0, SEQ // CH, part, 0)
    dk_ref[...] = acc_k[...].astype(BF)
    dv_ref[...] = acc_v[...].astype(BF)


def attend_back(proj, probs, att, inv, dctx, dq_conv):
    rows = proj.shape[0]
    pairs = HEADS // 2
    col = lambda base: pl.BlockSpec((SEQ, 128), lambda s, p: (s, base + p))
    return pl.pallas_call(
        attend_back_kernel,
        grid=(rows // SEQ, pairs),
        in_specs=[
            col(0), col(pairs), col(2 * pairs),
            pl.BlockSpec((1, 2, SEQ, SEQ), lambda s, p: (s, p, 0, 0)),
            col(0), col(0), col(0), col(0),
        ],
        out_specs=[col(0)] * 3,
        out_shape=[jax.ShapeDtypeStruct((rows, ATT), BF)] * 3,
        scratch_shapes=[pltpu.VMEM((SEQ, 128), F32), pltpu.VMEM((SEQ, 128), F32)],
        compiler_params=params(2),
        cost_estimate=cost(30e9, 40e6),
        name="attend_back",
    )(proj, proj, proj, probs, att, inv, dctx, dq_conv)


def weight_kernel(core_ref, inp_ref, left_ref, right_ref, extra_ref, *refs):
    grad_refs, acc = refs[:-1], refs[-1]
    step = pl.program_id(0)
    last = pl.num_programs(0) - 1
    inp_t = inp_ref[...].astype(F32).T.astype(BF)
    for i, ref in enumerate((left_ref, right_ref)):
        cols = slice(i * ATT, (i + 1) * ATT)
        part = mm(inp_t, ref[...])

        @pl.when(step == 0)
        def _():
            acc[:, cols] = part

        @pl.when(step > 0)
        def _():
            acc[:, cols] += part

    @pl.when(step == last)
    def _():
        if len(grad_refs) == 1:
            grad_refs[0][...] = acc[...].astype(BF)
            return
        for c in (0, 1):

            def emit(i, carry):
                owner = (i // 8) * 16 + (core_ref[0] ^ c) * 8 + i % 8
                o = acc[pl.ds(pl.multiple_of(owner * 24, 8), 24), :]
                rows = jnp.concatenate([o[:, :ATT], o[:, ATT:], extra_ref[owner]], 0)
                grad_refs[c][i] = rows.astype(BF)
                return carry

            lax.fori_loop(0, 16, emit, 0)


def weight_grad(inputs, left, right, extra=None, core=None):
    rows = inputs.shape[0]
    block = lambda n: pl.BlockSpec((512, n), lambda s: (s, 0))
    if core is None:
        shapes, core, extra = [(WIDTH, 2 * ATT)], jnp.zeros((1,), jnp.int32), jnp.zeros((1, 8, LANES), F32)
    else:
        shapes = [(16, 48 + extra.shape[1], LANES)] * 2
    return pl.pallas_call(
        weight_kernel,
        grid=(rows // 512,),
        in_specs=[pl.BlockSpec(memory_space=pltpu.SMEM), block(WIDTH), block(ATT), block(ATT)]
        + [whole(extra.shape)],
        out_specs=[whole_out(s) for s in shapes],
        out_shape=[jax.ShapeDtypeStruct(s, BF) for s in shapes],
        scratch_shapes=[pltpu.VMEM((WIDTH, 2 * ATT), F32)],
        compiler_params=params(1),
        cost_estimate=cost(5e9, 8e6),
        name="weight_grad",
    )(core, inputs, left, right, extra)


def leave_kernel(
    dq_ref, dk_ref, dv_ref, dcv_ref, conv_ref, first_ref, mask_ref, to_ref, w_in_ref, *refs
):
    out_ref, moved = refs[-2:]
    def make(i, carry):
        rows = pl.ds(pl.multiple_of(i * CH, CH), CH)
        total = conv_ref[rows, :] + first_ref[rows, :]
        for n, ref in enumerate((dq_ref, dk_ref, dv_ref, dcv_ref)):
            total = total + mm_nt(ref[rows, :], w_in_ref[:, n * ATT : (n + 1) * ATT])
        moved[rows, :] = total.astype(BF)
        out_ref[rows, :] = jnp.where(mask_ref[rows, :] == 1, 0.0, total)
        return carry

    lax.fori_loop(0, SEQ // CH, make, 0)

    def scatter(i, carry):
        r = pl.multiple_of(i * CH, CH)
        rows = pl.ds(r, CH)
        target = lax.broadcasted_iota(jnp.int32, (CH, SEQ), 0) + r
        hot = (target == to_ref[0]).astype(F32).astype(BF)
        out_ref[rows, :] += mm(hot, moved[...])
        return carry

    lax.fori_loop(0, SEQ // CH, scatter, 0)


def leave(dq, dk, dv, dcv, d_conv_in, d_first_in, mask_col, to_row, w_in, seq, earlier=None):
    rows = dq.shape[0]
    block = lambda n: pl.BlockSpec((SEQ, n), lambda s: (seq, 0))
    extra = [] if earlier is None else [earlier]
    return pl.pallas_call(
        leave_kernel,
        grid=(1,),
        in_specs=[block(ATT)] * 4
        + [block(WIDTH)] * 2
        + [block(1), pl.BlockSpec((1, 1, SEQ), lambda s: (seq, 0, 0)), whole((WIDTH, 4 * ATT))]
        + [pl.BlockSpec(memory_space=pl.ANY)] * len(extra),
        out_specs=block(WIDTH),
        out_shape=jax.ShapeDtypeStruct((rows, WIDTH), F32),
        scratch_shapes=[pltpu.VMEM((SEQ, WIDTH), BF)],
        input_output_aliases={9: 0} if extra else {},
        compiler_params=params(1),
        cost_estimate=cost(8e9, 15e6),
        name="leave",
    )(dq, dk, dv, dcv, d_conv_in, d_first_in, mask_col, to_row, w_in, *extra)


def pack_taps(kernel_full):
    by_tap = kernel_full.reshape(ATT, HEADS, KER).transpose(0, 2, 1)
    return jnp.pad(by_tap, ((0, 0), (0, 16 - KER), (0, 8 - HEADS))).reshape(ATT, 128)


def unpack_taps(packed):
    return packed.reshape(ATT, 16, 8)[:, :KER, :HEADS].transpose(0, 2, 1).reshape(ATT, HEADS * KER)


def per_device(
    tokens,
    masked,
    replace_ids,
    in_weight,
    depth_weight,
    point_weight,
    kernel_weight,
    out_weight,
    gain_one,
    shift_one,
    ffn_in,
    feedforward_output,
    gain_two,
    shift_two,
    cotangent,
):
    rows = tokens.shape[0]
    seqs = rows // SEQ
    dp, fsdp = lax.axis_size("dp"), lax.axis_size("fsdp")
    devices = dp * fsdp
    near = dp == 4 and fsdp == 8
    own, hid = in_weight.shape[0], ffn_in.shape[2]
    n_depth, n_vec, n_kern = KER * own, 4 * own, kernel_weight.size
    hit = masked == 1
    here = jnp.arange(rows, dtype=jnp.int32) % SEQ
    pick = jnp.where(hit, replace_ids, here)[:, None]
    to_row = jnp.where(hit, replace_ids, -1).reshape(seqs, 1, SEQ)

    small_own = as_rows(jnp.concatenate([depth_weight.reshape(-1), kernel_weight.reshape(-1)]))
    mid_own = jnp.concatenate(
        [
            out_weight.reshape(-1, LANES),
            ffn_in.transpose(0, 2, 1).reshape(-1, LANES),
            feedforward_output.reshape(-1, LANES),
            as_rows(jnp.stack([gain_one, shift_one, gain_two, shift_two])),
        ]
    )
    if near:
        big = jnp.concatenate([in_weight.reshape(own, 4, ATT).transpose(1, 0, 2), point_weight[None]])
        slabs = pair_slabs(big, small_own)
        mid_own, *slabs = lax.optimization_barrier((mid_own, *slabs))
        small_all = jnp.stack([s[240:256] for s in slabs]).reshape(16, -1)
        place = (lax.axis_index("dp") * 8 + lax.axis_index("fsdp")) // 2
        back = [SLAB_BITS.index(b) for b in range(16)]
        order = jnp.take(jnp.array(back, jnp.int32), jnp.arange(16, dtype=jnp.int32) ^ place)
        small_all = jnp.take(small_all, order, axis=0).reshape(devices, -1)
    else:
        head_own = jnp.concatenate([in_weight.reshape(-1, LANES), point_weight, small_own])
        head = lax.all_gather(head_own, AXES, axis=0)
        w_in = head[:, : 4 * own].reshape(WIDTH, 4 * ATT)
        w_point = head[:, 4 * own : 5 * own].reshape(WIDTH, ATT)
        small_all = head[:, 5 * own :].reshape(devices, -1)
    mid = lax.all_gather(mid_own, AXES, axis=0)
    w_depth = small_all[:, :n_depth].reshape(devices, KER, own).transpose(1, 0, 2).reshape(KER, WIDTH)
    w_depth = w_depth.astype(F32)
    w_kern = pack_taps(small_all[:fsdp, n_depth : n_depth + n_kern].reshape(ATT, HEADS * KER))
    w_out = mid[:, : 2 * own].reshape(WIDTH, WIDTH)
    up = mid[:, 2 * own : 2 * own + 2 * hid].reshape(devices, 2, hid, ATT)
    w_up_t = up.transpose(1, 0, 2, 3).reshape(2, FF, ATT)
    down = mid[:, 2 * own + 2 * hid : 2 * own + 4 * hid].reshape(devices, 2, hid, ATT)
    w_down = down.transpose(1, 0, 2, 3).reshape(2, FF, ATT)
    vecs = mid[:, 2 * own + 4 * hid :].reshape(devices, -1)[:, :n_vec].reshape(devices, 4, own)
    vecs = vecs.transpose(1, 0, 2).reshape(4, WIDTH).astype(F32)

    if near:
        core = seat("core").astype(jnp.int32).reshape(1)
        inputs, proj, spread, ck, kern, conv, w_in, w_point = enter_slabs(
            pick, tokens, w_depth, w_kern, slabs
        )
    else:
        core = None
        inputs, proj, spread, ck, kern, conv = enter(pick, tokens, w_in, w_depth, w_point, w_kern)
    probs, att, inv = attend(proj)
    out, dctx, d_first_in, d_vecs, *mid_grads = middle(
        att, conv, inputs, cotangent, w_out, w_up_t, w_down, vecs, near
    )
    if near:
        mid_packed = mid_grads[0]
    else:
        d_out, d_up, d_down = mid_grads
        split = lambda g: g.reshape(2, devices, hid, ATT).transpose(1, 0, 2, 3).reshape(devices, -1, LANES)
        mid_packed = jnp.concatenate([d_out.reshape(devices, -1, LANES), split(d_up), split(d_down)], 1)
    mid_sum = lax.psum_scatter(mid_packed, AXES, scatter_dimension=0, tiled=True)[0]
    dq_conv, dcv, d_conv_in, d_point, d_kern, d_depth = conv_back(
        dctx, kern, proj, ck, spread, inputs, w_depth, w_point, w_kern
    )
    by_owner = lambda g: g.reshape(-1, devices, own).transpose(1, 0, 2).reshape(devices, -1)
    kern_by = jnp.tile(unpack_taps(d_kern).reshape(fsdp, -1), (dp, 1))
    small_grad = jnp.concatenate([by_owner(d_depth), by_owner(d_vecs), kern_by], 1)
    small_grad = jnp.pad(small_grad, ((0, 0), (0, -small_grad.shape[1] % LANES)))
    small_grad = small_grad.reshape(devices, -1, LANES)
    dq, dk, dv = attend_back(proj, probs, att, inv, dctx, dq_conv)
    mask_col = masked[:, None]
    if near:
        part_b = weight_grad(inputs, dv, dcv, d_point.reshape(devices, -1, LANES), core)
        part_a = weight_grad(inputs, dq, dk, small_grad, core)
        part_b, left_b = fold_step(spread_out(part_b, "core"), SPAN, "y")
        part_a, left_a = fold_step(spread_out(part_a, "core"), SPAN, "x")
        (part_a, part_b), dq = tie((part_a, part_b), dq)
        d_tokens = leave(dq, dk, dv, dcv, d_conv_in, d_first_in, mask_col, to_row, w_in, 0)
        for seq in range(1, seqs):
            if seq == 1:
                sent = (spread_out(part_a, "x"), spread_out(part_b, "y"))
                d_tokens, sent = tie(d_tokens, sent)
                part_a, left_a = fold_step(sent[0], left_a, "z")
                part_b, left_b = fold_step(sent[1], left_b, "z")
                (part_a, part_b), dq = tie((part_a, part_b), dq)
            d_tokens = leave(dq, dk, dv, dcv, d_conv_in, d_first_in, mask_col, to_row, w_in, seq, d_tokens)
        sent = (spread_out(part_a, "z"), spread_out(part_b, "z"))
        d_tokens, sent = tie(d_tokens, sent)
        part_a, _ = fold_step(sent[0], left_a, "y")
        part_b, _ = fold_step(sent[1], left_b, "x")
        total = lambda parts: sum(p.astype(F32) for p in parts).reshape(-1, LANES)
        sum_a, sum_b = total(spread_out(part_a, "y")), total(spread_out(part_b, "x"))
        d_in = jnp.concatenate([sum_a[:own], sum_a[own : 2 * own], sum_b[:own], sum_b[own : 2 * own]], 1)
        small_sum, d_point = sum_a[2 * own :], sum_b[2 * own :]
        d_out = jnp.concatenate([mid_sum[:own], mid_sum[own : 2 * own]], 1)
    else:
        d_in = jnp.concatenate(weight_grad(inputs, dq, dk) + weight_grad(inputs, dv, dcv), 1)
        packed = [d_in.reshape(devices, -1, LANES)]
        packed += [g.astype(BF) for g in (d_point.reshape(devices, -1, LANES), small_grad)]
        packed = jnp.concatenate(packed, 1)
        total = lax.psum_scatter(packed, AXES, scatter_dimension=0, tiled=True)[0].astype(F32)
        d_in, d_point = total[: 4 * own].reshape(own, 4 * ATT), total[4 * own : 5 * own]
        small_sum = total[5 * own :]
        d_out = mid_sum[: 2 * own].reshape(own, WIDTH)
        d_tokens = None
        for seq in range(seqs):
            d_tokens = leave(dq, dk, dv, dcv, d_conv_in, d_first_in, mask_col, to_row, w_in, seq, d_tokens)
    d_up, d_down = mid_sum[2 * own : 2 * own + 2 * hid], mid_sum[2 * own + 2 * hid :]

    scale = 1.0 / math.sqrt(rows * devices)
    small_sum = small_sum.reshape(-1) * scale
    vec_sum = small_sum[n_depth : n_depth + n_vec].reshape(4, own)
    kern_sum = small_sum[n_depth + n_vec :][:n_kern].reshape(kernel_weight.shape)
    return (
        out,
        d_tokens,
        d_in * scale,
        small_sum[:n_depth].reshape(KER, own),
        d_point * scale,
        kern_sum,
        d_out.astype(F32) * scale,
        vec_sum[0],
        vec_sum[1],
        d_up.astype(F32).reshape(2, hid, ATT).transpose(0, 2, 1) * scale,
        d_down.astype(F32).reshape(2, hid, ATT) * scale,
        vec_sum[2],
        vec_sum[3],
    )


def solution(mesh):
    return jax.shard_map(
        per_device,
        mesh=mesh,
        in_specs=(
            P(("dp", "fsdp"), None),
            P(("dp", "fsdp")),
            P(("dp", "fsdp")),
            P(("dp", "fsdp"), None),
            P(None, ("dp", "fsdp")),
            P(("dp", "fsdp"), None),
            P("fsdp", None),
            P(("dp", "fsdp"), None),
            P(("dp", "fsdp")),
            P(("dp", "fsdp")),
            P(None, None, ("dp", "fsdp")),
            P(None, ("dp", "fsdp"), None),
            P(("dp", "fsdp")),
            P(("dp", "fsdp")),
            P(("dp", "fsdp"), None),
        ),
        out_specs=(
            P(("dp", "fsdp"), None),
            P(("dp", "fsdp"), None),
            P(("dp", "fsdp"), None),
            P(None, ("dp", "fsdp")),
            P(("dp", "fsdp"), None),
            P("fsdp", None),
            P(("dp", "fsdp"), None),
            P(("dp", "fsdp")),
            P(("dp", "fsdp")),
            P(None, None, ("dp", "fsdp")),
            P(None, ("dp", "fsdp"), None),
            P(("dp", "fsdp")),
            P(("dp", "fsdp")),
        ),
        check_vma=False,
    )
```

```python
from functools import partial
import math

import jax
import jax.numpy as jnp
from jax import lax
from jax.experimental import pallas as pl
from jax.experimental.pallas import tpu as pltpu
from jax.sharding import PartitionSpec as P

BF = jnp.bfloat16
F32 = jnp.float32
HEADS = 6
HEAD = 64
SEQ = 1024
KER = 9
ATT = HEADS * HEAD
WIDTH = 768
VMEM_MAX = 60 * 1024 * 1024


def mm(a, b):
    return jnp.dot(a, b, preferred_element_type=F32)


def mm_nt(a, b):
    return lax.dot_general(a, b, (((1,), (1,)), ((), ())), preferred_element_type=F32)


def mm_tn(a, b):
    return lax.dot_general(a, b, (((0,), (0,)), ((), ())), preferred_element_type=F32)


def params(count):
    return pltpu.CompilerParams(
        dimension_semantics=("arbitrary",) * count, vmem_limit_bytes=VMEM_MAX
    )


def cost(flops, moved):
    return pl.CostEstimate(flops=int(flops), bytes_accessed=int(moved), transcendentals=0)


def whole(shape):
    zeros = (0,) * len(shape)
    return pl.BlockSpec(shape, lambda *_: zeros, pipeline_mode=pl.Buffered(1))


def whole_out(shape):
    zeros = (0,) * len(shape)
    return pl.BlockSpec(shape, lambda *_: zeros)


AXES = ("dp", "fsdp")
LANES = 384
NEAR = {"dp": 4, "fsdp": 8}
X_BIT, CORE_BIT, Z_BIT, Y_BIT = 16, 8, 2, 1


def as_rows(x):
    flat = x.reshape(-1)
    return jnp.pad(flat, (0, -flat.size % LANES)).reshape(-1, LANES)


def place():
    return lax.axis_index("dp") * NEAR["fsdp"] + lax.axis_index("fsdp")


def hop(x, mask):
    return lax.ppermute(x, AXES, [(i, i ^ mask) for i in range(32)])


def tie(first, second):
    return lax.optimization_barrier((first, second))


def fold_xy_kernel(me_ref, mine_ref, other_ref, *outs):
    x, y = me_ref[0] // X_BIT, me_ref[0] % 2
    for k, out in enumerate(outs):
        at = (x ^ (k // 2), 0, y ^ (k % 2))
        out[0] = (mine_ref[at].astype(F32) + other_ref[at].astype(F32)).astype(BF)


def fold_xy(me, mine, other):
    rows = mine.shape[-2]
    views = [a.reshape(2, 4, 2, rows, LANES) for a in (mine, other)]
    return pl.pallas_call(
        fold_xy_kernel,
        grid=(4,),
        in_specs=[pl.BlockSpec(memory_space=pltpu.SMEM)]
        + [pl.BlockSpec((2, 1, 2, rows, LANES), lambda z: (0, z, 0, 0, 0))] * 2,
        out_specs=[pl.BlockSpec((1, rows, LANES), lambda z: (z, 0, 0))] * 4,
        out_shape=[jax.ShapeDtypeStruct((4, rows, LANES), BF)] * 4,
        compiler_params=params(1),
        cost_estimate=cost(0, 6 * mine.size),
        name="fold_xy",
    )(me, *views)


def fold_z_kernel(me_ref, *refs):
    z = (me_ref[0] // Z_BIT) % 4
    for k, out in enumerate(refs[4:]):
        total = refs[0][z ^ k].astype(F32)
        for ref in refs[1:4]:
            total = total + ref[z ^ k].astype(F32)
        out[...] = total.astype(BF)


def fold_z(me, arrays):
    rows = arrays[0].shape[-2]
    return pl.pallas_call(
        fold_z_kernel,
        in_specs=[pl.BlockSpec(memory_space=pltpu.SMEM)] + [pl.BlockSpec(memory_space=pltpu.VMEM)] * 4,
        out_specs=[pl.BlockSpec(memory_space=pltpu.VMEM)] * 4,
        out_shape=[jax.ShapeDtypeStruct((rows, LANES), BF)] * 4,
        compiler_params=pltpu.CompilerParams(vmem_limit_bytes=16 * 1024 * 1024),
        cost_estimate=cost(0, 10 * arrays[0].size),
        name="fold_z",
    )(me, *arrays)


def finish_kernel(scale, a_ref, b_ref, c_ref, d_ref, in_ref, point_ref, small_ref):
    total = sum(ref[...].astype(F32) for ref in (a_ref, b_ref, c_ref, d_ref)) * scale
    for n in range(4):
        in_ref[:, n * ATT : (n + 1) * ATT] = total[24 * n : 24 * n + 24]
    point_ref[...] = total[96:120]
    small_ref[...] = total[120:128]


def finish(scale, arrays):
    vmem = pl.BlockSpec(memory_space=pltpu.VMEM)
    return pl.pallas_call(
        partial(finish_kernel, scale),
        in_specs=[vmem] * 4,
        out_specs=[vmem] * 3,
        out_shape=[
            jax.ShapeDtypeStruct((24, 4 * ATT), F32),
            jax.ShapeDtypeStruct((24, ATT), F32),
            jax.ShapeDtypeStruct((8, LANES), F32),
        ],
        name="finish",
    )(*arrays)


def finish_mid_kernel(scale, sum_ref, out_ref, up_ref, down_ref):
    total = sum_ref[...].astype(F32) * scale
    out_ref[:, :ATT] = total[:24]
    out_ref[:, ATT:] = total[24:48]
    for g in (0, 1):
        up_ref[g] = total[48 + 48 * g : 96 + 48 * g].T
        down_ref[g] = total[144 + 48 * g : 192 + 48 * g]


def finish_mid(scale, packed):
    vmem = pl.BlockSpec(memory_space=pltpu.VMEM)
    return pl.pallas_call(
        partial(finish_mid_kernel, scale),
        in_specs=[vmem],
        out_specs=[vmem] * 3,
        out_shape=[
            jax.ShapeDtypeStruct((24, WIDTH), F32),
            jax.ShapeDtypeStruct((2, ATT, 48), F32),
            jax.ShapeDtypeStruct((2, 48, ATT), F32),
        ],
        name="finish_mid",
    )(packed)


SLAB_BITS = [((s // 4) % 2 * X_BIT + (s // 8) * CORE_BIT + s % 4 * Z_BIT) // 2 for s in range(16)]


def pair_slab(own, small):
    packed = jnp.concatenate([own.reshape(-1, LANES), small])
    other = hop(packed, Y_BIT)
    even = place() % 2 == 0
    first, second = jnp.where(even, packed, other), jnp.where(even, other, packed)
    both = [x[:120].reshape(5, 24, LANES) for x in (first, second)]
    return jnp.concatenate([jnp.concatenate(both, 1).reshape(-1, LANES), first[120:], second[120:]])


def small_rows(slabs, pair):
    spot = jnp.array([SLAB_BITS.index(b) for b in range(16)], jnp.int32)
    order = jnp.take(spot, jnp.arange(16, dtype=jnp.int32) ^ pair)
    return jnp.take(jnp.stack([slab[240:] for slab in slabs]), order, axis=0).reshape(32, -1)


def lane_groups(x, combine):
    for step in (64, 32, 16, 8):
        x = combine(x, pltpu.roll(x, step, 1))
    return x


def tap_spread(block):
    rows = lax.broadcasted_iota(jnp.int32, (128, KER * 128), 0)
    cols = lax.broadcasted_iota(jnp.int32, (128, KER * 128), 1)
    want = (cols // 128) * 8 + block * 2 + (cols % 128) // HEAD
    return (rows == want).astype(F32).astype(BF)


EC = 1024
FB = 512
BB = 1024
DB = 512


def pick_kernel(pick_ref, tok_ref, inp_ref):
    cols = lax.broadcasted_iota(jnp.int32, (SEQ, SEQ), 1)
    hot = (cols == pick_ref[...]).astype(F32).astype(BF)
    inp_ref[...] = mm(hot, tok_ref[...]).astype(BF)


def pick_rows(pick, tokens):
    block = lambda n: pl.BlockSpec((SEQ, n), lambda s: (s, 0))
    return pl.pallas_call(
        pick_kernel,
        grid=(tokens.shape[0] // SEQ,),
        in_specs=[block(1), block(WIDTH)],
        out_specs=block(WIDTH),
        out_shape=jax.ShapeDtypeStruct(tokens.shape, BF),
        compiler_params=params(1),
        cost_estimate=cost(6e9, 6e6),
        name="pick",
    )(pick, tokens)


def enter_kernel(
    inp_ref, w_in_ref, w_depth_ref, w_point_ref, w_kern_ref,
    proj_ref, spread_ref, ck_ref, kern_ref, conv_ref,
    x_pad, cv_pad,
):
    x_pad[0:8, :] = jnp.zeros((8, WIDTH), F32)
    x_pad[SEQ + 8 : SEQ + 16, :] = jnp.zeros((8, WIDTH), F32)
    cv_pad[0:8, :] = jnp.zeros((8, ATT), F32)
    cv_pad[SEQ + 8 : SEQ + 16, :] = jnp.zeros((8, ATT), F32)

    def load(i, carry):
        r = pl.multiple_of(i * EC, EC)
        low = inp_ref[pl.ds(r, EC), :]
        x_pad[pl.ds(r + 8, EC), :] = low.astype(F32)
        proj = mm(low, w_in_ref[...])
        proj_low = proj.astype(BF)
        proj_ref[pl.ds(r, EC), :] = proj_low
        cv_pad[pl.ds(r + 8, EC), :] = proj_low[:, 3 * ATT :].astype(F32)
        return carry

    lax.fori_loop(0, SEQ // EC, load, 0)

    def conv(i, carry):
        r = pl.multiple_of(i * EC, EC)
        for b in range(WIDTH // 128):
            lanes = slice(b * 128, (b + 1) * 128)
            xs = x_pad[pl.ds(r, (EC + 16)), lanes]
            shifted = [xs] + [pltpu.roll(xs, (EC + 16) - s, 0) for s in (1, 2, 3)]
            tap = lambda j: w_depth_ref[j : j + 1, lanes]
            low_part = sum(tap(s) * shifted[s] for s in range(4))
            mid_part = sum(tap(4 + s) * shifted[s] for s in range(4))
            high_part = tap(8) * xs
            low_part = pltpu.roll(low_part, (EC + 16) - 4, 0)
            high_part = pltpu.roll(high_part, (EC + 16) - 4, 0)
            total = low_part[0:EC] + mid_part[8 : 8 + EC] + high_part[8 : 8 + EC]
            spread_ref[pl.ds(r, EC), lanes] = total.astype(BF)
        ck = mm(spread_ref[pl.ds(r, EC), :], w_point_ref[...]).astype(BF)
        ck_ref[pl.ds(r, EC), :] = ck
        q = proj_ref[pl.ds(r, EC), 0:ATT].astype(F32)
        mixed = (ck.astype(F32) * q).astype(BF)
        logits = mm(mixed, w_kern_ref[...])
        lane = lax.broadcasted_iota(jnp.int32, (EC, 128), 1)
        logits = jnp.where(lane < KER * 8, logits, -1e30)
        top = lane_groups(logits, jnp.maximum)
        e = jnp.exp(logits - top)
        kern = e / lane_groups(e, jnp.add)
        kern_ref[pl.ds(r, EC), :] = kern
        kern_low = kern.astype(BF)
        for b in range(ATT // 128):
            lanes = slice(b * 128, (b + 1) * 128)
            wide = mm(kern_low, tap_spread(b))
            cs = cv_pad[pl.ds(r, (EC + 16)), lanes]
            total = jnp.zeros((EC, 128), F32)
            for j in range(KER):
                moved = cs if j == 4 else pltpu.roll(cs, ((EC + 16) - (j - 4)) % (EC + 16), 0)
                total = total + wide[:, j * 128 : (j + 1) * 128] * moved[8 : 8 + EC]
            conv_ref[pl.ds(r, EC), lanes] = total.astype(BF)
        return carry

    lax.fori_loop(0, SEQ // EC, conv, 0)


def enter_slabs_kernel(pair_ref, inp_ref, w_depth_ref, w_kern_ref, *refs):
    slabs, outs = refs[:16], refs[16:]
    results, w_in_ref, w_point_ref, scratch, sems = outs[:5], outs[5], outs[6], outs[7:9], outs[9]

    @pl.when(pl.program_id(0) == 0)
    def _():
        copies = []
        for s, slab in enumerate(slabs):
            spot = pl.ds(pl.multiple_of((pair_ref[0] ^ SLAB_BITS[s]) * 48, 16), 48)
            for b in range(5):
                to = w_in_ref.at[spot, b * ATT : (b + 1) * ATT] if b < 4 else w_point_ref.at[spot, :]
                copies.append(pltpu.make_async_copy(slab.at[b * 48 : (b + 1) * 48, :], to, sems.at[s, b]))
        for copy in copies:
            copy.start()
        for copy in copies:
            copy.wait()

    enter_kernel(inp_ref, w_in_ref, w_depth_ref, w_point_ref, w_kern_ref, *results, *scratch)


def enter(inputs, pair, w_depth, w_kern, slabs):
    rows = inputs.shape[0]
    block = lambda n: pl.BlockSpec((SEQ, n), lambda s: (s, 0))
    widths = ((4 * ATT, BF), (WIDTH, BF), (ATT, BF), (128, F32), (ATT, BF))
    return pl.pallas_call(
        enter_slabs_kernel,
        grid=(rows // SEQ,),
        in_specs=[
            pl.BlockSpec(memory_space=pltpu.SMEM), block(WIDTH), whole((KER, WIDTH)), whole((ATT, 128)),
        ]
        + [pl.BlockSpec(memory_space=pl.ANY)] * 16,
        out_specs=[block(n) for n, _ in widths] + [whole_out((WIDTH, 4 * ATT)), whole_out((WIDTH, ATT))],
        out_shape=[jax.ShapeDtypeStruct((rows, n), t) for n, t in widths]
        + [jax.ShapeDtypeStruct((WIDTH, 4 * ATT), BF), jax.ShapeDtypeStruct((WIDTH, ATT), BF)],
        scratch_shapes=[
            pltpu.VMEM((SEQ + 16, WIDTH), F32),
            pltpu.VMEM((SEQ + 16, ATT), F32),
            pltpu.SemaphoreType.DMA((16, 5)),
        ],
        compiler_params=params(1),
        cost_estimate=cost(20e9, 20e6),
        name="enter",
    )(pair, inputs, w_depth, w_kern, *slabs)


def own_lanes(rows, head):
    lane = lax.broadcasted_iota(jnp.int32, (rows, 128), 1)
    return (lane // HEAD) == head


AC = 512


def attend_kernel(q_ref, k_ref, v_ref, p_ref, o_ref, inv_ref):
    k = k_ref[...]
    v_all = v_ref[...].astype(F32)
    vs = [jnp.where(own_lanes(SEQ, head), v_all, 1.0).astype(BF) for head in (0, 1)]
    first = own_lanes(AC, 0)

    def part(i, carry):
        rows = pl.ds(pl.multiple_of(i * AC, AC), AC)
        q_all = q_ref[rows, :].astype(F32) * (HEAD**-0.5)
        outs = []
        for head in (0, 1):
            q = jnp.where(first if head == 0 else ~first, q_all, 0.0).astype(BF)
            s = mm_nt(q, k)
            p = jnp.exp(s - jnp.max(s, -1, keepdims=True)).astype(BF)
            p_ref[0, head, rows, :] = p
            outs.append(mm(p, vs[head]))
        inv = 1.0 / pltpu.roll(jnp.where(first, outs[1], outs[0]), HEAD, 1)
        o_ref[rows, :] = (jnp.where(first, outs[0], outs[1]) * inv).astype(BF)
        inv_ref[rows, :] = inv
        return carry

    lax.fori_loop(0, SEQ // AC, part, 0, unroll=2)


def attend(proj):
    rows = proj.shape[0]
    pairs = HEADS // 2
    col = lambda base: pl.BlockSpec((SEQ, 128), lambda s, p: (s, base + p))
    return pl.pallas_call(
        attend_kernel,
        grid=(rows // SEQ, pairs),
        in_specs=[col(0), col(pairs), col(2 * pairs)],
        out_specs=[pl.BlockSpec((1, 2, SEQ, SEQ), lambda s, p: (s, p, 0, 0)), col(0), col(0)],
        out_shape=[
            jax.ShapeDtypeStruct((rows // SEQ, HEADS, SEQ, SEQ), BF),
            jax.ShapeDtypeStruct((rows, ATT), BF),
            jax.ShapeDtypeStruct((rows, ATT), F32),
        ],
        compiler_params=params(2),
        cost_estimate=cost(25e9, 35e6),
        name="attend",
    )(proj, proj, proj)


ERF_P = 0.3275911 / math.sqrt(2.0)
ERF_A = (0.254829592, -0.284496736, 1.421413741, -1.453152027, 1.061405429)
PHI = 1.0 / math.sqrt(2.0 * math.pi)


def gelu_both(u):
    mag = jnp.abs(u)
    t = 1.0 / (1.0 + ERF_P * mag)
    poly = ERF_A[4]
    for a in ERF_A[3::-1]:
        poly = poly * t + a
    e = jnp.exp(-0.5 * (u * u))
    tail = (0.5 * t) * poly * e
    cdf = jnp.where(u > 0, 1.0 - tail, tail)
    return u * cdf, cdf + (PHI * u) * e


def norm_parts(z):
    mean = jnp.mean(z, -1, keepdims=True)
    centred = z - mean
    var = jnp.mean(centred * centred, -1, keepdims=True)
    r = lax.rsqrt(var + 1e-12)
    return centred * r, r


def norm_back(c, xh, r, gain):
    gc = c * gain
    return r * (gc - jnp.mean(gc, -1, keepdims=True) - xh * jnp.mean(gc * xh, -1, keepdims=True))


def fold_rows(x):
    return jnp.sum(x.reshape(-1, 8, x.shape[-1]), 0)


MID = 256
FF = 1536
FC = 768
GROUP = 48
BLOCKS = FF // GROUP


def middle_kernel(
    att_ref, conv_ref, inp_ref, cot_ref, mid_ref, vec_ref,
    out_ref, dctx_ref, dfirst_ref, dvec_ref, packed_ref,
    acc_out, acc_up, acc_down, acc_vec, act_ref, slope_ref, flip_ref,
    w_out_ref, w_rows, w_up_blocks, w_down_blocks, sems,
):
    step = pl.program_id(0)
    last = pl.num_programs(0) - 1

    @pl.when(step == 0)
    def _():
        targets = [w_rows] + [w.at[g] for w in (w_up_blocks, w_down_blocks) for g in (0, 1)]
        copies = [
            pltpu.make_async_copy(mid_ref.at[:, n * GROUP : (n + 1) * GROUP, :], to, sems.at[n])
            for n, to in enumerate(targets)
        ]
        for copy in copies:
            copy.start()
        acc_up[...] = jnp.zeros_like(acc_up)
        acc_down[...] = jnp.zeros_like(acc_down)
        acc_vec[...] = jnp.zeros_like(acc_vec)
        copies[0].wait()
        half = GROUP // 2

        def unfold(i, carry):
            both = w_rows[i].astype(F32)
            rows = pl.ds(pl.multiple_of(i * half, 8), half)
            acc_out[rows, :] = jnp.concatenate([both[:half], both[half:]], 1)
            return carry

        lax.fori_loop(0, BLOCKS, unfold, 0)
        w_out_ref[...] = acc_out[...].astype(BF)
        acc_out[...] = jnp.zeros_like(acc_out)
        for copy in copies[1:]:
            copy.wait()

    def w_up(g, f):
        return w_up_blocks[g, f * FC // GROUP : (f + 1) * FC // GROUP].reshape(FC, ATT)

    def w_down(g, f):
        return w_down_blocks[g, f * FC // GROUP : (f + 1) * FC // GROUP].reshape(FC, ATT)

    ctx = jnp.concatenate([att_ref[...], conv_ref[...]], -1)
    g_one, s_one = vec_ref[0:1, :], vec_ref[1:2, :]
    g_two, s_two = vec_ref[2:3, :], vec_ref[3:4, :]
    first_in = mm(ctx, w_out_ref[...]) + inp_ref[...].astype(F32)
    xh_one, r_one = norm_parts(first_in)
    first = xh_one * g_one + s_one
    first_low = first.astype(BF)
    outs = []
    for g in (0, 1):
        cols = slice(g * ATT, (g + 1) * ATT)
        total = None
        for f in range(FF // FC):
            hid = slice(f * FC, (f + 1) * FC)
            inner = mm_nt(first_low[:, cols], w_up(g, f))
            act, slope = gelu_both(inner)
            act = act.astype(BF)
            act_ref[g, :, hid] = act
            slope_ref[g, :, hid] = slope.astype(slope_ref.dtype)
            part = mm(act, w_down(g, f))
            total = part if total is None else total + part
        outs.append(total)
    xh_two, r_two = norm_parts(jnp.concatenate(outs, -1) + first)
    out_ref[...] = (xh_two * g_two + s_two).astype(BF)
    c = cot_ref[...].astype(F32)
    acc_vec[2] += fold_rows(c * xh_two)
    acc_vec[3] += fold_rows(c)
    d_second = norm_back(c, xh_two, r_two, g_two)
    d_outer = d_second.astype(BF)
    d_outer_t = d_second.T.astype(BF)
    first_t = first.T.astype(BF)
    backs = []
    for g in (0, 1):
        cols = slice(g * ATT, (g + 1) * ATT)
        total = None
        for f in range(FF // FC):
            hid = slice(f * FC, (f + 1) * FC)
            d_act = mm_nt(d_outer[:, cols], w_down(g, f))
            d_inner = (d_act * slope_ref[g, :, hid].astype(F32)).astype(BF)
            acc_down[g, :, hid] += mm(d_outer_t[cols, :], act_ref[g, :, hid])
            acc_up[g, :, hid] += mm(first_t[cols, :], d_inner)
            part = mm(d_inner, w_up(g, f))
            total = part if total is None else total + part
        backs.append(total)
    d_first = jnp.concatenate(backs, -1) + d_second
    acc_vec[0] += fold_rows(d_first * xh_one)
    acc_vec[1] += fold_rows(d_first)
    d_first_in = norm_back(d_first, xh_one, r_one, g_one)
    dfirst_ref[...] = d_first_in
    d_dense = d_first_in.astype(BF)
    acc_out[...] += mm_tn(ctx, d_dense)
    dctx_ref[...] = mm_nt(d_dense, w_out_ref[...]).astype(BF)

    @pl.when(step == last)
    def _():
        dvec_ref[...] = jnp.sum(acc_vec[...], 1)
        for g in (0, 1):
            flip_ref[0, g] = acc_up[g].T.astype(BF)
            flip_ref[1, g] = acc_down[g].T.astype(BF)

        def emit(i, carry):
            o = acc_out[pl.ds(pl.multiple_of(i * 24, 8), 24), :]
            packed_ref[i, 0:48, :] = jnp.concatenate([o[:, :ATT], o[:, ATT:]], 0).astype(BF)
            hidden = pl.ds(pl.multiple_of(i * 48, 16), 48)
            for n in range(4):
                packed_ref[i, 48 * n + 48 : 48 * n + 96, :] = flip_ref[n // 2, n % 2, hidden, :]
            return carry

        lax.fori_loop(0, BLOCKS, emit, 0)


def middle(att, conv, inputs, cot, mid, vecs):
    rows = att.shape[0]
    block = lambda n: pl.BlockSpec((MID, n), lambda s: (s, 0))
    packed = (BLOCKS, 5 * GROUP, LANES)
    return pl.pallas_call(
        middle_kernel,
        grid=(rows // MID,),
        in_specs=[
            block(ATT), block(ATT), block(WIDTH), block(WIDTH),
            pl.BlockSpec(memory_space=pl.ANY), whole((4, WIDTH)),
        ],
        out_specs=[block(WIDTH), block(WIDTH), block(WIDTH), whole_out((4, WIDTH)), whole_out(packed)],
        out_shape=[
            jax.ShapeDtypeStruct((rows, WIDTH), BF),
            jax.ShapeDtypeStruct((rows, WIDTH), BF),
            jax.ShapeDtypeStruct((rows, WIDTH), F32),
            jax.ShapeDtypeStruct((4, WIDTH), F32),
            jax.ShapeDtypeStruct(packed, BF),
        ],
        scratch_shapes=[
            pltpu.VMEM((WIDTH, WIDTH), F32),
            pltpu.VMEM((2, ATT, FF), F32),
            pltpu.VMEM((2, ATT, FF), F32),
            pltpu.VMEM((4, 8, WIDTH), F32),
            pltpu.VMEM((2, MID, FF), BF),
            pltpu.VMEM((2, MID, FF), F32),
            pltpu.VMEM((2, 2, FF, ATT), BF),
            pltpu.VMEM((WIDTH, WIDTH), BF),
            pltpu.VMEM((BLOCKS, GROUP, LANES), BF),
            pltpu.VMEM((2, BLOCKS, GROUP, ATT), BF),
            pltpu.VMEM((2, BLOCKS, GROUP, ATT), BF),
            pltpu.SemaphoreType.DMA((5,)),
        ],
        compiler_params=params(1),
        cost_estimate=cost(60e9, 40e6),
        name="middle",
    )(att, conv, inputs, cot, mid, vecs)


def conv_back_kernel(
    dconv_ref, kern_ref, q_ref, cv_ref, ck_ref, spread_ref, inp_ref, first_ref, w_depth_ref, w_point_ref, w_kern_ref,
    dq_ref, dcv_ref, din_ref, dpoint_ref, dkern_ref, ddepth_ref,
    x_pad, cv_pad, dc_pad, kl_pad, ds_pad, acc_point, acc_kern, acc_depth,
):
    step = pl.program_id(0)
    last = pl.num_programs(0) - 1
    zero = lambda n: jnp.zeros((8, n), F32)
    for ref, n in ((x_pad, WIDTH), (cv_pad, ATT), (dc_pad, ATT), (kl_pad, 128), (ds_pad, WIDTH)):
        ref[0:8, :] = zero(n)
        ref[SEQ + 8 : SEQ + 16, :] = zero(n)

    @pl.when(step == 0)
    def _():
        acc_point[...] = jnp.zeros_like(acc_point)
        acc_kern[...] = jnp.zeros_like(acc_kern)
        acc_depth[...] = jnp.zeros_like(acc_depth)

    def fill(i, carry):
        r = pl.multiple_of(i * FB, FB)
        rows = pl.ds(r, FB)
        there = pl.ds(r + 8, FB)
        x_pad[there, :] = inp_ref[rows, :].astype(F32)
        cv_pad[there, :] = cv_ref[rows, :].astype(F32)
        dc_pad[there, :] = dconv_ref[rows, :].astype(F32)
        kl_pad[there, :] = kern_ref[rows, :]
        return carry

    lax.fori_loop(0, SEQ // FB, fill, 0)

    def back(i, carry):
        r = pl.multiple_of(i * BB, BB)
        rows = pl.ds(r, BB)
        d_kern = jnp.zeros((BB, 128), F32)
        kl = kl_pad[pl.ds(r, (BB + 16)), :].astype(BF)
        for b in range(ATT // 128):
            lanes = slice(b * 128, (b + 1) * 128)
            spreader = tap_spread(b)
            cs = cv_pad[pl.ds(r, (BB + 16)), lanes]
            dc = dc_pad[pl.ds(r + 8, BB), lanes]
            prods = []
            for j in range(KER):
                moved = cs if j == 4 else pltpu.roll(cs, ((BB + 16) - (j - 4)) % (BB + 16), 0)
                prods.append((dc * moved[8 : 8 + BB]).astype(BF))
            d_kern = d_kern + mm_nt(jnp.concatenate(prods, -1), spreader)
            wide = mm(kl, spreader)
            dch = dc_pad[pl.ds(r, (BB + 16)), lanes]
            total = jnp.zeros((BB, 128), F32)
            for j in range(KER):
                term = wide[:, j * 128 : (j + 1) * 128] * dch
                moved = term if j == 4 else pltpu.roll(term, ((BB + 16) + (j - 4)) % (BB + 16), 0)
                total = total + moved[8 : 8 + BB]
            dcv_ref[rows, lanes] = total.astype(BF)
        kern = kern_ref[rows, :]
        dot_rows = lane_groups(kern * d_kern, jnp.add)
        d_logits = (kern * (d_kern - dot_rows)).astype(BF)
        q = q_ref[rows, :].astype(F32)
        ck = ck_ref[rows, :].astype(F32)
        mixed = (ck * q).astype(BF)
        acc_kern[...] += mm_tn(mixed, d_logits)
        d_mixed = mm_nt(d_logits, w_kern_ref[...])
        dq_ref[rows, :] = d_mixed * ck
        d_ck = (d_mixed * q).astype(BF)
        acc_point[...] += mm_tn(spread_ref[rows, :], d_ck)
        ds_pad[pl.ds(r + 8, BB), :] = mm_nt(d_ck, w_point_ref[...])
        return carry

    lax.fori_loop(0, SEQ // BB, back, 0)

    def depth(i, carry):
        r = pl.multiple_of(i * DB, DB)
        rows = pl.ds(r, DB)
        for b in range(WIDTH // 128):
            lanes = slice(b * 128, (b + 1) * 128)
            dsh = ds_pad[pl.ds(r, (DB + 16)), lanes]
            tap = lambda j: w_depth_ref[j : j + 1, lanes]
            shifted = [dsh] + [pltpu.roll(dsh, s, 0) for s in (1, 2, 3)]
            low_part = sum(tap(s) * shifted[s] for s in range(4))
            mid_part = sum(tap(4 + s) * shifted[s] for s in range(4))
            high_part = tap(8) * dsh
            low_part = pltpu.roll(low_part, (DB + 16) - 4, 0)
            high_part = pltpu.roll(high_part, 4, 0)
            taps = (low_part + mid_part + high_part)[8 : 8 + DB]
            din_ref[rows, lanes] = taps + first_ref[rows, lanes]
            xs = x_pad[pl.ds(r + 8, DB), lanes]
            far_low = [pltpu.roll(shifted[s], (DB + 16) - 4, 0) for s in range(4)]
            far_high = pltpu.roll(dsh, 4, 0)
            for j in range(KER):
                src = far_low[j] if j < 4 else (shifted[j - 4] if j < 8 else far_high)
                acc_depth[j, :, lanes] += fold_rows(src[8 : 8 + DB] * xs)
        return carry

    lax.fori_loop(0, SEQ // DB, depth, 0)

    @pl.when(step == last)
    def _():
        dpoint_ref[...] = acc_point[...]
        dkern_ref[...] = acc_kern[...]
        ddepth_ref[...] = jnp.sum(acc_depth[...], 1)


def conv_back(dctx, kern, proj, ck, spread, inputs, d_first_in, w_depth, w_point, w_kern):
    rows = inputs.shape[0]
    block = lambda n: pl.BlockSpec((SEQ, n), lambda s: (s, 0))
    at = lambda c: pl.BlockSpec((SEQ, ATT), lambda s: (s, c))
    return pl.pallas_call(
        conv_back_kernel,
        grid=(rows // SEQ,),
        in_specs=[
            at(1), block(128), at(0), at(3), block(ATT), block(WIDTH), block(WIDTH), block(WIDTH),
            whole((KER, WIDTH)), whole((WIDTH, ATT)), whole((ATT, 128)),
        ],
        out_specs=[
            block(ATT), block(ATT), block(WIDTH), whole_out((WIDTH, ATT)), whole_out((ATT, 128)),
            whole_out((KER, WIDTH)),
        ],
        out_shape=[
            jax.ShapeDtypeStruct((rows, ATT), F32),
            jax.ShapeDtypeStruct((rows, ATT), BF),
            jax.ShapeDtypeStruct((rows, WIDTH), F32),
            jax.ShapeDtypeStruct((WIDTH, ATT), F32),
            jax.ShapeDtypeStruct((ATT, 128), F32),
            jax.ShapeDtypeStruct((KER, WIDTH), F32),
        ],
        scratch_shapes=[
            pltpu.VMEM((SEQ + 16, WIDTH), F32),
            pltpu.VMEM((SEQ + 16, ATT), F32),
            pltpu.VMEM((SEQ + 16, ATT), F32),
            pltpu.VMEM((SEQ + 16, 128), F32),
            pltpu.VMEM((SEQ + 16, WIDTH), F32),
            pltpu.VMEM((WIDTH, ATT), F32),
            pltpu.VMEM((ATT, 128), F32),
            pltpu.VMEM((KER, 8, WIDTH), F32),
        ],
        compiler_params=params(1),
        cost_estimate=cost(25e9, 30e6),
        name="conv_back",
    )(dctx, kern, proj, proj, ck, spread, inputs, d_first_in, w_depth, w_point, w_kern)


def attend_back_kernel(
    q_ref, k_ref, v_ref, p_ref, o_ref, inv_ref, datt_ref, dqc_ref, dq_ref, dk_ref, dv_ref
):
    scale = HEAD**-0.5
    v = v_ref[...]
    d_att = datt_ref[...].astype(F32) * inv_ref[...]
    o = o_ref[...].astype(F32)
    q_all = q_ref[...].astype(F32) * scale
    k_all = k_ref[...].astype(F32) * scale
    dq, dk_t, dv_t = dqc_ref[...], 0.0, 0.0
    for head in (0, 1):
        mine = own_lanes(SEQ, head)
        da = jnp.where(mine, d_att, 0.0)
        dot_rows = jnp.sum(da * o, -1, keepdims=True)
        p = p_ref[0, head]
        ds = mm_nt(da.astype(BF), v)
        ds = (p.astype(F32) * (ds - dot_rows)).astype(BF)
        dq = dq + mm(ds, jnp.where(mine, k_all, 0.0).astype(BF))
        dk_t = dk_t + mm(jnp.where(mine, q_all, 0.0).T.astype(BF), ds)
        dv_t = dv_t + mm(da.T.astype(BF), p)
    dq_ref[...] = dq.astype(BF)
    dk_ref[...] = dk_t.T.astype(BF)
    dv_ref[...] = dv_t.T.astype(BF)


def attend_back(proj, probs, att, inv, dctx, dq_conv):
    rows = proj.shape[0]
    pairs = HEADS // 2
    col = lambda base: pl.BlockSpec((SEQ, 128), lambda s, p: (s, base + p))
    return pl.pallas_call(
        attend_back_kernel,
        grid=(rows // SEQ, pairs),
        in_specs=[
            col(0), col(pairs), col(2 * pairs),
            pl.BlockSpec((1, 2, SEQ, SEQ), lambda s, p: (s, p, 0, 0)),
            col(0), col(0), col(0), col(0),
        ],
        out_specs=[col(0)] * 3,
        out_shape=[jax.ShapeDtypeStruct((rows, ATT), BF)] * 3,
        compiler_params=params(2),
        cost_estimate=cost(30e9, 40e6),
        name="attend_back",
    )(proj, proj, proj, probs, att, inv, dctx, dq_conv)


WB = 512


def weight_kernel(core_ref, inp_ref, dq_ref, dk_ref, dv_ref, dcv_ref, point_ref, extra_ref, *refs):
    grad_refs, acc = refs[:-1], refs[-1]
    step = pl.program_id(0)
    last = pl.num_programs(0) - 1
    inp = inp_ref[...]

    @pl.when(step == 0)
    def _():
        acc[...] = jnp.zeros_like(acc)

    for n, ref in enumerate((dq_ref, dk_ref, dv_ref, dcv_ref)):
        acc[:, n * ATT : (n + 1) * ATT] += mm_tn(inp, ref[...])

    @pl.when(step == last)
    def _():
        for c, grad in enumerate(grad_refs):

            def emit(i, carry):
                owner = i
                if len(grad_refs) == 2:
                    owner = (i // 8) * 16 + (core_ref[0] ^ c) * 8 + i % 8
                rows = pl.ds(pl.multiple_of(owner * 24, 8), 24)
                o = acc[rows, :]
                cols = [o[:, n * ATT : (n + 1) * ATT] for n in range(4)]
                grad[i] = jnp.concatenate(cols + [point_ref[rows, :], extra_ref[owner]], 0).astype(BF)
                return carry

            lax.fori_loop(0, grad.shape[0], emit, 0)


def weight_grad(inputs, dq, dk, dv, dcv, d_point, extra, core=None):
    rows = inputs.shape[0]
    block = lambda n: pl.BlockSpec((WB, n), lambda s: (s, 0))
    shapes = [(32, 128, LANES)] if core is None else [(16, 128, LANES)] * 2
    core = jnp.zeros((1,), jnp.int32) if core is None else core
    return pl.pallas_call(
        weight_kernel,
        grid=(rows // WB,),
        in_specs=[pl.BlockSpec(memory_space=pltpu.SMEM), block(WIDTH)]
        + [block(ATT)] * 4
        + [whole(d_point.shape), whole(extra.shape)],
        out_specs=[whole_out(s) for s in shapes],
        out_shape=[jax.ShapeDtypeStruct(s, BF) for s in shapes],
        scratch_shapes=[pltpu.VMEM((WIDTH, 4 * ATT), F32)],
        compiler_params=params(1),
        cost_estimate=cost(12e9, 12e6),
        name="weight_grad",
    )(core, inputs, dq, dk, dv, dcv, d_point, extra)


LC = 512
STEPS = SEQ // LC


def leave_kernel(
    dq_ref, dk_ref, dv_ref, dcv_ref, rest_ref, mask_ref, to_ref, w_in_ref, out_ref, moved, kept
):
    step = pl.program_id(1)
    rows = pl.ds(pl.multiple_of((step % STEPS) * LC, LC), LC)

    @pl.when(step < STEPS)
    def _():
        d_proj = jnp.concatenate([dq_ref[...], dk_ref[...], dv_ref[...], dcv_ref[...]], 1)
        total = mm_nt(d_proj, w_in_ref[...]) + rest_ref[...]
        moved[rows, :] = total.astype(BF)
        kept[rows, :] = jnp.where(mask_ref[...] == 1, 0.0, total)

    @pl.when(step >= STEPS)
    def _():
        target = lax.broadcasted_iota(jnp.int32, (LC, SEQ), 0) + (step - STEPS) * LC
        hot = (target == to_ref[0]).astype(F32).astype(BF)
        out_ref[...] = kept[rows, :] + mm(hot, moved[...])


def leave(dq, dk, dv, dcv, d_rest, mask_col, to_row, w_in):
    rows = dq.shape[0]
    block = lambda n: pl.BlockSpec((LC, n), lambda s, i: (s * STEPS + jnp.minimum(i, STEPS - 1), 0))
    return pl.pallas_call(
        leave_kernel,
        grid=(rows // SEQ, 2 * STEPS),
        in_specs=[block(ATT)] * 4
        + [block(WIDTH), block(1), pl.BlockSpec((1, 1, SEQ), lambda s, i: (s, 0, 0)), whole((WIDTH, 4 * ATT))],
        out_specs=pl.BlockSpec((LC, WIDTH), lambda s, i: (s * STEPS + jnp.maximum(i - STEPS, 0), 0)),
        out_shape=jax.ShapeDtypeStruct((rows, WIDTH), F32),
        scratch_shapes=[pltpu.VMEM((SEQ, WIDTH), BF), pltpu.VMEM((SEQ, WIDTH), F32)],
        compiler_params=params(2),
        cost_estimate=cost(15e9, 30e6),
        name="leave",
    )(dq, dk, dv, dcv, d_rest, mask_col, to_row, w_in)


def pack_taps(kernel_full):
    by_tap = kernel_full.reshape(ATT, HEADS, KER).transpose(0, 2, 1)
    return jnp.pad(by_tap, ((0, 0), (0, 16 - KER), (0, 8 - HEADS))).reshape(ATT, 128)


def unpack_taps(packed):
    return packed.reshape(ATT, 16, 8)[:, :KER, :HEADS].transpose(0, 2, 1).reshape(ATT, HEADS * KER)


def per_device(
    tokens,
    masked,
    replace_ids,
    in_weight,
    depth_weight,
    point_weight,
    kernel_weight,
    out_weight,
    gain_one,
    shift_one,
    ffn_in,
    feedforward_output,
    gain_two,
    shift_two,
    cotangent,
):
    rows = tokens.shape[0]
    seqs = rows // SEQ
    dp, fsdp = lax.axis_size("dp"), lax.axis_size("fsdp")
    devices = dp * fsdp
    near = dp == NEAR["dp"] and fsdp == NEAR["fsdp"]
    own, hid = in_weight.shape[0], ffn_in.shape[2]
    n_depth, n_kern, n_vec = KER * own, kernel_weight.size, 4 * own
    hit = masked == 1
    here = jnp.arange(rows, dtype=jnp.int32) % SEQ
    pick = jnp.where(hit, replace_ids, here)[:, None]
    to_row = jnp.where(hit, replace_ids, -1).reshape(seqs, 1, SEQ)
    scale = 1.0 / math.sqrt(rows * devices)

    vec_own = jnp.stack([gain_one, shift_one, gain_two, shift_two])
    small_own = as_rows(
        jnp.concatenate([depth_weight.reshape(-1), kernel_weight.reshape(-1), vec_own.reshape(-1)])
    )
    head_own = jnp.concatenate([in_weight.reshape(own, 4, ATT).transpose(1, 0, 2), point_weight[None]])
    mid_own = jnp.concatenate(
        [
            out_weight.reshape(own, 2, ATT).transpose(1, 0, 2).reshape(-1, LANES),
            ffn_in.transpose(0, 2, 1).reshape(-1, LANES),
            feedforward_output.reshape(-1, LANES),
        ]
    )
    if near:
        me = place().astype(jnp.int32).reshape(1)
        pair, core = me // 2, me // CORE_BIT % 2
        slab, pick = tie(pair_slab(head_own, small_own), pick)
        slabs = [slab] + [hop(slab, k * Z_BIT) for k in (1, 2, 3)]
        inputs, slabs = tie(pick_rows(pick, tokens), slabs)
        slabs, mid_own = tie(slabs, mid_own)
        mid = lax.all_gather(mid_own, AXES, axis=0)
        slabs = slabs + [hop(slab, X_BIT) for slab in slabs]
        slabs = slabs + [hop(slab, CORE_BIT) for slab in slabs]
        small_all = small_rows(slabs, pair)
    else:
        small_all = lax.all_gather(small_own, AXES, axis=0).reshape(devices, -1)
        w_all = lax.all_gather(head_own, AXES, axis=1, tiled=True).reshape(5, 16, 48, LANES)
        slabs = [w_all[:, bits].reshape(-1, LANES) for bits in SLAB_BITS]
        mid = lax.all_gather(mid_own, AXES, axis=0)
        w_out = mid[:, : 2 * own].reshape(devices, 2, own, ATT).transpose(1, 0, 2, 3)
        w_out = w_out.reshape(2, BLOCKS, 24, ATT).transpose(1, 0, 2, 3).reshape(BLOCKS, 48, ATT)
        w_ffn = mid[:, 2 * own :].reshape(devices, 4, hid, ATT).transpose(1, 0, 2, 3)
        w_ffn = w_ffn.reshape(4, BLOCKS, 48, ATT).transpose(1, 0, 2, 3).reshape(BLOCKS, 192, ATT)
        mid = jnp.concatenate([w_out, w_ffn], 1)
        pair, core = jnp.zeros((1,), jnp.int32), None
        inputs = pick_rows(pick, tokens)
    w_depth = small_all[:, :n_depth].reshape(devices, KER, own).transpose(1, 0, 2).reshape(KER, WIDTH)
    w_depth = w_depth.astype(F32)
    w_kern = pack_taps(small_all[:fsdp, n_depth : n_depth + n_kern].reshape(ATT, HEADS * KER))
    vecs = small_all[:, n_depth + n_kern :][:, :n_vec].reshape(devices, 4, own)
    vecs = vecs.transpose(1, 0, 2).reshape(4, WIDTH).astype(F32)

    proj, spread, ck, kern, conv, w_in, w_point = enter(inputs, pair, w_depth, w_kern, slabs)
    probs, att, inv = attend(proj)
    out, dctx, d_first_in, d_vecs, mid_grad = middle(att, conv, inputs, cotangent, mid, vecs)
    if near:
        mid_sum = lax.psum_scatter(mid_grad, AXES, scatter_dimension=0, tiled=True)[0]
    dq_conv, dcv, d_rest, d_point, d_kern, d_depth = conv_back(
        dctx, kern, proj, ck, spread, inputs, d_first_in, w_depth, w_point, w_kern
    )
    by_owner = lambda g: g.reshape(-1, devices, own).transpose(1, 0, 2).reshape(devices, -1)
    kern_by = jnp.tile(unpack_taps(d_kern).reshape(fsdp, -1), (dp, 1))
    small_grad = jnp.concatenate([by_owner(d_depth), kern_by, by_owner(d_vecs)], 1)
    small_grad = jnp.pad(small_grad, ((0, 0), (0, -small_grad.shape[1] % LANES)))
    small_grad = small_grad.reshape(devices, -1, LANES)
    dq, dk, dv = attend_back(proj, probs, att, inv, dctx, dq_conv)
    mask_col = masked[:, None]
    if near:
        mine, other = weight_grad(inputs, dq, dk, dv, dcv, d_point, small_grad, core)
        parts = fold_xy(me, mine, hop(other, CORE_BIT))
        parts = [parts[0]] + [hop(part, bit) for part, bit in zip(parts[1:], (Y_BIT, X_BIT, X_BIT + Y_BIT))]
        parts[0], dq = tie(parts[0], dq)
        d_tokens = leave(dq, dk, dv, dcv, d_rest, mask_col, to_row, w_in)
        d_tokens, parts = tie(d_tokens, parts)
        parts = fold_z(me, parts)
        parts = [parts[0]] + [hop(parts[k], k * Z_BIT) for k in (1, 2, 3)]
        parts[0], mid_sum = tie(parts[0], mid_sum)
        d_out, d_up, d_down = finish_mid(scale, mid_sum)
        d_in, d_point, small_sum = finish(scale, parts)
        small_sum = small_sum.reshape(-1)
    else:
        (grads,) = weight_grad(inputs, dq, dk, dv, dcv, d_point, jnp.zeros((32, 8, LANES), F32))
        d_in = grads[:, :96].reshape(32, 4, 24, ATT).transpose(0, 2, 1, 3).reshape(devices, -1, LANES)
        d_point = grads[:, 96:120].reshape(devices, -1, LANES)
        w_out = mid_grad[:, :48].reshape(BLOCKS, 2, 24, ATT).transpose(0, 2, 1, 3).reshape(devices, -1, LANES)
        w_ffn = mid_grad[:, 48:].reshape(BLOCKS, 4, 48, ATT).transpose(1, 0, 2, 3)
        w_ffn = w_ffn.reshape(4, devices, hid, ATT).transpose(1, 0, 2, 3).reshape(devices, -1, LANES)
        packed = jnp.concatenate([w_out, w_ffn, d_in, d_point, small_grad.astype(BF)], 1)
        total = lax.psum_scatter(packed, AXES, scatter_dimension=0, tiled=True)[0].astype(F32) * scale
        cuts = [2 * own, 2 * own + 2 * hid, 2 * own + 4 * hid, 6 * own + 4 * hid, 7 * own + 4 * hid]
        d_out, d_up, d_down, d_in, d_point, small_sum = jnp.split(total, cuts)
        d_out, d_in, small_sum = d_out.reshape(own, WIDTH), d_in.reshape(own, 4 * ATT), small_sum.reshape(-1)
        d_up, d_down = d_up.reshape(2, hid, ATT).transpose(0, 2, 1), d_down.reshape(2, hid, ATT)
        d_tokens = leave(dq, dk, dv, dcv, d_rest, mask_col, to_row, w_in)
    kern_sum = small_sum[n_depth : n_depth + n_kern].reshape(kernel_weight.shape)
    vec_sum = small_sum[n_depth + n_kern :][:n_vec].reshape(4, own)
    return (
        out,
        d_tokens,
        d_in,
        small_sum[:n_depth].reshape(KER, own),
        d_point,
        kern_sum,
        d_out,
        vec_sum[0],
        vec_sum[1],
        d_up,
        d_down,
        vec_sum[2],
        vec_sum[3],
    )


def solution(mesh):
    return jax.shard_map(
        per_device,
        mesh=mesh,
        in_specs=(
            P(("dp", "fsdp"), None),
            P(("dp", "fsdp")),
            P(("dp", "fsdp")),
            P(("dp", "fsdp"), None),
            P(None, ("dp", "fsdp")),
            P(("dp", "fsdp"), None),
            P("fsdp", None),
            P(("dp", "fsdp"), None),
            P(("dp", "fsdp")),
            P(("dp", "fsdp")),
            P(None, None, ("dp", "fsdp")),
            P(None, ("dp", "fsdp"), None),
            P(("dp", "fsdp")),
            P(("dp", "fsdp")),
            P(("dp", "fsdp"), None),
        ),
        out_specs=(
            P(("dp", "fsdp"), None),
            P(("dp", "fsdp"), None),
            P(("dp", "fsdp"), None),
            P(None, ("dp", "fsdp")),
            P(("dp", "fsdp"), None),
            P("fsdp", None),
            P(("dp", "fsdp"), None),
            P(("dp", "fsdp")),
            P(("dp", "fsdp")),
            P(None, None, ("dp", "fsdp")),
            P(None, ("dp", "fsdp"), None),
            P(("dp", "fsdp")),
            P(("dp", "fsdp")),
        ),
        check_vma=False,
    )
```

```python
from functools import partial
import math

import jax
import jax.numpy as jnp
from jax import lax
from jax.experimental import pallas as pl
from jax.experimental.pallas import tpu as pltpu
from jax.sharding import PartitionSpec as P

BF = jnp.bfloat16
F32 = jnp.float32
HEADS = 6
HEAD = 64
SEQ = 1024
KER = 9
ATT = HEADS * HEAD
WIDTH = 768
VMEM_MAX = 60 * 1024 * 1024


def mm(a, b):
    return jnp.dot(a, b, preferred_element_type=F32)


def mm_nt(a, b):
    return lax.dot_general(a, b, (((1,), (1,)), ((), ())), preferred_element_type=F32)


def mm_tn(a, b):
    return lax.dot_general(a, b, (((0,), (0,)), ((), ())), preferred_element_type=F32)


def params(count):
    return pltpu.CompilerParams(
        dimension_semantics=("arbitrary",) * count, vmem_limit_bytes=VMEM_MAX
    )


def cost(flops, moved):
    return pl.CostEstimate(flops=int(flops), bytes_accessed=int(moved), transcendentals=0)


def whole(shape):
    zeros = (0,) * len(shape)
    return pl.BlockSpec(shape, lambda *_: zeros, pipeline_mode=pl.Buffered(1))


def whole_out(shape):
    zeros = (0,) * len(shape)
    return pl.BlockSpec(shape, lambda *_: zeros)


AXES = ("dp", "fsdp")
LANES = 384
NEAR = {"dp": 4, "fsdp": 8}
X_BIT, CORE_BIT, Z_BIT, Y_BIT = 16, 8, 2, 1


def as_rows(x):
    flat = x.reshape(-1)
    return jnp.pad(flat, (0, -flat.size % LANES)).reshape(-1, LANES)


def place():
    return lax.axis_index("dp") * NEAR["fsdp"] + lax.axis_index("fsdp")


def hop(x, mask):
    return lax.ppermute(x, AXES, [(i, i ^ mask) for i in range(32)])


def tie(first, second):
    return lax.optimization_barrier((first, second))


def fold_xy_kernel(me_ref, mine_ref, other_ref, *outs):
    x, y = me_ref[0] // X_BIT, me_ref[0] % 2
    for k, out in enumerate(outs):
        at = (x ^ (k // 2), 0, y ^ (k % 2))
        out[0] = (mine_ref[at].astype(F32) + other_ref[at].astype(F32)).astype(BF)


def fold_xy(me, mine, other):
    rows = mine.shape[-2]
    views = [a.reshape(2, 4, 2, rows, LANES) for a in (mine, other)]
    return pl.pallas_call(
        fold_xy_kernel,
        grid=(4,),
        in_specs=[pl.BlockSpec(memory_space=pltpu.SMEM)]
        + [pl.BlockSpec((2, 1, 2, rows, LANES), lambda z: (0, z, 0, 0, 0))] * 2,
        out_specs=[pl.BlockSpec((1, rows, LANES), lambda z: (z, 0, 0))] * 4,
        out_shape=[jax.ShapeDtypeStruct((4, rows, LANES), BF)] * 4,
        compiler_params=params(1),
        cost_estimate=cost(0, 6 * mine.size),
        name="fold_xy",
    )(me, *views)


def fold_z_kernel(me_ref, *refs):
    z = (me_ref[0] // Z_BIT) % 4
    for k, out in enumerate(refs[4:]):
        total = refs[0][z ^ k].astype(F32)
        for ref in refs[1:4]:
            total = total + ref[z ^ k].astype(F32)
        out[...] = total.astype(BF)


def fold_z(me, arrays):
    rows = arrays[0].shape[-2]
    return pl.pallas_call(
        fold_z_kernel,
        in_specs=[pl.BlockSpec(memory_space=pltpu.SMEM)] + [pl.BlockSpec(memory_space=pltpu.VMEM)] * 4,
        out_specs=[pl.BlockSpec(memory_space=pltpu.VMEM)] * 4,
        out_shape=[jax.ShapeDtypeStruct((rows, LANES), BF)] * 4,
        compiler_params=pltpu.CompilerParams(vmem_limit_bytes=16 * 1024 * 1024),
        cost_estimate=cost(0, 10 * arrays[0].size),
        name="fold_z",
    )(me, *arrays)


def finish_kernel(scale, a_ref, b_ref, c_ref, d_ref, in_ref, point_ref, small_ref):
    total = sum(ref[...].astype(F32) for ref in (a_ref, b_ref, c_ref, d_ref)) * scale
    for n in range(4):
        in_ref[:, n * ATT : (n + 1) * ATT] = total[24 * n : 24 * n + 24]
    point_ref[...] = total[96:120]
    small_ref[...] = total[120:128]


def finish(scale, arrays):
    vmem = pl.BlockSpec(memory_space=pltpu.VMEM)
    return pl.pallas_call(
        partial(finish_kernel, scale),
        in_specs=[vmem] * 4,
        out_specs=[vmem] * 3,
        out_shape=[
            jax.ShapeDtypeStruct((24, 4 * ATT), F32),
            jax.ShapeDtypeStruct((24, ATT), F32),
            jax.ShapeDtypeStruct((8, LANES), F32),
        ],
        name="finish",
    )(*arrays)


def finish_mid_kernel(scale, sum_ref, out_ref, up_ref, down_ref):
    total = sum_ref[...].astype(F32) * scale
    out_ref[:, :ATT] = total[:24]
    out_ref[:, ATT:] = total[24:48]
    for g in (0, 1):
        up_ref[g] = total[48 + 48 * g : 96 + 48 * g]
        down_ref[g] = total[144 + 48 * g : 192 + 48 * g]


def finish_mid(scale, packed):
    vmem = pl.BlockSpec(memory_space=pltpu.VMEM)
    return pl.pallas_call(
        partial(finish_mid_kernel, scale),
        in_specs=[vmem],
        out_specs=[vmem] * 3,
        out_shape=[
            jax.ShapeDtypeStruct((24, WIDTH), F32),
            jax.ShapeDtypeStruct((2, 48, ATT), F32),
            jax.ShapeDtypeStruct((2, 48, ATT), F32),
        ],
        name="finish_mid",
    )(packed)


SLAB_BITS = [((s // 4) % 2 * X_BIT + (s // 8) * CORE_BIT + s % 4 * Z_BIT) // 2 for s in range(16)]


def pair_slab(own, small):
    packed = jnp.concatenate([own.reshape(-1, LANES), small])
    other = hop(packed, Y_BIT)
    even = place() % 2 == 0
    first, second = jnp.where(even, packed, other), jnp.where(even, other, packed)
    both = [x[:120].reshape(5, 24, LANES) for x in (first, second)]
    return jnp.concatenate([jnp.concatenate(both, 1).reshape(-1, LANES), first[120:], second[120:]])


def small_rows(slabs, pair):
    spot = jnp.array([SLAB_BITS.index(b) for b in range(16)], jnp.int32)
    order = jnp.take(spot, jnp.arange(16, dtype=jnp.int32) ^ pair)
    return jnp.take(jnp.stack([slab[240:] for slab in slabs]), order, axis=0).reshape(32, -1)


def lane_groups(x, combine):
    for step in (64, 32, 16, 8):
        x = combine(x, pltpu.roll(x, step, 1))
    return x


def tap_spread(block):
    rows = lax.broadcasted_iota(jnp.int32, (128, KER * 128), 0)
    cols = lax.broadcasted_iota(jnp.int32, (128, KER * 128), 1)
    want = (cols // 128) * 8 + block * 2 + (cols % 128) // HEAD
    return (rows == want).astype(F32).astype(BF)


EC = 1024
FB = 512
BB = 1024
DB = 512


def pick_kernel(pick_ref, tok_ref, inp_ref):
    cols = lax.broadcasted_iota(jnp.int32, (SEQ, SEQ), 1)
    hot = (cols == pick_ref[...]).astype(F32).astype(BF)
    inp_ref[...] = mm(hot, tok_ref[...]).astype(BF)


def pick_rows(pick, tokens):
    block = lambda n: pl.BlockSpec((SEQ, n), lambda s: (s, 0))
    return pl.pallas_call(
        pick_kernel,
        grid=(tokens.shape[0] // SEQ,),
        in_specs=[block(1), block(WIDTH)],
        out_specs=block(WIDTH),
        out_shape=jax.ShapeDtypeStruct(tokens.shape, BF),
        compiler_params=params(1),
        cost_estimate=cost(6e9, 6e6),
        name="pick",
    )(pick, tokens)


def enter_kernel(
    inp_ref, w_in_ref, w_depth_ref, w_point_ref, w_kern_ref,
    proj_ref, spread_ref, ck_ref, kern_ref, conv_ref,
    x_pad, cv_pad,
):
    x_pad[0:8, :] = jnp.zeros((8, WIDTH), F32)
    x_pad[SEQ + 8 : SEQ + 16, :] = jnp.zeros((8, WIDTH), F32)
    cv_pad[0:8, :] = jnp.zeros((8, ATT), F32)
    cv_pad[SEQ + 8 : SEQ + 16, :] = jnp.zeros((8, ATT), F32)

    def load(i, carry):
        r = pl.multiple_of(i * EC, EC)
        low = inp_ref[pl.ds(r, EC), :]
        x_pad[pl.ds(r + 8, EC), :] = low.astype(F32)
        proj = mm(low, w_in_ref[...])
        proj_low = proj.astype(BF)
        proj_ref[pl.ds(r, EC), :] = proj_low
        cv_pad[pl.ds(r + 8, EC), :] = proj_low[:, 3 * ATT :].astype(F32)
        return carry

    lax.fori_loop(0, SEQ // EC, load, 0)

    def conv(i, carry):
        r = pl.multiple_of(i * EC, EC)
        for b in range(WIDTH // 128):
            lanes = slice(b * 128, (b + 1) * 128)
            xs = x_pad[pl.ds(r, (EC + 16)), lanes]
            shifted = [xs] + [pltpu.roll(xs, (EC + 16) - s, 0) for s in (1, 2, 3)]
            tap = lambda j: w_depth_ref[j : j + 1, lanes]
            low_part = sum(tap(s) * shifted[s] for s in range(4))
            mid_part = sum(tap(4 + s) * shifted[s] for s in range(4))
            high_part = tap(8) * xs
            low_part = pltpu.roll(low_part, (EC + 16) - 4, 0)
            high_part = pltpu.roll(high_part, (EC + 16) - 4, 0)
            total = low_part[0:EC] + mid_part[8 : 8 + EC] + high_part[8 : 8 + EC]
            spread_ref[pl.ds(r, EC), lanes] = total.astype(BF)
        ck = mm(spread_ref[pl.ds(r, EC), :], w_point_ref[...]).astype(BF)
        ck_ref[pl.ds(r, EC), :] = ck
        q = proj_ref[pl.ds(r, EC), 0:ATT].astype(F32)
        mixed = (ck.astype(F32) * q).astype(BF)
        logits = mm(mixed, w_kern_ref[...])
        lane = lax.broadcasted_iota(jnp.int32, (EC, 128), 1)
        logits = jnp.where(lane < KER * 8, logits, -1e30)
        top = lane_groups(logits, jnp.maximum)
        e = jnp.exp(logits - top)
        kern = e / lane_groups(e, jnp.add)
        kern_ref[pl.ds(r, EC), :] = kern
        kern_low = kern.astype(BF)
        for b in range(ATT // 128):
            lanes = slice(b * 128, (b + 1) * 128)
            wide = mm(kern_low, tap_spread(b))
            cs = cv_pad[pl.ds(r, (EC + 16)), lanes]
            total = jnp.zeros((EC, 128), F32)
            for j in range(KER):
                moved = cs if j == 4 else pltpu.roll(cs, ((EC + 16) - (j - 4)) % (EC + 16), 0)
                total = total + wide[:, j * 128 : (j + 1) * 128] * moved[8 : 8 + EC]
            conv_ref[pl.ds(r, EC), lanes] = total.astype(BF)
        return carry

    lax.fori_loop(0, SEQ // EC, conv, 0)


def enter_slabs_kernel(pair_ref, inp_ref, w_depth_ref, w_kern_ref, *refs):
    slabs, outs = refs[:16], refs[16:]
    results, w_in_ref, w_point_ref, scratch, sems = outs[:5], outs[5], outs[6], outs[7:9], outs[9]

    @pl.when(pl.program_id(0) == 0)
    def _():
        copies = []
        for s, slab in enumerate(slabs):
            spot = pl.ds(pl.multiple_of((pair_ref[0] ^ SLAB_BITS[s]) * 48, 16), 48)
            for b in range(5):
                to = w_in_ref.at[spot, b * ATT : (b + 1) * ATT] if b < 4 else w_point_ref.at[spot, :]
                copies.append(pltpu.make_async_copy(slab.at[b * 48 : (b + 1) * 48, :], to, sems.at[s, b]))
        for copy in copies:
            copy.start()
        for copy in copies:
            copy.wait()

    enter_kernel(inp_ref, w_in_ref, w_depth_ref, w_point_ref, w_kern_ref, *results, *scratch)


def enter(inputs, pair, w_depth, w_kern, slabs):
    rows = inputs.shape[0]
    block = lambda n: pl.BlockSpec((SEQ, n), lambda s: (s, 0))
    widths = ((4 * ATT, BF), (WIDTH, BF), (ATT, BF), (128, F32), (ATT, BF))
    return pl.pallas_call(
        enter_slabs_kernel,
        grid=(rows // SEQ,),
        in_specs=[
            pl.BlockSpec(memory_space=pltpu.SMEM), block(WIDTH), whole((KER, WIDTH)), whole((ATT, 128)),
        ]
        + [pl.BlockSpec(memory_space=pl.ANY)] * 16,
        out_specs=[block(n) for n, _ in widths] + [whole_out((WIDTH, 4 * ATT)), whole_out((WIDTH, ATT))],
        out_shape=[jax.ShapeDtypeStruct((rows, n), t) for n, t in widths]
        + [jax.ShapeDtypeStruct((WIDTH, 4 * ATT), BF), jax.ShapeDtypeStruct((WIDTH, ATT), BF)],
        scratch_shapes=[
            pltpu.VMEM((SEQ + 16, WIDTH), F32),
            pltpu.VMEM((SEQ + 16, ATT), F32),
            pltpu.SemaphoreType.DMA((16, 5)),
        ],
        compiler_params=params(1),
        cost_estimate=cost(20e9, 20e6),
        name="enter",
    )(pair, inputs, w_depth, w_kern, *slabs)


def own_lanes(rows, head):
    lane = lax.broadcasted_iota(jnp.int32, (rows, 128), 1)
    return (lane // HEAD) == head


AC = 512


def attend_kernel(q_ref, k_ref, v_ref, p_ref, o_ref, inv_ref):
    k = k_ref[...]
    v_all = v_ref[...].astype(F32)
    vs = [jnp.where(own_lanes(SEQ, head), v_all, 1.0).astype(BF) for head in (0, 1)]
    first = own_lanes(AC, 0)

    def part(i, carry):
        rows = pl.ds(pl.multiple_of(i * AC, AC), AC)
        q_all = q_ref[rows, :].astype(F32) * (HEAD**-0.5)
        outs = []
        for head in (0, 1):
            q = jnp.where(first if head == 0 else ~first, q_all, 0.0).astype(BF)
            s = mm_nt(q, k)
            p = jnp.exp(s - jnp.max(s, -1, keepdims=True)).astype(BF)
            p_ref[0, head, rows, :] = p
            outs.append(mm(p, vs[head]))
        inv = 1.0 / pltpu.roll(jnp.where(first, outs[1], outs[0]), HEAD, 1)
        o_ref[rows, :] = (jnp.where(first, outs[0], outs[1]) * inv).astype(BF)
        inv_ref[rows, :] = inv
        return carry

    lax.fori_loop(0, SEQ // AC, part, 0, unroll=2)


def attend(proj):
    rows = proj.shape[0]
    pairs = HEADS // 2
    col = lambda base: pl.BlockSpec((SEQ, 128), lambda s, p: (s, base + p))
    return pl.pallas_call(
        attend_kernel,
        grid=(rows // SEQ, pairs),
        in_specs=[col(0), col(pairs), col(2 * pairs)],
        out_specs=[pl.BlockSpec((1, 2, SEQ, SEQ), lambda s, p: (s, p, 0, 0)), col(0), col(0)],
        out_shape=[
            jax.ShapeDtypeStruct((rows // SEQ, HEADS, SEQ, SEQ), BF),
            jax.ShapeDtypeStruct((rows, ATT), BF),
            jax.ShapeDtypeStruct((rows, ATT), F32),
        ],
        compiler_params=params(2),
        cost_estimate=cost(25e9, 35e6),
        name="attend",
    )(proj, proj, proj)


ERF_P = 0.3275911 / math.sqrt(2.0)
ERF_A = (0.254829592, -0.284496736, 1.421413741, -1.453152027, 1.061405429)
PHI = 1.0 / math.sqrt(2.0 * math.pi)


def gelu_both(u):
    t = 1.0 / (1.0 + ERF_P * jnp.abs(u))
    poly = 0.5 * ERF_A[4]
    for a in ERF_A[3::-1]:
        poly = poly * t + 0.5 * a
    e = jnp.exp2((-0.5 * math.log2(math.e)) * (u * u))
    tail = t * poly * e
    cdf = jnp.where(u > 0, 1.0 - tail, tail)
    return u * cdf, cdf + (PHI * u) * e


def norm_parts(z):
    mean = jnp.mean(z, -1, keepdims=True)
    centred = z - mean
    var = jnp.mean(centred * centred, -1, keepdims=True)
    r = lax.rsqrt(var + 1e-12)
    return centred * r, r


def norm_back(c, xh, r, gain):
    gc = c * gain
    return r * (gc - jnp.mean(gc, -1, keepdims=True) - xh * jnp.mean(gc * xh, -1, keepdims=True))


def fold_rows(x):
    return jnp.sum(x.reshape(-1, 8, x.shape[-1]), 0)


MID = 256
FF = 1536
FC = 768
GROUP = 48
BLOCKS = FF // GROUP


def middle_kernel(
    att_ref, conv_ref, inp_ref, cot_ref, mid_ref, vec_ref,
    out_ref, dctx_ref, dfirst_ref, dvec_ref, packed_ref,
    acc_out, acc_up, acc_down, acc_vec, act_ref, slope_ref, flip_ref,
    w_out_ref, w_rows, w_up_blocks, w_down_blocks, sems,
):
    step = pl.program_id(0)
    last = pl.num_programs(0) - 1

    @pl.when(step == 0)
    def _():
        targets = [w_rows] + [w.at[g] for w in (w_up_blocks, w_down_blocks) for g in (0, 1)]
        copies = [
            pltpu.make_async_copy(mid_ref.at[:, n * GROUP : (n + 1) * GROUP, :], to, sems.at[n])
            for n, to in enumerate(targets)
        ]
        for copy in copies:
            copy.start()
        acc_up[...] = jnp.zeros_like(acc_up)
        acc_down[...] = jnp.zeros_like(acc_down)
        acc_vec[...] = jnp.zeros_like(acc_vec)
        copies[0].wait()
        half = GROUP // 2

        def unfold(i, carry):
            both = w_rows[i].astype(F32)
            rows = pl.ds(pl.multiple_of(i * half, 8), half)
            acc_out[rows, :] = jnp.concatenate([both[:half], both[half:]], 1)
            return carry

        lax.fori_loop(0, BLOCKS, unfold, 0)
        w_out_ref[...] = acc_out[...].astype(BF)
        acc_out[...] = jnp.zeros_like(acc_out)
        for copy in copies[1:]:
            copy.wait()

    def w_up(g, f):
        return w_up_blocks[g, f * FC // GROUP : (f + 1) * FC // GROUP].reshape(FC, ATT)

    def w_down(g, f):
        return w_down_blocks[g, f * FC // GROUP : (f + 1) * FC // GROUP].reshape(FC, ATT)

    ctx = jnp.concatenate([att_ref[...], conv_ref[...]], -1)
    g_one, s_one = vec_ref[0:1, :], vec_ref[1:2, :]
    g_two, s_two = vec_ref[2:3, :], vec_ref[3:4, :]
    first_in = mm(ctx, w_out_ref[...]) + inp_ref[...].astype(F32)
    xh_one, r_one = norm_parts(first_in)
    first = xh_one * g_one + s_one
    first_low = first.astype(BF)
    outs = []
    for g in (0, 1):
        cols = slice(g * ATT, (g + 1) * ATT)
        total = None
        for f in range(FF // FC):
            hid = slice(f * FC, (f + 1) * FC)
            inner = mm_nt(first_low[:, cols], w_up(g, f))
            act, slope = gelu_both(inner)
            act = act.astype(BF)
            act_ref[g, :, hid] = act
            slope_ref[g, :, hid] = slope.astype(slope_ref.dtype)
            part = mm(act, w_down(g, f))
            total = part if total is None else total + part
        outs.append(total)
    xh_two, r_two = norm_parts(jnp.concatenate(outs, -1) + first)
    out_ref[...] = (xh_two * g_two + s_two).astype(BF)
    c = cot_ref[...].astype(F32)
    acc_vec[2] += fold_rows(c * xh_two)
    acc_vec[3] += fold_rows(c)
    d_second = norm_back(c, xh_two, r_two, g_two)
    d_outer = d_second.astype(BF)
    d_outer_t = d_second.T.astype(BF)
    first_t = first.T.astype(BF)
    backs = []
    for g in (0, 1):
        cols = slice(g * ATT, (g + 1) * ATT)
        total = None
        for f in range(FF // FC):
            hid = slice(f * FC, (f + 1) * FC)
            d_act = mm_nt(d_outer[:, cols], w_down(g, f))
            d_inner = (d_act * slope_ref[g, :, hid].astype(F32)).astype(BF)
            acc_down[g, :, hid] += mm(d_outer_t[cols, :], act_ref[g, :, hid])
            acc_up[g, :, hid] += mm(first_t[cols, :], d_inner)
            part = mm(d_inner, w_up(g, f))
            total = part if total is None else total + part
        backs.append(total)
    d_first = jnp.concatenate(backs, -1) + d_second
    acc_vec[0] += fold_rows(d_first * xh_one)
    acc_vec[1] += fold_rows(d_first)
    d_first_in = norm_back(d_first, xh_one, r_one, g_one)
    dfirst_ref[...] = d_first_in
    d_dense = d_first_in.astype(BF)
    acc_out[...] += mm_tn(ctx, d_dense)
    dctx_ref[...] = mm_nt(d_dense, w_out_ref[...]).astype(BF)

    @pl.when(step == last)
    def _():
        dvec_ref[...] = jnp.sum(acc_vec[...], 1)
        for g in (0, 1):
            flip_ref[0, g] = acc_up[g].T.astype(BF)
            flip_ref[1, g] = acc_down[g].T.astype(BF)

        def emit(i, carry):
            o = acc_out[pl.ds(pl.multiple_of(i * 24, 8), 24), :]
            packed_ref[i, 0:48, :] = jnp.concatenate([o[:, :ATT], o[:, ATT:]], 0).astype(BF)
            hidden = pl.ds(pl.multiple_of(i * 48, 16), 48)
            for n in range(4):
                packed_ref[i, 48 * n + 48 : 48 * n + 96, :] = flip_ref[n // 2, n % 2, hidden, :]
            return carry

        lax.fori_loop(0, BLOCKS, emit, 0)


def middle(att, conv, inputs, cot, mid, vecs):
    rows = att.shape[0]
    block = lambda n: pl.BlockSpec((MID, n), lambda s: (s, 0))
    packed = (BLOCKS, 5 * GROUP, LANES)
    return pl.pallas_call(
        middle_kernel,
        grid=(rows // MID,),
        in_specs=[
            block(ATT), block(ATT), block(WIDTH), block(WIDTH),
            pl.BlockSpec(memory_space=pl.ANY), whole((4, WIDTH)),
        ],
        out_specs=[block(WIDTH), block(WIDTH), block(WIDTH), whole_out((4, WIDTH)), whole_out(packed)],
        out_shape=[
            jax.ShapeDtypeStruct((rows, WIDTH), BF),
            jax.ShapeDtypeStruct((rows, WIDTH), BF),
            jax.ShapeDtypeStruct((rows, WIDTH), F32),
            jax.ShapeDtypeStruct((4, WIDTH), F32),
            jax.ShapeDtypeStruct(packed, BF),
        ],
        scratch_shapes=[
            pltpu.VMEM((WIDTH, WIDTH), F32),
            pltpu.VMEM((2, ATT, FF), F32),
            pltpu.VMEM((2, ATT, FF), F32),
            pltpu.VMEM((4, 8, WIDTH), F32),
            pltpu.VMEM((2, MID, FF), BF),
            pltpu.VMEM((2, MID, FF), F32),
            pltpu.VMEM((2, 2, FF, ATT), BF),
            pltpu.VMEM((WIDTH, WIDTH), BF),
            pltpu.VMEM((BLOCKS, GROUP, LANES), BF),
            pltpu.VMEM((2, BLOCKS, GROUP, ATT), BF),
            pltpu.VMEM((2, BLOCKS, GROUP, ATT), BF),
            pltpu.SemaphoreType.DMA((5,)),
        ],
        compiler_params=params(1),
        cost_estimate=cost(60e9, 40e6),
        name="middle",
    )(att, conv, inputs, cot, mid, vecs)


def conv_back_kernel(
    dconv_ref, kern_ref, q_ref, cv_ref, ck_ref, spread_ref, inp_ref, first_ref, w_depth_ref, w_point_ref, w_kern_ref,
    dq_ref, dcv_ref, din_ref, dpoint_ref, dkern_ref, ddepth_ref,
    x_pad, cv_pad, dc_pad, kl_pad, ds_pad, acc_point, acc_kern, acc_depth,
):
    step = pl.program_id(0)
    last = pl.num_programs(0) - 1
    zero = lambda n: jnp.zeros((8, n), F32)
    for ref, n in ((x_pad, WIDTH), (cv_pad, ATT), (dc_pad, ATT), (kl_pad, 128), (ds_pad, WIDTH)):
        ref[0:8, :] = zero(n)
        ref[SEQ + 8 : SEQ + 16, :] = zero(n)

    @pl.when(step == 0)
    def _():
        acc_point[...] = jnp.zeros_like(acc_point)
        acc_kern[...] = jnp.zeros_like(acc_kern)
        acc_depth[...] = jnp.zeros_like(acc_depth)

    def fill(i, carry):
        r = pl.multiple_of(i * FB, FB)
        rows = pl.ds(r, FB)
        there = pl.ds(r + 8, FB)
        x_pad[there, :] = inp_ref[rows, :].astype(F32)
        cv_pad[there, :] = cv_ref[rows, :].astype(F32)
        dc_pad[there, :] = dconv_ref[rows, :].astype(F32)
        kl_pad[there, :] = kern_ref[rows, :]
        return carry

    lax.fori_loop(0, SEQ // FB, fill, 0)

    def back(i, carry):
        r = pl.multiple_of(i * BB, BB)
        rows = pl.ds(r, BB)
        d_kern = jnp.zeros((BB, 128), F32)
        kl = kl_pad[pl.ds(r, (BB + 16)), :].astype(BF)
        for b in range(ATT // 128):
            lanes = slice(b * 128, (b + 1) * 128)
            spreader = tap_spread(b)
            cs = cv_pad[pl.ds(r, (BB + 16)), lanes]
            dc = dc_pad[pl.ds(r + 8, BB), lanes]
            prods = []
            for j in range(KER):
                moved = cs if j == 4 else pltpu.roll(cs, ((BB + 16) - (j - 4)) % (BB + 16), 0)
                prods.append((dc * moved[8 : 8 + BB]).astype(BF))
            d_kern = d_kern + mm_nt(jnp.concatenate(prods, -1), spreader)
            wide = mm(kl, spreader)
            dch = dc_pad[pl.ds(r, (BB + 16)), lanes]
            total = jnp.zeros((BB, 128), F32)
            for j in range(KER):
                term = wide[:, j * 128 : (j + 1) * 128] * dch
                moved = term if j == 4 else pltpu.roll(term, ((BB + 16) + (j - 4)) % (BB + 16), 0)
                total = total + moved[8 : 8 + BB]
            dcv_ref[rows, lanes] = total.astype(BF)
        kern = kern_ref[rows, :]
        dot_rows = lane_groups(kern * d_kern, jnp.add)
        d_logits = (kern * (d_kern - dot_rows)).astype(BF)
        q = q_ref[rows, :].astype(F32)
        ck = ck_ref[rows, :].astype(F32)
        mixed = (ck * q).astype(BF)
        acc_kern[...] += mm_tn(mixed, d_logits)
        d_mixed = mm_nt(d_logits, w_kern_ref[...])
        dq_ref[rows, :] = d_mixed * ck
        d_ck = (d_mixed * q).astype(BF)
        acc_point[...] += mm_tn(spread_ref[rows, :], d_ck)
        ds_pad[pl.ds(r + 8, BB), :] = mm_nt(d_ck, w_point_ref[...])
        return carry

    lax.fori_loop(0, SEQ // BB, back, 0)

    def depth(i, carry):
        r = pl.multiple_of(i * DB, DB)
        rows = pl.ds(r, DB)
        for b in range(WIDTH // 128):
            lanes = slice(b * 128, (b + 1) * 128)
            dsh = ds_pad[pl.ds(r, (DB + 16)), lanes]
            tap = lambda j: w_depth_ref[j : j + 1, lanes]
            shifted = [dsh] + [pltpu.roll(dsh, s, 0) for s in (1, 2, 3)]
            low_part = sum(tap(s) * shifted[s] for s in range(4))
            mid_part = sum(tap(4 + s) * shifted[s] for s in range(4))
            high_part = tap(8) * dsh
            low_part = pltpu.roll(low_part, (DB + 16) - 4, 0)
            high_part = pltpu.roll(high_part, 4, 0)
            taps = (low_part + mid_part + high_part)[8 : 8 + DB]
            din_ref[rows, lanes] = taps + first_ref[rows, lanes]
            xs = x_pad[pl.ds(r + 8, DB), lanes]
            far_low = [pltpu.roll(shifted[s], (DB + 16) - 4, 0) for s in range(4)]
            far_high = pltpu.roll(dsh, 4, 0)
            for j in range(KER):
                src = far_low[j] if j < 4 else (shifted[j - 4] if j < 8 else far_high)
                acc_depth[j, :, lanes] += fold_rows(src[8 : 8 + DB] * xs)
        return carry

    lax.fori_loop(0, SEQ // DB, depth, 0)

    @pl.when(step == last)
    def _():
        dpoint_ref[...] = acc_point[...]
        dkern_ref[...] = acc_kern[...]
        ddepth_ref[...] = jnp.sum(acc_depth[...], 1)


def conv_back(dctx, kern, proj, ck, spread, inputs, d_first_in, w_depth, w_point, w_kern):
    rows = inputs.shape[0]
    block = lambda n: pl.BlockSpec((SEQ, n), lambda s: (s, 0))
    at = lambda c: pl.BlockSpec((SEQ, ATT), lambda s: (s, c))
    return pl.pallas_call(
        conv_back_kernel,
        grid=(rows // SEQ,),
        in_specs=[
            at(1), block(128), at(0), at(3), block(ATT), block(WIDTH), block(WIDTH), block(WIDTH),
            whole((KER, WIDTH)), whole((WIDTH, ATT)), whole((ATT, 128)),
        ],
        out_specs=[
            block(ATT), block(ATT), block(WIDTH), whole_out((WIDTH, ATT)), whole_out((ATT, 128)),
            whole_out((KER, WIDTH)),
        ],
        out_shape=[
            jax.ShapeDtypeStruct((rows, ATT), F32),
            jax.ShapeDtypeStruct((rows, ATT), BF),
            jax.ShapeDtypeStruct((rows, WIDTH), F32),
            jax.ShapeDtypeStruct((WIDTH, ATT), F32),
            jax.ShapeDtypeStruct((ATT, 128), F32),
            jax.ShapeDtypeStruct((KER, WIDTH), F32),
        ],
        scratch_shapes=[
            pltpu.VMEM((SEQ + 16, WIDTH), F32),
            pltpu.VMEM((SEQ + 16, ATT), F32),
            pltpu.VMEM((SEQ + 16, ATT), F32),
            pltpu.VMEM((SEQ + 16, 128), F32),
            pltpu.VMEM((SEQ + 16, WIDTH), F32),
            pltpu.VMEM((WIDTH, ATT), F32),
            pltpu.VMEM((ATT, 128), F32),
            pltpu.VMEM((KER, 8, WIDTH), F32),
        ],
        compiler_params=params(1),
        cost_estimate=cost(25e9, 30e6),
        name="conv_back",
    )(dctx, kern, proj, proj, ck, spread, inputs, d_first_in, w_depth, w_point, w_kern)


def attend_back_kernel(
    q_ref, k_ref, v_ref, p_ref, o_ref, inv_ref, datt_ref, dqc_ref, dq_ref, dk_ref, dv_ref
):
    scale = HEAD**-0.5
    v = v_ref[...]
    d_att = datt_ref[...].astype(F32) * inv_ref[...]
    o = o_ref[...].astype(F32)
    q_all = q_ref[...].astype(F32) * scale
    k_all = k_ref[...].astype(F32) * scale
    dq, dk_t, dv_t = dqc_ref[...], 0.0, 0.0
    for head in (0, 1):
        mine = own_lanes(SEQ, head)
        da = jnp.where(mine, d_att, 0.0)
        dot_rows = jnp.sum(da * o, -1, keepdims=True)
        p = p_ref[0, head]
        ds = mm_nt(da.astype(BF), v)
        ds = (p.astype(F32) * (ds - dot_rows)).astype(BF)
        dq = dq + mm(ds, jnp.where(mine, k_all, 0.0).astype(BF))
        dk_t = dk_t + mm(jnp.where(mine, q_all, 0.0).T.astype(BF), ds)
        dv_t = dv_t + mm(da.T.astype(BF), p)
    dq_ref[...] = dq.astype(BF)
    dk_ref[...] = dk_t.T.astype(BF)
    dv_ref[...] = dv_t.T.astype(BF)


def attend_back(proj, probs, att, inv, dctx, dq_conv):
    rows = proj.shape[0]
    pairs = HEADS // 2
    col = lambda base: pl.BlockSpec((SEQ, 128), lambda s, p: (s, base + p))
    return pl.pallas_call(
        attend_back_kernel,
        grid=(rows // SEQ, pairs),
        in_specs=[
            col(0), col(pairs), col(2 * pairs),
            pl.BlockSpec((1, 2, SEQ, SEQ), lambda s, p: (s, p, 0, 0)),
            col(0), col(0), col(0), col(0),
        ],
        out_specs=[col(0)] * 3,
        out_shape=[jax.ShapeDtypeStruct((rows, ATT), BF)] * 3,
        compiler_params=params(2),
        cost_estimate=cost(30e9, 40e6),
        name="attend_back",
    )(proj, proj, proj, probs, att, inv, dctx, dq_conv)


WB = 512


def weight_kernel(core_ref, inp_ref, dq_ref, dk_ref, dv_ref, dcv_ref, point_ref, extra_ref, *refs):
    grad_refs, acc = refs[:-1], refs[-1]
    step = pl.program_id(0)
    last = pl.num_programs(0) - 1
    inp = inp_ref[...]

    @pl.when(step == 0)
    def _():
        acc[...] = jnp.zeros_like(acc)

    for n, ref in enumerate((dq_ref, dk_ref, dv_ref, dcv_ref)):
        acc[:, n * ATT : (n + 1) * ATT] += mm_tn(inp, ref[...])

    @pl.when(step == last)
    def _():
        for c, grad in enumerate(grad_refs):

            def emit(i, carry):
                owner = i
                if len(grad_refs) == 2:
                    owner = (i // 8) * 16 + (core_ref[0] ^ c) * 8 + i % 8
                rows = pl.ds(pl.multiple_of(owner * 24, 8), 24)
                o = acc[rows, :]
                cols = [o[:, n * ATT : (n + 1) * ATT] for n in range(4)]
                grad[i] = jnp.concatenate(cols + [point_ref[rows, :], extra_ref[owner]], 0).astype(BF)
                return carry

            lax.fori_loop(0, grad.shape[0], emit, 0)


def weight_grad(inputs, dq, dk, dv, dcv, d_point, extra, core=None):
    rows = inputs.shape[0]
    block = lambda n: pl.BlockSpec((WB, n), lambda s: (s, 0))
    shapes = [(32, 128, LANES)] if core is None else [(16, 128, LANES)] * 2
    core = jnp.zeros((1,), jnp.int32) if core is None else core
    return pl.pallas_call(
        weight_kernel,
        grid=(rows // WB,),
        in_specs=[pl.BlockSpec(memory_space=pltpu.SMEM), block(WIDTH)]
        + [block(ATT)] * 4
        + [whole(d_point.shape), whole(extra.shape)],
        out_specs=[whole_out(s) for s in shapes],
        out_shape=[jax.ShapeDtypeStruct(s, BF) for s in shapes],
        scratch_shapes=[pltpu.VMEM((WIDTH, 4 * ATT), F32)],
        compiler_params=params(1),
        cost_estimate=cost(12e9, 12e6),
        name="weight_grad",
    )(core, inputs, dq, dk, dv, dcv, d_point, extra)


LC = 512
STEPS = SEQ // LC


def leave_kernel(
    dq_ref, dk_ref, dv_ref, dcv_ref, rest_ref, mask_ref, to_ref, w_in_ref, out_ref, moved, kept
):
    step = pl.program_id(1)
    rows = pl.ds(pl.multiple_of((step % STEPS) * LC, LC), LC)

    @pl.when(step < STEPS)
    def _():
        d_proj = jnp.concatenate([dq_ref[...], dk_ref[...], dv_ref[...], dcv_ref[...]], 1)
        total = mm_nt(d_proj, w_in_ref[...]) + rest_ref[...]
        moved[rows, :] = total.astype(BF)
        kept[rows, :] = jnp.where(mask_ref[...] == 1, 0.0, total)

    @pl.when(step >= STEPS)
    def _():
        target = lax.broadcasted_iota(jnp.int32, (LC, SEQ), 0) + (step - STEPS) * LC
        hot = (target == to_ref[0]).astype(F32).astype(BF)
        out_ref[...] = kept[rows, :] + mm(hot, moved[...])


def leave(dq, dk, dv, dcv, d_rest, mask_col, to_row, w_in):
    rows = dq.shape[0]
    block = lambda n: pl.BlockSpec((LC, n), lambda s, i: (s * STEPS + jnp.minimum(i, STEPS - 1), 0))
    return pl.pallas_call(
        leave_kernel,
        grid=(rows // SEQ, 2 * STEPS),
        in_specs=[block(ATT)] * 4
        + [block(WIDTH), block(1), pl.BlockSpec((1, 1, SEQ), lambda s, i: (s, 0, 0)), whole((WIDTH, 4 * ATT))],
        out_specs=pl.BlockSpec((LC, WIDTH), lambda s, i: (s * STEPS + jnp.maximum(i - STEPS, 0), 0)),
        out_shape=jax.ShapeDtypeStruct((rows, WIDTH), F32),
        scratch_shapes=[pltpu.VMEM((SEQ, WIDTH), BF), pltpu.VMEM((SEQ, WIDTH), F32)],
        compiler_params=params(2),
        cost_estimate=cost(15e9, 30e6),
        name="leave",
    )(dq, dk, dv, dcv, d_rest, mask_col, to_row, w_in)


def pack_taps(kernel_full):
    by_tap = kernel_full.reshape(ATT, HEADS, KER).transpose(0, 2, 1)
    return jnp.pad(by_tap, ((0, 0), (0, 16 - KER), (0, 8 - HEADS))).reshape(ATT, 128)


def unpack_taps(packed):
    return packed.reshape(ATT, 16, 8)[:, :KER, :HEADS].transpose(0, 2, 1).reshape(ATT, HEADS * KER)


def per_device(
    tokens,
    masked,
    replace_ids,
    in_weight,
    depth_weight,
    point_weight,
    kernel_weight,
    out_weight,
    gain_one,
    shift_one,
    ffn_in,
    feedforward_output,
    gain_two,
    shift_two,
    cotangent,
):
    rows = tokens.shape[0]
    seqs = rows // SEQ
    dp, fsdp = lax.axis_size("dp"), lax.axis_size("fsdp")
    devices = dp * fsdp
    near = dp == NEAR["dp"] and fsdp == NEAR["fsdp"]
    own, hid = in_weight.shape[0], ffn_in.shape[2]
    n_depth, n_kern, n_vec = KER * own, kernel_weight.size, 4 * own
    hit = masked == 1
    here = jnp.arange(rows, dtype=jnp.int32) % SEQ
    pick = jnp.where(hit, replace_ids, here)[:, None]
    to_row = jnp.where(hit, replace_ids, -1).reshape(seqs, 1, SEQ)
    scale = 1.0 / math.sqrt(rows * devices)

    vec_own = jnp.stack([gain_one, shift_one, gain_two, shift_two])
    small_own = as_rows(
        jnp.concatenate([depth_weight.reshape(-1), kernel_weight.reshape(-1), vec_own.reshape(-1)])
    )
    head_own = jnp.concatenate([in_weight.reshape(own, 4, ATT).transpose(1, 0, 2), point_weight[None]])
    mid_own = jnp.concatenate(
        [
            out_weight.reshape(own, 2, ATT).transpose(1, 0, 2).reshape(-1, LANES),
            ffn_in.transpose(0, 2, 1).reshape(-1, LANES),
            feedforward_output.reshape(-1, LANES),
        ]
    )
    if near:
        me = place().astype(jnp.int32).reshape(1)
        pair, core = me // 2, me // CORE_BIT % 2
        slab, pick = tie(pair_slab(head_own, small_own), pick)
        slabs = [slab] + [hop(slab, k * Z_BIT) for k in (1, 2, 3)]
        across = [hop(slab, X_BIT)]
        inputs, (across, slabs[1:]) = tie(pick_rows(pick, tokens), (across, slabs[1:]))
        slabs[1:], mid_own = tie(slabs[1:], mid_own)
        mid = lax.all_gather(mid_own, AXES, axis=0)
        slabs = slabs + across + [hop(slab, X_BIT) for slab in slabs[1:]]
        slabs = slabs + [hop(slab, CORE_BIT) for slab in slabs]
        small_all = small_rows(slabs, pair)
    else:
        small_all = lax.all_gather(small_own, AXES, axis=0).reshape(devices, -1)
        w_all = lax.all_gather(head_own, AXES, axis=1, tiled=True).reshape(5, 16, 48, LANES)
        slabs = [w_all[:, bits].reshape(-1, LANES) for bits in SLAB_BITS]
        mid = lax.all_gather(mid_own, AXES, axis=0)
        w_out = mid[:, : 2 * own].reshape(devices, 2, own, ATT).transpose(1, 0, 2, 3)
        w_out = w_out.reshape(2, BLOCKS, 24, ATT).transpose(1, 0, 2, 3).reshape(BLOCKS, 48, ATT)
        w_ffn = mid[:, 2 * own :].reshape(devices, 4, hid, ATT).transpose(1, 0, 2, 3)
        w_ffn = w_ffn.reshape(4, BLOCKS, 48, ATT).transpose(1, 0, 2, 3).reshape(BLOCKS, 192, ATT)
        mid = jnp.concatenate([w_out, w_ffn], 1)
        pair, core = jnp.zeros((1,), jnp.int32), None
        inputs = pick_rows(pick, tokens)
    w_depth = small_all[:, :n_depth].reshape(devices, KER, own).transpose(1, 0, 2).reshape(KER, WIDTH)
    w_depth = w_depth.astype(F32)
    w_kern = pack_taps(small_all[:fsdp, n_depth : n_depth + n_kern].reshape(ATT, HEADS * KER))
    vecs = small_all[:, n_depth + n_kern :][:, :n_vec].reshape(devices, 4, own)
    vecs = vecs.transpose(1, 0, 2).reshape(4, WIDTH).astype(F32)

    proj, spread, ck, kern, conv, w_in, w_point = enter(inputs, pair, w_depth, w_kern, slabs)
    probs, att, inv = attend(proj)
    out, dctx, d_first_in, d_vecs, mid_grad = middle(att, conv, inputs, cotangent, mid, vecs)
    if near:
        mid_sum = lax.psum_scatter(mid_grad, AXES, scatter_dimension=0, tiled=True)[0]
    dq_conv, dcv, d_rest, d_point, d_kern, d_depth = conv_back(
        dctx, kern, proj, ck, spread, inputs, d_first_in, w_depth, w_point, w_kern
    )
    by_owner = lambda g: g.reshape(-1, devices, own).transpose(1, 0, 2).reshape(devices, -1)
    kern_by = jnp.tile(unpack_taps(d_kern).reshape(fsdp, -1), (dp, 1))
    small_grad = jnp.concatenate([by_owner(d_depth), kern_by, by_owner(d_vecs)], 1)
    small_grad = jnp.pad(small_grad, ((0, 0), (0, -small_grad.shape[1] % LANES)))
    small_grad = small_grad.reshape(devices, -1, LANES)
    dq, dk, dv = attend_back(proj, probs, att, inv, dctx, dq_conv)
    mask_col = masked[:, None]
    if near:
        mine, other = weight_grad(inputs, dq, dk, dv, dcv, d_point, small_grad, core)
        parts = fold_xy(me, mine, hop(other, CORE_BIT))
        parts = [parts[0]] + [hop(part, bit) for part, bit in zip(parts[1:], (Y_BIT, X_BIT, X_BIT + Y_BIT))]
        parts[0], dq = tie(parts[0], dq)
        d_tokens = leave(dq, dk, dv, dcv, d_rest, mask_col, to_row, w_in)
        d_tokens, parts = tie(d_tokens, parts)
        parts = fold_z(me, parts)
        parts = [parts[0]] + [hop(parts[k], k * Z_BIT) for k in (1, 2, 3)]
        parts[0], mid_sum = tie(parts[0], mid_sum)
        d_out, d_up, d_down = finish_mid(scale, mid_sum)
        d_up = d_up.transpose(0, 2, 1)
        parts[3], d_out = tie(parts[3], d_out)
        d_in, d_point, small_sum = finish(scale, parts)
        small_sum = small_sum.reshape(-1)
    else:
        (grads,) = weight_grad(inputs, dq, dk, dv, dcv, d_point, jnp.zeros((32, 8, LANES), F32))
        d_in = grads[:, :96].reshape(32, 4, 24, ATT).transpose(0, 2, 1, 3).reshape(devices, -1, LANES)
        d_point = grads[:, 96:120].reshape(devices, -1, LANES)
        w_out = mid_grad[:, :48].reshape(BLOCKS, 2, 24, ATT).transpose(0, 2, 1, 3).reshape(devices, -1, LANES)
        w_ffn = mid_grad[:, 48:].reshape(BLOCKS, 4, 48, ATT).transpose(1, 0, 2, 3)
        w_ffn = w_ffn.reshape(4, devices, hid, ATT).transpose(1, 0, 2, 3).reshape(devices, -1, LANES)
        packed = jnp.concatenate([w_out, w_ffn, d_in, d_point, small_grad.astype(BF)], 1)
        total = lax.psum_scatter(packed, AXES, scatter_dimension=0, tiled=True)[0].astype(F32) * scale
        cuts = [2 * own, 2 * own + 2 * hid, 2 * own + 4 * hid, 6 * own + 4 * hid, 7 * own + 4 * hid]
        d_out, d_up, d_down, d_in, d_point, small_sum = jnp.split(total, cuts)
        d_out, d_in, small_sum = d_out.reshape(own, WIDTH), d_in.reshape(own, 4 * ATT), small_sum.reshape(-1)
        d_up, d_down = d_up.reshape(2, hid, ATT).transpose(0, 2, 1), d_down.reshape(2, hid, ATT)
        d_tokens = leave(dq, dk, dv, dcv, d_rest, mask_col, to_row, w_in)
    kern_sum = small_sum[n_depth : n_depth + n_kern].reshape(kernel_weight.shape)
    vec_sum = small_sum[n_depth + n_kern :][:n_vec].reshape(4, own)
    return (
        out,
        d_tokens,
        d_in,
        small_sum[:n_depth].reshape(KER, own),
        d_point,
        kern_sum,
        d_out,
        vec_sum[0],
        vec_sum[1],
        d_up,
        d_down,
        vec_sum[2],
        vec_sum[3],
    )


def solution(mesh):
    return jax.shard_map(
        per_device,
        mesh=mesh,
        in_specs=(
            P(("dp", "fsdp"), None),
            P(("dp", "fsdp")),
            P(("dp", "fsdp")),
            P(("dp", "fsdp"), None),
            P(None, ("dp", "fsdp")),
            P(("dp", "fsdp"), None),
            P("fsdp", None),
            P(("dp", "fsdp"), None),
            P(("dp", "fsdp")),
            P(("dp", "fsdp")),
            P(None, None, ("dp", "fsdp")),
            P(None, ("dp", "fsdp"), None),
            P(("dp", "fsdp")),
            P(("dp", "fsdp")),
            P(("dp", "fsdp"), None),
        ),
        out_specs=(
            P(("dp", "fsdp"), None),
            P(("dp", "fsdp"), None),
            P(("dp", "fsdp"), None),
            P(None, ("dp", "fsdp")),
            P(("dp", "fsdp"), None),
            P("fsdp", None),
            P(("dp", "fsdp"), None),
            P(("dp", "fsdp")),
            P(("dp", "fsdp")),
            P(None, None, ("dp", "fsdp")),
            P(None, ("dp", "fsdp"), None),
            P(("dp", "fsdp")),
            P(("dp", "fsdp")),
        ),
        check_vma=False,
    )
```

```python
from functools import partial
import math

import jax
import jax.numpy as jnp
from jax import lax
from jax.experimental import pallas as pl
from jax.experimental.pallas import tpu as pltpu
from jax.sharding import PartitionSpec as P

BF = jnp.bfloat16
F32 = jnp.float32
HEADS = 6
HEAD = 64
SEQ = 1024
KER = 9
ATT = HEADS * HEAD
WIDTH = 768
VMEM_MAX = 60 * 1024 * 1024


def mm(a, b):
    return jnp.dot(a, b, preferred_element_type=F32)


def mm_nt(a, b):
    return lax.dot_general(a, b, (((1,), (1,)), ((), ())), preferred_element_type=F32)


def mm_tn(a, b):
    return lax.dot_general(a, b, (((0,), (0,)), ((), ())), preferred_element_type=F32)


def params(count):
    return pltpu.CompilerParams(
        dimension_semantics=("arbitrary",) * count, vmem_limit_bytes=VMEM_MAX
    )


def cost(flops, moved):
    return pl.CostEstimate(flops=int(flops), bytes_accessed=int(moved), transcendentals=0)


def whole(shape):
    zeros = (0,) * len(shape)
    return pl.BlockSpec(shape, lambda *_: zeros, pipeline_mode=pl.Buffered(1))


def whole_out(shape):
    zeros = (0,) * len(shape)
    return pl.BlockSpec(shape, lambda *_: zeros)


AXES = ("dp", "fsdp")
LANES = 384
NEAR = {"dp": 4, "fsdp": 8}
X_BIT, CORE_BIT, Z_BIT, Y_BIT = 16, 8, 2, 1


def as_rows(x):
    flat = x.reshape(-1)
    return jnp.pad(flat, (0, -flat.size % LANES)).reshape(-1, LANES)


def place():
    return lax.axis_index("dp") * NEAR["fsdp"] + lax.axis_index("fsdp")


def hop(x, mask):
    return lax.ppermute(x, AXES, [(i, i ^ mask) for i in range(32)])


def tie(first, second):
    return lax.optimization_barrier((first, second))


def fold_xy_kernel(me_ref, mine_ref, other_ref, *outs):
    x, y = me_ref[0] // X_BIT, me_ref[0] % 2
    for k, out in enumerate(outs):
        at = (x ^ (k // 2), 0, y ^ (k % 2))
        out[0] = (mine_ref[at].astype(F32) + other_ref[at].astype(F32)).astype(BF)


def fold_xy(me, mine, other):
    rows = mine.shape[-2]
    views = [a.reshape(2, 4, 2, rows, LANES) for a in (mine, other)]
    return pl.pallas_call(
        fold_xy_kernel,
        grid=(4,),
        in_specs=[pl.BlockSpec(memory_space=pltpu.SMEM)]
        + [pl.BlockSpec((2, 1, 2, rows, LANES), lambda z: (0, z, 0, 0, 0))] * 2,
        out_specs=[pl.BlockSpec((1, rows, LANES), lambda z: (z, 0, 0))] * 4,
        out_shape=[jax.ShapeDtypeStruct((4, rows, LANES), BF)] * 4,
        compiler_params=params(1),
        cost_estimate=cost(0, 6 * mine.size),
        name="fold_xy",
    )(me, *views)


def fold_z_kernel(me_ref, *refs):
    z = (me_ref[0] // Z_BIT) % 4
    for k, out in enumerate(refs[4:]):
        total = refs[0][z ^ k].astype(F32)
        for ref in refs[1:4]:
            total = total + ref[z ^ k].astype(F32)
        out[...] = total.astype(BF)


def fold_z(me, arrays):
    rows = arrays[0].shape[-2]
    return pl.pallas_call(
        fold_z_kernel,
        in_specs=[pl.BlockSpec(memory_space=pltpu.SMEM)] + [pl.BlockSpec(memory_space=pltpu.VMEM)] * 4,
        out_specs=[pl.BlockSpec(memory_space=pltpu.VMEM)] * 4,
        out_shape=[jax.ShapeDtypeStruct((rows, LANES), BF)] * 4,
        compiler_params=pltpu.CompilerParams(vmem_limit_bytes=16 * 1024 * 1024),
        cost_estimate=cost(0, 10 * arrays[0].size),
        name="fold_z",
    )(me, *arrays)


def finish_kernel(scale, a_ref, b_ref, c_ref, d_ref, in_ref, point_ref, depth_ref, kern_ref, vec_ref):
    total = sum(ref[...].astype(F32) for ref in (a_ref, b_ref, c_ref, d_ref)) * scale
    for n in range(4):
        in_ref[:, n * ATT : (n + 1) * ATT] = total[24 * n : 24 * n + 24]
    point_ref[...] = total[96:120]
    at = 0
    for ref in (depth_ref, kern_ref, vec_ref):
        count, width = ref.shape
        for i in range(count):
            row, lane = 120 + at // LANES, at % LANES
            here = min(width, LANES - lane)
            ref[i : i + 1, :here] = total[row : row + 1, lane : lane + here]
            if here < width:
                ref[i : i + 1, here:] = total[row + 1 : row + 2, : width - here]
            at += width


def finish(scale, arrays, small_shapes):
    vmem = pl.BlockSpec(memory_space=pltpu.VMEM)
    return pl.pallas_call(
        partial(finish_kernel, scale),
        in_specs=[vmem] * 4,
        out_specs=[vmem] * 5,
        out_shape=[
            jax.ShapeDtypeStruct((24, 4 * ATT), F32),
            jax.ShapeDtypeStruct((24, ATT), F32),
        ]
        + [jax.ShapeDtypeStruct(shape, F32) for shape in small_shapes],
        name="finish",
    )(*arrays)


def finish_mid_kernel(scale, sum_ref, out_ref, up_ref, down_ref):
    total = sum_ref[...].astype(F32) * scale
    out_ref[:, :ATT] = total[:24]
    out_ref[:, ATT:] = total[24:48]
    for g in (0, 1):
        up_ref[g] = total[48 + 48 * g : 96 + 48 * g]
        down_ref[g] = total[144 + 48 * g : 192 + 48 * g]


def finish_mid(scale, packed):
    vmem = pl.BlockSpec(memory_space=pltpu.VMEM)
    return pl.pallas_call(
        partial(finish_mid_kernel, scale),
        in_specs=[vmem],
        out_specs=[vmem] * 3,
        out_shape=[
            jax.ShapeDtypeStruct((24, WIDTH), F32),
            jax.ShapeDtypeStruct((2, 48, ATT), F32),
            jax.ShapeDtypeStruct((2, 48, ATT), F32),
        ],
        name="finish_mid",
    )(packed)


SLAB_BITS = [((s // 4) % 2 * X_BIT + (s // 8) * CORE_BIT + s % 4 * Z_BIT) // 2 for s in range(16)]


def pair_slab(own, small):
    packed = jnp.concatenate([own.reshape(-1, LANES), small])
    other = hop(packed, Y_BIT)
    even = place() % 2 == 0
    first, second = jnp.where(even, packed, other), jnp.where(even, other, packed)
    both = [x[:120].reshape(5, 24, LANES) for x in (first, second)]
    return jnp.concatenate([jnp.concatenate(both, 1).reshape(-1, LANES), first[120:], second[120:]])


def small_rows(slabs, pair):
    spot = jnp.array([SLAB_BITS.index(b) for b in range(16)], jnp.int32)
    order = jnp.take(spot, jnp.arange(16, dtype=jnp.int32) ^ pair)
    return jnp.take(jnp.stack([slab[240:] for slab in slabs]), order, axis=0).reshape(32, -1)


def lane_groups(x, combine):
    for step in (64, 32, 16, 8):
        x = combine(x, pltpu.roll(x, step, 1))
    return x


def tap_spread(block):
    rows = lax.broadcasted_iota(jnp.int32, (128, KER * 128), 0)
    cols = lax.broadcasted_iota(jnp.int32, (128, KER * 128), 1)
    want = (cols // 128) * 8 + block * 2 + (cols % 128) // HEAD
    return (rows == want).astype(F32).astype(BF)


EC = 1024
FB = 512
BB = 1024
DB = 512


def pick_kernel(pick_ref, tok_ref, inp_ref):
    cols = lax.broadcasted_iota(jnp.int32, (SEQ, SEQ), 1)
    hot = (cols == pick_ref[...]).astype(F32).astype(BF)
    inp_ref[...] = mm(hot, tok_ref[...]).astype(BF)


def pick_rows(pick, tokens):
    block = lambda n: pl.BlockSpec((SEQ, n), lambda s: (s, 0))
    return pl.pallas_call(
        pick_kernel,
        grid=(tokens.shape[0] // SEQ,),
        in_specs=[block(1), block(WIDTH)],
        out_specs=block(WIDTH),
        out_shape=jax.ShapeDtypeStruct(tokens.shape, BF),
        compiler_params=params(1),
        cost_estimate=cost(6e9, 6e6),
        name="pick",
    )(pick, tokens)


def enter_kernel(
    inp_ref, w_in_ref, w_depth_ref, w_point_ref, w_kern_ref,
    proj_ref, spread_ref, ck_ref, kern_ref, conv_ref,
    x_pad, cv_pad,
):
    x_pad[0:8, :] = jnp.zeros((8, WIDTH), F32)
    x_pad[SEQ + 8 : SEQ + 16, :] = jnp.zeros((8, WIDTH), F32)
    cv_pad[0:8, :] = jnp.zeros((8, ATT), F32)
    cv_pad[SEQ + 8 : SEQ + 16, :] = jnp.zeros((8, ATT), F32)

    def load(i, carry):
        r = pl.multiple_of(i * EC, EC)
        low = inp_ref[pl.ds(r, EC), :]
        x_pad[pl.ds(r + 8, EC), :] = low.astype(F32)
        proj = mm(low, w_in_ref[...])
        proj_low = proj.astype(BF)
        proj_ref[pl.ds(r, EC), :] = proj_low
        cv_pad[pl.ds(r + 8, EC), :] = proj_low[:, 3 * ATT :].astype(F32)
        return carry

    lax.fori_loop(0, SEQ // EC, load, 0)

    def conv(i, carry):
        r = pl.multiple_of(i * EC, EC)
        for b in range(WIDTH // 128):
            lanes = slice(b * 128, (b + 1) * 128)
            xs = x_pad[pl.ds(r, (EC + 16)), lanes]
            shifted = [xs] + [pltpu.roll(xs, (EC + 16) - s, 0) for s in (1, 2, 3)]
            tap = lambda j: w_depth_ref[j : j + 1, lanes]
            low_part = sum(tap(s) * shifted[s] for s in range(4))
            mid_part = sum(tap(4 + s) * shifted[s] for s in range(4))
            high_part = tap(8) * xs
            low_part = pltpu.roll(low_part, (EC + 16) - 4, 0)
            high_part = pltpu.roll(high_part, (EC + 16) - 4, 0)
            total = low_part[0:EC] + mid_part[8 : 8 + EC] + high_part[8 : 8 + EC]
            spread_ref[pl.ds(r, EC), lanes] = total.astype(BF)
        ck = mm(spread_ref[pl.ds(r, EC), :], w_point_ref[...]).astype(BF)
        ck_ref[pl.ds(r, EC), :] = ck
        q = proj_ref[pl.ds(r, EC), 0:ATT].astype(F32)
        mixed = (ck.astype(F32) * q).astype(BF)
        logits = mm(mixed, w_kern_ref[...])
        lane = lax.broadcasted_iota(jnp.int32, (EC, 128), 1)
        logits = jnp.where(lane < KER * 8, logits, -1e30)
        top = lane_groups(logits, jnp.maximum)
        e = jnp.exp(logits - top)
        kern = e / lane_groups(e, jnp.add)
        kern_ref[pl.ds(r, EC), :] = kern
        kern_low = kern.astype(BF)
        for b in range(ATT // 128):
            lanes = slice(b * 128, (b + 1) * 128)
            wide = mm(kern_low, tap_spread(b))
            cs = cv_pad[pl.ds(r, (EC + 16)), lanes]
            total = jnp.zeros((EC, 128), F32)
            for j in range(KER):
                moved = cs if j == 4 else pltpu.roll(cs, ((EC + 16) - (j - 4)) % (EC + 16), 0)
                total = total + wide[:, j * 128 : (j + 1) * 128] * moved[8 : 8 + EC]
            conv_ref[pl.ds(r, EC), lanes] = total.astype(BF)
        return carry

    lax.fori_loop(0, SEQ // EC, conv, 0)


def enter_slabs_kernel(pair_ref, inp_ref, w_depth_ref, w_kern_ref, *refs):
    slabs, outs = refs[:16], refs[16:]
    results, w_in_ref, w_point_ref, scratch, sems = outs[:5], outs[5], outs[6], outs[7:9], outs[9]

    @pl.when(pl.program_id(0) == 0)
    def _():
        copies = []
        for s, slab in enumerate(slabs):
            spot = pl.ds(pl.multiple_of((pair_ref[0] ^ SLAB_BITS[s]) * 48, 16), 48)
            for b in range(5):
                to = w_in_ref.at[spot, b * ATT : (b + 1) * ATT] if b < 4 else w_point_ref.at[spot, :]
                copies.append(pltpu.make_async_copy(slab.at[b * 48 : (b + 1) * 48, :], to, sems.at[s, b]))
        for copy in copies:
            copy.start()
        for copy in copies:
            copy.wait()

    enter_kernel(inp_ref, w_in_ref, w_depth_ref, w_point_ref, w_kern_ref, *results, *scratch)


def enter(inputs, pair, w_depth, w_kern, slabs):
    rows = inputs.shape[0]
    block = lambda n: pl.BlockSpec((SEQ, n), lambda s: (s, 0))
    widths = ((4 * ATT, BF), (WIDTH, BF), (ATT, BF), (128, F32), (ATT, BF))
    return pl.pallas_call(
        enter_slabs_kernel,
        grid=(rows // SEQ,),
        in_specs=[
            pl.BlockSpec(memory_space=pltpu.SMEM), block(WIDTH), whole((KER, WIDTH)), whole((ATT, 128)),
        ]
        + [pl.BlockSpec(memory_space=pl.ANY)] * 16,
        out_specs=[block(n) for n, _ in widths] + [whole_out((WIDTH, 4 * ATT)), whole_out((WIDTH, ATT))],
        out_shape=[jax.ShapeDtypeStruct((rows, n), t) for n, t in widths]
        + [jax.ShapeDtypeStruct((WIDTH, 4 * ATT), BF), jax.ShapeDtypeStruct((WIDTH, ATT), BF)],
        scratch_shapes=[
            pltpu.VMEM((SEQ + 16, WIDTH), F32),
            pltpu.VMEM((SEQ + 16, ATT), F32),
            pltpu.SemaphoreType.DMA((16, 5)),
        ],
        compiler_params=params(1),
        cost_estimate=cost(20e9, 20e6),
        name="enter",
    )(pair, inputs, w_depth, w_kern, *slabs)


def own_lanes(rows, head):
    lane = lax.broadcasted_iota(jnp.int32, (rows, 128), 1)
    return (lane // HEAD) == head


AC = 512


def attend_kernel(q_ref, k_ref, v_ref, p_ref, o_ref, inv_ref):
    k = k_ref[...]
    v_all = v_ref[...].astype(F32)
    vs = [jnp.where(own_lanes(SEQ, head), v_all, 1.0).astype(BF) for head in (0, 1)]
    first = own_lanes(AC, 0)

    def part(i, carry):
        rows = pl.ds(pl.multiple_of(i * AC, AC), AC)
        q_all = q_ref[rows, :].astype(F32) * (HEAD**-0.5)
        outs = []
        for head in (0, 1):
            q = jnp.where(first if head == 0 else ~first, q_all, 0.0).astype(BF)
            s = mm_nt(q, k)
            p = jnp.exp(s - jnp.max(s, -1, keepdims=True)).astype(BF)
            p_ref[0, head, rows, :] = p
            outs.append(mm(p, vs[head]))
        inv = 1.0 / pltpu.roll(jnp.where(first, outs[1], outs[0]), HEAD, 1)
        o_ref[rows, :] = (jnp.where(first, outs[0], outs[1]) * inv).astype(BF)
        inv_ref[rows, :] = inv
        return carry

    lax.fori_loop(0, SEQ // AC, part, 0, unroll=2)


def attend(proj):
    rows = proj.shape[0]
    pairs = HEADS // 2
    col = lambda base: pl.BlockSpec((SEQ, 128), lambda s, p: (s, base + p))
    return pl.pallas_call(
        attend_kernel,
        grid=(rows // SEQ, pairs),
        in_specs=[col(0), col(pairs), col(2 * pairs)],
        out_specs=[pl.BlockSpec((1, 2, SEQ, SEQ), lambda s, p: (s, p, 0, 0)), col(0), col(0)],
        out_shape=[
            jax.ShapeDtypeStruct((rows // SEQ, HEADS, SEQ, SEQ), BF),
            jax.ShapeDtypeStruct((rows, ATT), BF),
            jax.ShapeDtypeStruct((rows, ATT), F32),
        ],
        compiler_params=params(2),
        cost_estimate=cost(25e9, 35e6),
        name="attend",
    )(proj, proj, proj)


ERF_P = 0.3275911 / math.sqrt(2.0)
ERF_A = (0.254829592, -0.284496736, 1.421413741, -1.453152027, 1.061405429)
PHI = 1.0 / math.sqrt(2.0 * math.pi)


def gelu_both(u):
    t = 1.0 / (1.0 + ERF_P * jnp.abs(u))
    poly = 0.5 * ERF_A[4]
    for a in ERF_A[3::-1]:
        poly = poly * t + 0.5 * a
    e = jnp.exp2((-0.5 * math.log2(math.e)) * (u * u))
    tail = t * poly * e
    cdf = jnp.where(u > 0, 1.0 - tail, tail)
    return u * cdf, cdf + (PHI * u) * e


def norm_parts(z):
    mean = jnp.mean(z, -1, keepdims=True)
    centred = z - mean
    var = jnp.mean(centred * centred, -1, keepdims=True)
    r = lax.rsqrt(var + 1e-12)
    return centred * r, r


def norm_back(c, xh, r, gain):
    gc = c * gain
    return r * (gc - jnp.mean(gc, -1, keepdims=True) - xh * jnp.mean(gc * xh, -1, keepdims=True))


def fold_rows(x):
    return jnp.sum(x.reshape(-1, 8, x.shape[-1]), 0)


MID = 256
FF = 1536
FC = 768
GROUP = 48
BLOCKS = FF // GROUP


def middle_kernel(
    att_ref, conv_ref, inp_ref, cot_ref, mid_ref, vec_ref,
    out_ref, dctx_ref, dfirst_ref, dvec_ref, packed_ref,
    acc_out, acc_up, acc_down, acc_vec, act_ref, slope_ref, flip_ref,
    w_out_ref, w_rows, w_up_blocks, w_down_blocks, sems,
):
    step = pl.program_id(0)
    last = pl.num_programs(0) - 1

    @pl.when(step == 0)
    def _():
        targets = [w_rows] + [w.at[g] for w in (w_up_blocks, w_down_blocks) for g in (0, 1)]
        copies = [
            pltpu.make_async_copy(mid_ref.at[:, n * GROUP : (n + 1) * GROUP, :], to, sems.at[n])
            for n, to in enumerate(targets)
        ]
        for copy in copies:
            copy.start()
        acc_up[...] = jnp.zeros_like(acc_up)
        acc_down[...] = jnp.zeros_like(acc_down)
        acc_vec[...] = jnp.zeros_like(acc_vec)
        copies[0].wait()
        half = GROUP // 2

        def unfold(i, carry):
            both = w_rows[i].astype(F32)
            rows = pl.ds(pl.multiple_of(i * half, 8), half)
            acc_out[rows, :] = jnp.concatenate([both[:half], both[half:]], 1)
            return carry

        lax.fori_loop(0, BLOCKS, unfold, 0)
        w_out_ref[...] = acc_out[...].astype(BF)
        acc_out[...] = jnp.zeros_like(acc_out)
        for copy in copies[1:]:
            copy.wait()

    def w_up(g, f):
        return w_up_blocks[g, f * FC // GROUP : (f + 1) * FC // GROUP].reshape(FC, ATT)

    def w_down(g, f):
        return w_down_blocks[g, f * FC // GROUP : (f + 1) * FC // GROUP].reshape(FC, ATT)

    ctx = jnp.concatenate([att_ref[...], conv_ref[...]], -1)
    g_one, s_one = vec_ref[0:1, :], vec_ref[1:2, :]
    g_two, s_two = vec_ref[2:3, :], vec_ref[3:4, :]
    first_in = mm(ctx, w_out_ref[...]) + inp_ref[...].astype(F32)
    xh_one, r_one = norm_parts(first_in)
    first = xh_one * g_one + s_one
    first_low = first.astype(BF)
    outs = []
    for g in (0, 1):
        cols = slice(g * ATT, (g + 1) * ATT)
        total = None
        for f in range(FF // FC):
            hid = slice(f * FC, (f + 1) * FC)
            inner = mm_nt(first_low[:, cols], w_up(g, f))
            act, slope = gelu_both(inner)
            act = act.astype(BF)
            act_ref[g, :, hid] = act
            slope_ref[g, :, hid] = slope.astype(slope_ref.dtype)
            part = mm(act, w_down(g, f))
            total = part if total is None else total + part
        outs.append(total)
    xh_two, r_two = norm_parts(jnp.concatenate(outs, -1) + first)
    out_ref[...] = (xh_two * g_two + s_two).astype(BF)
    c = cot_ref[...].astype(F32)
    acc_vec[2] += fold_rows(c * xh_two)
    acc_vec[3] += fold_rows(c)
    d_second = norm_back(c, xh_two, r_two, g_two)
    d_outer = d_second.astype(BF)
    d_outer_t = d_second.T.astype(BF)
    first_t = first.T.astype(BF)
    backs = []
    for g in (0, 1):
        cols = slice(g * ATT, (g + 1) * ATT)
        total = None
        for f in range(FF // FC):
            hid = slice(f * FC, (f + 1) * FC)
            d_act = mm_nt(d_outer[:, cols], w_down(g, f))
            d_inner = (d_act * slope_ref[g, :, hid].astype(F32)).astype(BF)
            acc_down[g, :, hid] += mm(d_outer_t[cols, :], act_ref[g, :, hid])
            acc_up[g, :, hid] += mm(first_t[cols, :], d_inner)
            part = mm(d_inner, w_up(g, f))
            total = part if total is None else total + part
        backs.append(total)
    d_first = jnp.concatenate(backs, -1) + d_second
    acc_vec[0] += fold_rows(d_first * xh_one)
    acc_vec[1] += fold_rows(d_first)
    d_first_in = norm_back(d_first, xh_one, r_one, g_one)
    dfirst_ref[...] = d_first_in
    d_dense = d_first_in.astype(BF)
    acc_out[...] += mm_tn(ctx, d_dense)
    dctx_ref[...] = mm_nt(d_dense, w_out_ref[...]).astype(BF)

    @pl.when(step == last)
    def _():
        dvec_ref[...] = jnp.sum(acc_vec[...], 1)
        for g in (0, 1):
            flip_ref[0, g] = acc_up[g].T.astype(BF)
            flip_ref[1, g] = acc_down[g].T.astype(BF)

        def emit(i, carry):
            o = acc_out[pl.ds(pl.multiple_of(i * 24, 8), 24), :]
            packed_ref[i, 0:48, :] = jnp.concatenate([o[:, :ATT], o[:, ATT:]], 0).astype(BF)
            hidden = pl.ds(pl.multiple_of(i * 48, 16), 48)
            for n in range(4):
                packed_ref[i, 48 * n + 48 : 48 * n + 96, :] = flip_ref[n // 2, n % 2, hidden, :]
            return carry

        lax.fori_loop(0, BLOCKS, emit, 0)


def middle(att, conv, inputs, cot, mid, vecs):
    rows = att.shape[0]
    block = lambda n: pl.BlockSpec((MID, n), lambda s: (s, 0))
    packed = (BLOCKS, 5 * GROUP, LANES)
    return pl.pallas_call(
        middle_kernel,
        grid=(rows // MID,),
        in_specs=[
            block(ATT), block(ATT), block(WIDTH), block(WIDTH),
            pl.BlockSpec(memory_space=pl.ANY), whole((4, WIDTH)),
        ],
        out_specs=[block(WIDTH), block(WIDTH), block(WIDTH), whole_out((4, WIDTH)), whole_out(packed)],
        out_shape=[
            jax.ShapeDtypeStruct((rows, WIDTH), BF),
            jax.ShapeDtypeStruct((rows, WIDTH), BF),
            jax.ShapeDtypeStruct((rows, WIDTH), F32),
            jax.ShapeDtypeStruct((4, WIDTH), F32),
            jax.ShapeDtypeStruct(packed, BF),
        ],
        scratch_shapes=[
            pltpu.VMEM((WIDTH, WIDTH), F32),
            pltpu.VMEM((2, ATT, FF), F32),
            pltpu.VMEM((2, ATT, FF), F32),
            pltpu.VMEM((4, 8, WIDTH), F32),
            pltpu.VMEM((2, MID, FF), BF),
            pltpu.VMEM((2, MID, FF), F32),
            pltpu.VMEM((2, 2, FF, ATT), BF),
            pltpu.VMEM((WIDTH, WIDTH), BF),
            pltpu.VMEM((BLOCKS, GROUP, LANES), BF),
            pltpu.VMEM((2, BLOCKS, GROUP, ATT), BF),
            pltpu.VMEM((2, BLOCKS, GROUP, ATT), BF),
            pltpu.SemaphoreType.DMA((5,)),
        ],
        compiler_params=params(1),
        cost_estimate=cost(60e9, 40e6),
        name="middle",
    )(att, conv, inputs, cot, mid, vecs)


def conv_back_kernel(
    dconv_ref, kern_ref, q_ref, cv_ref, ck_ref, spread_ref, inp_ref, first_ref, w_depth_ref, w_point_ref, w_kern_ref,
    dq_ref, dcv_ref, din_ref, dpoint_ref, dkern_ref, ddepth_ref,
    x_pad, cv_pad, dc_pad, kl_pad, ds_pad, acc_point, acc_kern, acc_depth,
):
    step = pl.program_id(0)
    last = pl.num_programs(0) - 1
    zero = lambda n: jnp.zeros((8, n), F32)
    for ref, n in ((x_pad, WIDTH), (cv_pad, ATT), (dc_pad, ATT), (kl_pad, 128), (ds_pad, WIDTH)):
        ref[0:8, :] = zero(n)
        ref[SEQ + 8 : SEQ + 16, :] = zero(n)

    @pl.when(step == 0)
    def _():
        acc_point[...] = jnp.zeros_like(acc_point)
        acc_kern[...] = jnp.zeros_like(acc_kern)
        acc_depth[...] = jnp.zeros_like(acc_depth)

    def fill(i, carry):
        r = pl.multiple_of(i * FB, FB)
        rows = pl.ds(r, FB)
        there = pl.ds(r + 8, FB)
        x_pad[there, :] = inp_ref[rows, :].astype(F32)
        cv_pad[there, :] = cv_ref[rows, :].astype(F32)
        dc_pad[there, :] = dconv_ref[rows, :].astype(F32)
        kl_pad[there, :] = kern_ref[rows, :]
        return carry

    lax.fori_loop(0, SEQ // FB, fill, 0)

    def back(i, carry):
        r = pl.multiple_of(i * BB, BB)
        rows = pl.ds(r, BB)
        d_kern = jnp.zeros((BB, 128), F32)
        kl = kl_pad[pl.ds(r, (BB + 16)), :].astype(BF)
        for b in range(ATT // 128):
            lanes = slice(b * 128, (b + 1) * 128)
            spreader = tap_spread(b)
            cs = cv_pad[pl.ds(r, (BB + 16)), lanes]
            dc = dc_pad[pl.ds(r + 8, BB), lanes]
            prods = []
            for j in range(KER):
                moved = cs if j == 4 else pltpu.roll(cs, ((BB + 16) - (j - 4)) % (BB + 16), 0)
                prods.append((dc * moved[8 : 8 + BB]).astype(BF))
            d_kern = d_kern + mm_nt(jnp.concatenate(prods, -1), spreader)
            wide = mm(kl, spreader)
            dch = dc_pad[pl.ds(r, (BB + 16)), lanes]
            total = jnp.zeros((BB, 128), F32)
            for j in range(KER):
                term = wide[:, j * 128 : (j + 1) * 128] * dch
                moved = term if j == 4 else pltpu.roll(term, ((BB + 16) + (j - 4)) % (BB + 16), 0)
                total = total + moved[8 : 8 + BB]
            dcv_ref[rows, lanes] = total.astype(BF)
        kern = kern_ref[rows, :]
        dot_rows = lane_groups(kern * d_kern, jnp.add)
        d_logits = (kern * (d_kern - dot_rows)).astype(BF)
        q = q_ref[rows, :].astype(F32)
        ck = ck_ref[rows, :].astype(F32)
        mixed = (ck * q).astype(BF)
        acc_kern[...] += mm_tn(mixed, d_logits)
        d_mixed = mm_nt(d_logits, w_kern_ref[...])
        dq_ref[rows, :] = d_mixed * ck
        d_ck = (d_mixed * q).astype(BF)
        acc_point[...] += mm_tn(spread_ref[rows, :], d_ck)
        ds_pad[pl.ds(r + 8, BB), :] = mm_nt(d_ck, w_point_ref[...])
        return carry

    lax.fori_loop(0, SEQ // BB, back, 0)

    def depth(i, carry):
        r = pl.multiple_of(i * DB, DB)
        rows = pl.ds(r, DB)
        for b in range(WIDTH // 128):
            lanes = slice(b * 128, (b + 1) * 128)
            dsh = ds_pad[pl.ds(r, (DB + 16)), lanes]
            tap = lambda j: w_depth_ref[j : j + 1, lanes]
            shifted = [dsh] + [pltpu.roll(dsh, s, 0) for s in (1, 2, 3)]
            low_part = sum(tap(s) * shifted[s] for s in range(4))
            mid_part = sum(tap(4 + s) * shifted[s] for s in range(4))
            high_part = tap(8) * dsh
            low_part = pltpu.roll(low_part, (DB + 16) - 4, 0)
            high_part = pltpu.roll(high_part, 4, 0)
            taps = (low_part + mid_part + high_part)[8 : 8 + DB]
            din_ref[rows, lanes] = taps + first_ref[rows, lanes]
            xs = x_pad[pl.ds(r + 8, DB), lanes]
            far_low = [pltpu.roll(shifted[s], (DB + 16) - 4, 0) for s in range(4)]
            far_high = pltpu.roll(dsh, 4, 0)
            for j in range(KER):
                src = far_low[j] if j < 4 else (shifted[j - 4] if j < 8 else far_high)
                acc_depth[j, :, lanes] += fold_rows(src[8 : 8 + DB] * xs)
        return carry

    lax.fori_loop(0, SEQ // DB, depth, 0)

    @pl.when(step == last)
    def _():
        dpoint_ref[...] = acc_point[...]
        dkern_ref[...] = acc_kern[...]
        ddepth_ref[...] = jnp.sum(acc_depth[...], 1)


def conv_back(dctx, kern, proj, ck, spread, inputs, d_first_in, w_depth, w_point, w_kern):
    rows = inputs.shape[0]
    block = lambda n: pl.BlockSpec((SEQ, n), lambda s: (s, 0))
    at = lambda c: pl.BlockSpec((SEQ, ATT), lambda s: (s, c))
    return pl.pallas_call(
        conv_back_kernel,
        grid=(rows // SEQ,),
        in_specs=[
            at(1), block(128), at(0), at(3), block(ATT), block(WIDTH), block(WIDTH), block(WIDTH),
            whole((KER, WIDTH)), whole((WIDTH, ATT)), whole((ATT, 128)),
        ],
        out_specs=[
            block(ATT), block(ATT), block(WIDTH), whole_out((WIDTH, ATT)), whole_out((ATT, 128)),
            whole_out((KER, WIDTH)),
        ],
        out_shape=[
            jax.ShapeDtypeStruct((rows, ATT), F32),
            jax.ShapeDtypeStruct((rows, ATT), BF),
            jax.ShapeDtypeStruct((rows, WIDTH), F32),
            jax.ShapeDtypeStruct((WIDTH, ATT), F32),
            jax.ShapeDtypeStruct((ATT, 128), F32),
            jax.ShapeDtypeStruct((KER, WIDTH), F32),
        ],
        scratch_shapes=[
            pltpu.VMEM((SEQ + 16, WIDTH), F32),
            pltpu.VMEM((SEQ + 16, ATT), F32),
            pltpu.VMEM((SEQ + 16, ATT), F32),
            pltpu.VMEM((SEQ + 16, 128), F32),
            pltpu.VMEM((SEQ + 16, WIDTH), F32),
            pltpu.VMEM((WIDTH, ATT), F32),
            pltpu.VMEM((ATT, 128), F32),
            pltpu.VMEM((KER, 8, WIDTH), F32),
        ],
        compiler_params=params(1),
        cost_estimate=cost(25e9, 30e6),
        name="conv_back",
    )(dctx, kern, proj, proj, ck, spread, inputs, d_first_in, w_depth, w_point, w_kern)


def attend_back_kernel(
    q_ref, k_ref, v_ref, p_ref, o_ref, inv_ref, datt_ref, dqc_ref, dq_ref, dk_ref, dv_ref
):
    scale = HEAD**-0.5
    v = v_ref[...]
    d_att = datt_ref[...].astype(F32) * inv_ref[...]
    o = o_ref[...].astype(F32)
    q_all = q_ref[...].astype(F32) * scale
    k_all = k_ref[...].astype(F32) * scale
    dq, dk_t, dv_t = dqc_ref[...], 0.0, 0.0
    for head in (0, 1):
        mine = own_lanes(SEQ, head)
        da = jnp.where(mine, d_att, 0.0)
        dot_rows = jnp.sum(da * o, -1, keepdims=True)
        p = p_ref[0, head]
        ds = mm_nt(da.astype(BF), v)
        ds = (p.astype(F32) * (ds - dot_rows)).astype(BF)
        dq = dq + mm(ds, jnp.where(mine, k_all, 0.0).astype(BF))
        dk_t = dk_t + mm(jnp.where(mine, q_all, 0.0).T.astype(BF), ds)
        dv_t = dv_t + mm(da.T.astype(BF), p)
    dq_ref[...] = dq.astype(BF)
    dk_ref[...] = dk_t.T.astype(BF)
    dv_ref[...] = dv_t.T.astype(BF)


def attend_back(proj, probs, att, inv, dctx, dq_conv):
    rows = proj.shape[0]
    pairs = HEADS // 2
    col = lambda base: pl.BlockSpec((SEQ, 128), lambda s, p: (s, base + p))
    return pl.pallas_call(
        attend_back_kernel,
        grid=(rows // SEQ, pairs),
        in_specs=[
            col(0), col(pairs), col(2 * pairs),
            pl.BlockSpec((1, 2, SEQ, SEQ), lambda s, p: (s, p, 0, 0)),
            col(0), col(0), col(0), col(0),
        ],
        out_specs=[col(0)] * 3,
        out_shape=[jax.ShapeDtypeStruct((rows, ATT), BF)] * 3,
        compiler_params=params(2),
        cost_estimate=cost(30e9, 40e6),
        name="attend_back",
    )(proj, proj, proj, probs, att, inv, dctx, dq_conv)


WB = 512


def weight_kernel(core_ref, inp_ref, dq_ref, dk_ref, dv_ref, dcv_ref, point_ref, extra_ref, *refs):
    grad_refs, acc = refs[:-1], refs[-1]
    step = pl.program_id(0)
    last = pl.num_programs(0) - 1
    inp = inp_ref[...]

    @pl.when(step == 0)
    def _():
        acc[...] = jnp.zeros_like(acc)

    for n, ref in enumerate((dq_ref, dk_ref, dv_ref, dcv_ref)):
        acc[:, n * ATT : (n + 1) * ATT] += mm_tn(inp, ref[...])

    @pl.when(step == last)
    def _():
        for c, grad in enumerate(grad_refs):

            def emit(i, carry):
                owner = i
                if len(grad_refs) == 2:
                    owner = (i // 8) * 16 + (core_ref[0] ^ c) * 8 + i % 8
                rows = pl.ds(pl.multiple_of(owner * 24, 8), 24)
                o = acc[rows, :]
                cols = [o[:, n * ATT : (n + 1) * ATT] for n in range(4)]
                grad[i] = jnp.concatenate(cols + [point_ref[rows, :], extra_ref[owner]], 0).astype(BF)
                return carry

            lax.fori_loop(0, grad.shape[0], emit, 0)


def weight_grad(inputs, dq, dk, dv, dcv, d_point, extra, core=None):
    rows = inputs.shape[0]
    block = lambda n: pl.BlockSpec((WB, n), lambda s: (s, 0))
    shapes = [(32, 128, LANES)] if core is None else [(16, 128, LANES)] * 2
    core = jnp.zeros((1,), jnp.int32) if core is None else core
    return pl.pallas_call(
        weight_kernel,
        grid=(rows // WB,),
        in_specs=[pl.BlockSpec(memory_space=pltpu.SMEM), block(WIDTH)]
        + [block(ATT)] * 4
        + [whole(d_point.shape), whole(extra.shape)],
        out_specs=[whole_out(s) for s in shapes],
        out_shape=[jax.ShapeDtypeStruct(s, BF) for s in shapes],
        scratch_shapes=[pltpu.VMEM((WIDTH, 4 * ATT), F32)],
        compiler_params=params(1),
        cost_estimate=cost(12e9, 12e6),
        name="weight_grad",
    )(core, inputs, dq, dk, dv, dcv, d_point, extra)


LC = 512
STEPS = SEQ // LC


def leave_kernel(
    dq_ref, dk_ref, dv_ref, dcv_ref, rest_ref, mask_ref, to_ref, w_in_ref, out_ref, moved, kept
):
    step = pl.program_id(1)
    rows = pl.ds(pl.multiple_of((step % STEPS) * LC, LC), LC)

    @pl.when(step < STEPS)
    def _():
        d_proj = jnp.concatenate([dq_ref[...], dk_ref[...], dv_ref[...], dcv_ref[...]], 1)
        total = mm_nt(d_proj, w_in_ref[...]) + rest_ref[...]
        moved[rows, :] = total.astype(BF)
        kept[rows, :] = jnp.where(mask_ref[...] == 1, 0.0, total)

    @pl.when(step >= STEPS)
    def _():
        target = lax.broadcasted_iota(jnp.int32, (LC, SEQ), 0) + (step - STEPS) * LC
        hot = (target == to_ref[0]).astype(F32).astype(BF)
        out_ref[...] = kept[rows, :] + mm(hot, moved[...])


def leave(dq, dk, dv, dcv, d_rest, mask_col, to_row, w_in):
    rows = dq.shape[0]
    block = lambda n: pl.BlockSpec((LC, n), lambda s, i: (s * STEPS + jnp.minimum(i, STEPS - 1), 0))
    return pl.pallas_call(
        leave_kernel,
        grid=(rows // SEQ, 2 * STEPS),
        in_specs=[block(ATT)] * 4
        + [block(WIDTH), block(1), pl.BlockSpec((1, 1, SEQ), lambda s, i: (s, 0, 0)), whole((WIDTH, 4 * ATT))],
        out_specs=pl.BlockSpec((LC, WIDTH), lambda s, i: (s * STEPS + jnp.maximum(i - STEPS, 0), 0)),
        out_shape=jax.ShapeDtypeStruct((rows, WIDTH), F32),
        scratch_shapes=[pltpu.VMEM((SEQ, WIDTH), BF), pltpu.VMEM((SEQ, WIDTH), F32)],
        compiler_params=params(2),
        cost_estimate=cost(15e9, 30e6),
        name="leave",
    )(dq, dk, dv, dcv, d_rest, mask_col, to_row, w_in)


def pack_taps(kernel_full):
    by_tap = kernel_full.reshape(ATT, HEADS, KER).transpose(0, 2, 1)
    return jnp.pad(by_tap, ((0, 0), (0, 16 - KER), (0, 8 - HEADS))).reshape(ATT, 128)


def unpack_taps(packed):
    return packed.reshape(ATT, 16, 8)[:, :KER, :HEADS].transpose(0, 2, 1).reshape(ATT, HEADS * KER)


def per_device(
    tokens,
    masked,
    replace_ids,
    in_weight,
    depth_weight,
    point_weight,
    kernel_weight,
    out_weight,
    gain_one,
    shift_one,
    ffn_in,
    feedforward_output,
    gain_two,
    shift_two,
    cotangent,
):
    rows = tokens.shape[0]
    seqs = rows // SEQ
    dp, fsdp = lax.axis_size("dp"), lax.axis_size("fsdp")
    devices = dp * fsdp
    near = dp == NEAR["dp"] and fsdp == NEAR["fsdp"]
    own, hid = in_weight.shape[0], ffn_in.shape[2]
    n_depth, n_kern, n_vec = KER * own, kernel_weight.size, 4 * own
    hit = masked == 1
    here = jnp.arange(rows, dtype=jnp.int32) % SEQ
    pick = jnp.where(hit, replace_ids, here)[:, None]
    to_row = jnp.where(hit, replace_ids, -1).reshape(seqs, 1, SEQ)
    scale = 1.0 / math.sqrt(rows * devices)

    vec_own = jnp.stack([gain_one, shift_one, gain_two, shift_two])
    small_own = as_rows(
        jnp.concatenate([depth_weight.reshape(-1), kernel_weight.reshape(-1), vec_own.reshape(-1)])
    )
    head_own = jnp.concatenate([in_weight.reshape(own, 4, ATT).transpose(1, 0, 2), point_weight[None]])
    mid_own = jnp.concatenate(
        [
            out_weight.reshape(own, 2, ATT).transpose(1, 0, 2).reshape(-1, LANES),
            ffn_in.transpose(0, 2, 1).reshape(-1, LANES),
            feedforward_output.reshape(-1, LANES),
        ]
    )
    if near:
        me = place().astype(jnp.int32).reshape(1)
        pair, core = me // 2, me // CORE_BIT % 2
        slab, pick = tie(pair_slab(head_own, small_own), pick)
        slabs = [slab] + [hop(slab, k * Z_BIT) for k in (1, 2, 3)]
        across = [hop(slab, X_BIT)]
        inputs, (across, slabs[1:]) = tie(pick_rows(pick, tokens), (across, slabs[1:]))
        slabs[1:], mid_own = tie(slabs[1:], mid_own)
        mid = lax.all_gather(mid_own, AXES, axis=0)
        slabs = slabs + across + [hop(slab, X_BIT) for slab in slabs[1:]]
        slabs = slabs + [hop(slab, CORE_BIT) for slab in slabs]
        small_all = small_rows(slabs, pair)
    else:
        small_all = lax.all_gather(small_own, AXES, axis=0).reshape(devices, -1)
        w_all = lax.all_gather(head_own, AXES, axis=1, tiled=True).reshape(5, 16, 48, LANES)
        slabs = [w_all[:, bits].reshape(-1, LANES) for bits in SLAB_BITS]
        mid = lax.all_gather(mid_own, AXES, axis=0)
        w_out = mid[:, : 2 * own].reshape(devices, 2, own, ATT).transpose(1, 0, 2, 3)
        w_out = w_out.reshape(2, BLOCKS, 24, ATT).transpose(1, 0, 2, 3).reshape(BLOCKS, 48, ATT)
        w_ffn = mid[:, 2 * own :].reshape(devices, 4, hid, ATT).transpose(1, 0, 2, 3)
        w_ffn = w_ffn.reshape(4, BLOCKS, 48, ATT).transpose(1, 0, 2, 3).reshape(BLOCKS, 192, ATT)
        mid = jnp.concatenate([w_out, w_ffn], 1)
        pair, core = jnp.zeros((1,), jnp.int32), None
        inputs = pick_rows(pick, tokens)
    w_depth = small_all[:, :n_depth].reshape(devices, KER, own).transpose(1, 0, 2).reshape(KER, WIDTH)
    w_depth = w_depth.astype(F32)
    w_kern = pack_taps(small_all[:fsdp, n_depth : n_depth + n_kern].reshape(ATT, HEADS * KER))
    vecs = small_all[:, n_depth + n_kern :][:, :n_vec].reshape(devices, 4, own)
    vecs = vecs.transpose(1, 0, 2).reshape(4, WIDTH).astype(F32)

    proj, spread, ck, kern, conv, w_in, w_point = enter(inputs, pair, w_depth, w_kern, slabs)
    probs, att, inv = attend(proj)
    out, dctx, d_first_in, d_vecs, mid_grad = middle(att, conv, inputs, cotangent, mid, vecs)
    if near:
        mid_sum = lax.psum_scatter(mid_grad, AXES, scatter_dimension=0, tiled=True)[0]
    dq_conv, dcv, d_rest, d_point, d_kern, d_depth = conv_back(
        dctx, kern, proj, ck, spread, inputs, d_first_in, w_depth, w_point, w_kern
    )
    by_owner = lambda g: g.reshape(-1, devices, own).transpose(1, 0, 2).reshape(devices, -1)
    kern_by = jnp.tile(unpack_taps(d_kern).reshape(fsdp, -1), (dp, 1))
    small_grad = jnp.concatenate([by_owner(d_depth), kern_by, by_owner(d_vecs)], 1)
    small_grad = jnp.pad(small_grad, ((0, 0), (0, -small_grad.shape[1] % LANES)))
    small_grad = small_grad.reshape(devices, -1, LANES)
    dq, dk, dv = attend_back(proj, probs, att, inv, dctx, dq_conv)
    mask_col = masked[:, None]
    if near:
        mine, other = weight_grad(inputs, dq, dk, dv, dcv, d_point, small_grad, core)
        parts = fold_xy(me, mine, hop(other, CORE_BIT))
        parts = [parts[0]] + [hop(part, bit) for part, bit in zip(parts[1:], (Y_BIT, X_BIT, X_BIT + Y_BIT))]
        parts[0], dq = tie(parts[0], dq)
        d_tokens = leave(dq, dk, dv, dcv, d_rest, mask_col, to_row, w_in)
        d_tokens, parts = tie(d_tokens, parts)
        parts = fold_z(me, parts)
        parts = [parts[0]] + [hop(parts[k], k * Z_BIT) for k in (1, 2, 3)]
        parts[0], mid_sum = tie(parts[0], mid_sum)
        d_out, d_up, d_down = finish_mid(scale, mid_sum)
        d_up = d_up.transpose(0, 2, 1)
        parts[3], d_out = tie(parts[3], d_out)
        small_shapes = [(KER, own), kernel_weight.shape, (4, own)]
        d_in, d_point, depth_sum, kern_sum, vec_sum = finish(scale, parts, small_shapes)
    else:
        (grads,) = weight_grad(inputs, dq, dk, dv, dcv, d_point, jnp.zeros((32, 8, LANES), F32))
        d_in = grads[:, :96].reshape(32, 4, 24, ATT).transpose(0, 2, 1, 3).reshape(devices, -1, LANES)
        d_point = grads[:, 96:120].reshape(devices, -1, LANES)
        w_out = mid_grad[:, :48].reshape(BLOCKS, 2, 24, ATT).transpose(0, 2, 1, 3).reshape(devices, -1, LANES)
        w_ffn = mid_grad[:, 48:].reshape(BLOCKS, 4, 48, ATT).transpose(1, 0, 2, 3)
        w_ffn = w_ffn.reshape(4, devices, hid, ATT).transpose(1, 0, 2, 3).reshape(devices, -1, LANES)
        packed = jnp.concatenate([w_out, w_ffn, d_in, d_point, small_grad.astype(BF)], 1)
        total = lax.psum_scatter(packed, AXES, scatter_dimension=0, tiled=True)[0].astype(F32) * scale
        cuts = [2 * own, 2 * own + 2 * hid, 2 * own + 4 * hid, 6 * own + 4 * hid, 7 * own + 4 * hid]
        d_out, d_up, d_down, d_in, d_point, small_sum = jnp.split(total, cuts)
        d_out, d_in, small_sum = d_out.reshape(own, WIDTH), d_in.reshape(own, 4 * ATT), small_sum.reshape(-1)
        d_up, d_down = d_up.reshape(2, hid, ATT).transpose(0, 2, 1), d_down.reshape(2, hid, ATT)
        d_tokens = leave(dq, dk, dv, dcv, d_rest, mask_col, to_row, w_in)
        depth_sum = small_sum[:n_depth].reshape(KER, own)
        kern_sum = small_sum[n_depth : n_depth + n_kern].reshape(kernel_weight.shape)
        vec_sum = small_sum[n_depth + n_kern :][:n_vec].reshape(4, own)
    return (
        out,
        d_tokens,
        d_in,
        depth_sum,
        d_point,
        kern_sum,
        d_out,
        vec_sum[0],
        vec_sum[1],
        d_up,
        d_down,
        vec_sum[2],
        vec_sum[3],
    )


def solution(mesh):
    return jax.shard_map(
        per_device,
        mesh=mesh,
        in_specs=(
            P(("dp", "fsdp"), None),
            P(("dp", "fsdp")),
            P(("dp", "fsdp")),
            P(("dp", "fsdp"), None),
            P(None, ("dp", "fsdp")),
            P(("dp", "fsdp"), None),
            P("fsdp", None),
            P(("dp", "fsdp"), None),
            P(("dp", "fsdp")),
            P(("dp", "fsdp")),
            P(None, None, ("dp", "fsdp")),
            P(None, ("dp", "fsdp"), None),
            P(("dp", "fsdp")),
            P(("dp", "fsdp")),
            P(("dp", "fsdp"), None),
        ),
        out_specs=(
            P(("dp", "fsdp"), None),
            P(("dp", "fsdp"), None),
            P(("dp", "fsdp"), None),
            P(None, ("dp", "fsdp")),
            P(("dp", "fsdp"), None),
            P("fsdp", None),
            P(("dp", "fsdp"), None),
            P(("dp", "fsdp")),
            P(("dp", "fsdp")),
            P(None, None, ("dp", "fsdp")),
            P(None, ("dp", "fsdp"), None),
            P(("dp", "fsdp")),
            P(("dp", "fsdp")),
        ),
        check_vma=False,
    )
```

```python
from functools import partial
import math

import jax
import jax.numpy as jnp
from jax import lax
from jax.experimental import pallas as pl
from jax.experimental.pallas import tpu as pltpu
from jax.sharding import PartitionSpec as P

BF = jnp.bfloat16
F32 = jnp.float32
HEADS = 6
HEAD = 64
SEQ = 1024
KER = 9
ATT = HEADS * HEAD
WIDTH = 768
VMEM_MAX = 60 * 1024 * 1024


def mm(a, b):
    return jnp.dot(a, b, preferred_element_type=F32)


def mm_nt(a, b):
    return lax.dot_general(a, b, (((1,), (1,)), ((), ())), preferred_element_type=F32)


def mm_tn(a, b):
    return lax.dot_general(a, b, (((0,), (0,)), ((), ())), preferred_element_type=F32)


def params(count):
    return pltpu.CompilerParams(
        dimension_semantics=("arbitrary",) * count, vmem_limit_bytes=VMEM_MAX
    )


def cost(flops, moved):
    return pl.CostEstimate(flops=int(flops), bytes_accessed=int(moved), transcendentals=0)


def whole(shape):
    zeros = (0,) * len(shape)
    return pl.BlockSpec(shape, lambda *_: zeros, pipeline_mode=pl.Buffered(1))


def whole_out(shape):
    zeros = (0,) * len(shape)
    return pl.BlockSpec(shape, lambda *_: zeros)


AXES = ("dp", "fsdp")
LANES = 384
NEAR = {"dp": 4, "fsdp": 8}
X_BIT, CORE_BIT, Z_BIT, Y_BIT = 16, 8, 2, 1


def as_rows(x):
    flat = x.reshape(-1)
    return jnp.pad(flat, (0, -flat.size % LANES)).reshape(-1, LANES)


def place():
    return lax.axis_index("dp") * NEAR["fsdp"] + lax.axis_index("fsdp")


def hop(x, mask):
    return lax.ppermute(x, AXES, [(i, i ^ mask) for i in range(32)])


def tie(first, second):
    return lax.optimization_barrier((first, second))


def fold_xy_kernel(me_ref, mine_ref, other_ref, *outs):
    x, y = me_ref[0] // X_BIT, me_ref[0] % 2
    for k, out in enumerate(outs):
        at = (x ^ (k // 2), 0, y ^ (k % 2))
        out[0] = (mine_ref[at].astype(F32) + other_ref[at].astype(F32)).astype(BF)


def fold_xy(me, mine, other):
    rows = mine.shape[-2]
    views = [a.reshape(2, 4, 2, rows, LANES) for a in (mine, other)]
    return pl.pallas_call(
        fold_xy_kernel,
        grid=(4,),
        in_specs=[pl.BlockSpec(memory_space=pltpu.SMEM)]
        + [pl.BlockSpec((2, 1, 2, rows, LANES), lambda z: (0, z, 0, 0, 0))] * 2,
        out_specs=[pl.BlockSpec((1, rows, LANES), lambda z: (z, 0, 0))] * 4,
        out_shape=[jax.ShapeDtypeStruct((4, rows, LANES), BF)] * 4,
        compiler_params=params(1),
        cost_estimate=cost(0, 6 * mine.size),
        name="fold_xy",
    )(me, *views)


def fold_z_kernel(me_ref, *refs):
    z = (me_ref[0] // Z_BIT) % 4
    for k, out in enumerate(refs[4:]):
        total = refs[0][z ^ k].astype(F32)
        for ref in refs[1:4]:
            total = total + ref[z ^ k].astype(F32)
        out[...] = total.astype(BF)


def fold_z(me, arrays):
    rows = arrays[0].shape[-2]
    return pl.pallas_call(
        fold_z_kernel,
        in_specs=[pl.BlockSpec(memory_space=pltpu.SMEM)] + [pl.BlockSpec(memory_space=pltpu.VMEM)] * 4,
        out_specs=[pl.BlockSpec(memory_space=pltpu.VMEM)] * 4,
        out_shape=[jax.ShapeDtypeStruct((rows, LANES), BF)] * 4,
        compiler_params=pltpu.CompilerParams(vmem_limit_bytes=16 * 1024 * 1024),
        cost_estimate=cost(0, 10 * arrays[0].size),
        name="fold_z",
    )(me, *arrays)


def finish_kernel(scale, a_ref, b_ref, c_ref, d_ref, in_ref, point_ref, depth_ref, kern_ref, vec_ref):
    total = sum(ref[...].astype(F32) for ref in (a_ref, b_ref, c_ref, d_ref)) * scale
    for n in range(4):
        in_ref[:, n * ATT : (n + 1) * ATT] = total[24 * n : 24 * n + 24]
    point_ref[...] = total[96:120]
    at = 0
    for ref in (depth_ref, kern_ref, vec_ref):
        count, width = ref.shape
        for i in range(count):
            row, lane = 120 + at // LANES, at % LANES
            here = min(width, LANES - lane)
            ref[i : i + 1, :here] = total[row : row + 1, lane : lane + here]
            if here < width:
                ref[i : i + 1, here:] = total[row + 1 : row + 2, : width - here]
            at += width


def finish(scale, arrays, small_shapes):
    vmem = pl.BlockSpec(memory_space=pltpu.VMEM)
    return pl.pallas_call(
        partial(finish_kernel, scale),
        in_specs=[vmem] * 4,
        out_specs=[vmem] * 5,
        out_shape=[
            jax.ShapeDtypeStruct((24, 4 * ATT), F32),
            jax.ShapeDtypeStruct((24, ATT), F32),
        ]
        + [jax.ShapeDtypeStruct(shape, F32) for shape in small_shapes],
        name="finish",
    )(*arrays)


def finish_mid_kernel(scale, sum_ref, out_ref, up_ref, down_ref):
    total = sum_ref[...].astype(F32) * scale
    out_ref[:, :ATT] = total[:24]
    out_ref[:, ATT:] = total[24:48]
    for g in (0, 1):
        up_ref[g] = total[48 + 48 * g : 96 + 48 * g]
        down_ref[g] = total[144 + 48 * g : 192 + 48 * g]


def finish_mid(scale, packed):
    vmem = pl.BlockSpec(memory_space=pltpu.VMEM)
    return pl.pallas_call(
        partial(finish_mid_kernel, scale),
        in_specs=[vmem],
        out_specs=[vmem] * 3,
        out_shape=[
            jax.ShapeDtypeStruct((24, WIDTH), F32),
            jax.ShapeDtypeStruct((2, 48, ATT), F32),
            jax.ShapeDtypeStruct((2, 48, ATT), F32),
        ],
        name="finish_mid",
    )(packed)


SLAB_BITS = [((s // 4) % 2 * X_BIT + (s // 8) * CORE_BIT + s % 4 * Z_BIT) // 2 for s in range(16)]


def pair_slab(own, small):
    packed = jnp.concatenate([own.reshape(-1, LANES), small])
    other = hop(packed, Y_BIT)
    even = place() % 2 == 0
    first, second = jnp.where(even, packed, other), jnp.where(even, other, packed)
    both = [x[:120].reshape(5, 24, LANES) for x in (first, second)]
    return jnp.concatenate([jnp.concatenate(both, 1).reshape(-1, LANES), first[120:], second[120:]])


def small_rows(slabs, pair):
    spot = jnp.array([SLAB_BITS.index(b) for b in range(16)], jnp.int32)
    order = jnp.take(spot, jnp.arange(16, dtype=jnp.int32) ^ pair)
    return jnp.take(jnp.stack([slab[240:] for slab in slabs]), order, axis=0).reshape(32, -1)


def lane_groups(x, combine):
    for step in (64, 32, 16, 8):
        x = combine(x, pltpu.roll(x, step, 1))
    return x


def tap_spread(block):
    rows = lax.broadcasted_iota(jnp.int32, (128, KER * 128), 0)
    cols = lax.broadcasted_iota(jnp.int32, (128, KER * 128), 1)
    want = (cols // 128) * 8 + block * 2 + (cols % 128) // HEAD
    return (rows == want).astype(F32).astype(BF)


EC = 1024
FB = 512
BB = 1024
DB = 512


def pick_kernel(pick_ref, tok_ref, inp_ref):
    cols = lax.broadcasted_iota(jnp.int32, (SEQ, SEQ), 1)
    hot = (cols == pick_ref[...]).astype(F32).astype(BF)
    inp_ref[...] = mm(hot, tok_ref[...]).astype(BF)


def pick_rows(pick, tokens):
    block = lambda n: pl.BlockSpec((SEQ, n), lambda s: (s, 0))
    return pl.pallas_call(
        pick_kernel,
        grid=(tokens.shape[0] // SEQ,),
        in_specs=[block(1), block(WIDTH)],
        out_specs=block(WIDTH),
        out_shape=jax.ShapeDtypeStruct(tokens.shape, BF),
        compiler_params=params(1),
        cost_estimate=cost(6e9, 6e6),
        name="pick",
    )(pick, tokens)


def enter_kernel(
    inp_ref, w_in_ref, w_depth_ref, w_point_ref, w_kern_ref,
    proj_ref, spread_ref, ck_ref, kern_ref, conv_ref,
    x_pad, cv_pad,
):
    x_pad[0:8, :] = jnp.zeros((8, WIDTH), F32)
    x_pad[SEQ + 8 : SEQ + 16, :] = jnp.zeros((8, WIDTH), F32)
    cv_pad[0:8, :] = jnp.zeros((8, ATT), F32)
    cv_pad[SEQ + 8 : SEQ + 16, :] = jnp.zeros((8, ATT), F32)

    def load(i, carry):
        r = pl.multiple_of(i * EC, EC)
        low = inp_ref[pl.ds(r, EC), :]
        x_pad[pl.ds(r + 8, EC), :] = low.astype(F32)
        proj = mm(low, w_in_ref[...])
        proj_low = proj.astype(BF)
        proj_ref[pl.ds(r, EC), :] = proj_low
        cv_pad[pl.ds(r + 8, EC), :] = proj_low[:, 3 * ATT :].astype(F32)
        return carry

    lax.fori_loop(0, SEQ // EC, load, 0)

    def conv(i, carry):
        r = pl.multiple_of(i * EC, EC)
        for b in range(WIDTH // 128):
            lanes = slice(b * 128, (b + 1) * 128)
            xs = x_pad[pl.ds(r, (EC + 16)), lanes]
            shifted = [xs] + [pltpu.roll(xs, (EC + 16) - s, 0) for s in (1, 2, 3)]
            tap = lambda j: w_depth_ref[j : j + 1, lanes]
            low_part = sum(tap(s) * shifted[s] for s in range(4))
            mid_part = sum(tap(4 + s) * shifted[s] for s in range(4))
            high_part = tap(8) * xs
            low_part = pltpu.roll(low_part, (EC + 16) - 4, 0)
            high_part = pltpu.roll(high_part, (EC + 16) - 4, 0)
            total = low_part[0:EC] + mid_part[8 : 8 + EC] + high_part[8 : 8 + EC]
            spread_ref[pl.ds(r, EC), lanes] = total.astype(BF)
        ck = mm(spread_ref[pl.ds(r, EC), :], w_point_ref[...]).astype(BF)
        ck_ref[pl.ds(r, EC), :] = ck
        q = proj_ref[pl.ds(r, EC), 0:ATT].astype(F32)
        mixed = (ck.astype(F32) * q).astype(BF)
        logits = mm(mixed, w_kern_ref[...])
        lane = lax.broadcasted_iota(jnp.int32, (EC, 128), 1)
        logits = jnp.where(lane < KER * 8, logits, -1e30)
        top = lane_groups(logits, jnp.maximum)
        e = jnp.exp(logits - top)
        kern = e / lane_groups(e, jnp.add)
        kern_ref[pl.ds(r, EC), :] = kern
        kern_low = kern.astype(BF)
        for b in range(ATT // 128):
            lanes = slice(b * 128, (b + 1) * 128)
            wide = mm(kern_low, tap_spread(b))
            cs = cv_pad[pl.ds(r, (EC + 16)), lanes]
            total = jnp.zeros((EC, 128), F32)
            for j in range(KER):
                moved = cs if j == 4 else pltpu.roll(cs, ((EC + 16) - (j - 4)) % (EC + 16), 0)
                total = total + wide[:, j * 128 : (j + 1) * 128] * moved[8 : 8 + EC]
            conv_ref[pl.ds(r, EC), lanes] = total.astype(BF)
        return carry

    lax.fori_loop(0, SEQ // EC, conv, 0)


def enter_slabs_kernel(pair_ref, inp_ref, w_depth_ref, w_kern_ref, *refs):
    slabs, outs = refs[:16], refs[16:]
    results, w_in_ref, w_point_ref, scratch, sems = outs[:5], outs[5], outs[6], outs[7:9], outs[9]

    @pl.when(pl.program_id(0) == 0)
    def _():
        copies = []
        for s, slab in enumerate(slabs):
            spot = pl.ds(pl.multiple_of((pair_ref[0] ^ SLAB_BITS[s]) * 48, 16), 48)
            for b in range(5):
                to = w_in_ref.at[spot, b * ATT : (b + 1) * ATT] if b < 4 else w_point_ref.at[spot, :]
                copies.append(pltpu.make_async_copy(slab.at[b * 48 : (b + 1) * 48, :], to, sems.at[s, b]))
        for copy in copies:
            copy.start()
        for copy in copies:
            copy.wait()

    enter_kernel(inp_ref, w_in_ref, w_depth_ref, w_point_ref, w_kern_ref, *results, *scratch)


def enter(inputs, pair, w_depth, w_kern, slabs):
    rows = inputs.shape[0]
    block = lambda n: pl.BlockSpec((SEQ, n), lambda s: (s, 0))
    widths = ((4 * ATT, BF), (WIDTH, BF), (ATT, BF), (128, F32), (ATT, BF))
    return pl.pallas_call(
        enter_slabs_kernel,
        grid=(rows // SEQ,),
        in_specs=[
            pl.BlockSpec(memory_space=pltpu.SMEM), block(WIDTH), whole((KER, WIDTH)), whole((ATT, 128)),
        ]
        + [pl.BlockSpec(memory_space=pl.ANY)] * 16,
        out_specs=[block(n) for n, _ in widths] + [whole_out((WIDTH, 4 * ATT)), whole_out((WIDTH, ATT))],
        out_shape=[jax.ShapeDtypeStruct((rows, n), t) for n, t in widths]
        + [jax.ShapeDtypeStruct((WIDTH, 4 * ATT), BF), jax.ShapeDtypeStruct((WIDTH, ATT), BF)],
        scratch_shapes=[
            pltpu.VMEM((SEQ + 16, WIDTH), F32),
            pltpu.VMEM((SEQ + 16, ATT), F32),
            pltpu.SemaphoreType.DMA((16, 5)),
        ],
        compiler_params=params(1),
        cost_estimate=cost(20e9, 20e6),
        name="enter",
    )(pair, inputs, w_depth, w_kern, *slabs)


def own_lanes(rows, head):
    lane = lax.broadcasted_iota(jnp.int32, (rows, 128), 1)
    return (lane // HEAD) == head


AC = 512


def attend_kernel(q_ref, k_ref, v_ref, p_ref, o_ref, inv_ref):
    k = k_ref[...]
    v_all = v_ref[...].astype(F32)
    vs = [jnp.where(own_lanes(SEQ, head), v_all, 1.0).astype(BF) for head in (0, 1)]
    first = own_lanes(AC, 0)

    def part(i, carry):
        rows = pl.ds(pl.multiple_of(i * AC, AC), AC)
        q_all = q_ref[rows, :].astype(F32) * (HEAD**-0.5)
        outs = []
        for head in (0, 1):
            q = jnp.where(first if head == 0 else ~first, q_all, 0.0).astype(BF)
            s = mm_nt(q, k)
            p = jnp.exp(s - jnp.max(s, -1, keepdims=True)).astype(BF)
            p_ref[0, head, rows, :] = p
            outs.append(mm(p, vs[head]))
        inv = 1.0 / pltpu.roll(jnp.where(first, outs[1], outs[0]), HEAD, 1)
        o_ref[rows, :] = (jnp.where(first, outs[0], outs[1]) * inv).astype(BF)
        inv_ref[rows, :] = inv
        return carry

    lax.fori_loop(0, SEQ // AC, part, 0, unroll=2)


def attend(proj):
    rows = proj.shape[0]
    pairs = HEADS // 2
    col = lambda base: pl.BlockSpec((SEQ, 128), lambda s, p: (s, base + p))
    return pl.pallas_call(
        attend_kernel,
        grid=(rows // SEQ, pairs),
        in_specs=[col(0), col(pairs), col(2 * pairs)],
        out_specs=[pl.BlockSpec((1, 2, SEQ, SEQ), lambda s, p: (s, p, 0, 0)), col(0), col(0)],
        out_shape=[
            jax.ShapeDtypeStruct((rows // SEQ, HEADS, SEQ, SEQ), BF),
            jax.ShapeDtypeStruct((rows, ATT), BF),
            jax.ShapeDtypeStruct((rows, ATT), F32),
        ],
        compiler_params=params(2),
        cost_estimate=cost(25e9, 35e6),
        name="attend",
    )(proj, proj, proj)


ERF_P = 0.3275911 / math.sqrt(2.0)
ERF_A = (0.254829592, -0.284496736, 1.421413741, -1.453152027, 1.061405429)
PHI = 1.0 / math.sqrt(2.0 * math.pi)


def gelu_both(u):
    t = 1.0 / (1.0 + ERF_P * jnp.abs(u))
    poly = 0.5 * ERF_A[4]
    for a in ERF_A[3::-1]:
        poly = poly * t + 0.5 * a
    e = jnp.exp2((-0.5 * math.log2(math.e)) * (u * u))
    tail = t * poly * e
    cdf = jnp.where(u > 0, 1.0 - tail, tail)
    return u * cdf, cdf + (PHI * u) * e


def norm_parts(z):
    mean = jnp.mean(z, -1, keepdims=True)
    centred = z - mean
    var = jnp.mean(centred * centred, -1, keepdims=True)
    r = lax.rsqrt(var + 1e-12)
    return centred * r, r


def norm_back(c, xh, r, gain):
    gc = c * gain
    return r * (gc - jnp.mean(gc, -1, keepdims=True) - xh * jnp.mean(gc * xh, -1, keepdims=True))


def fold_rows(x):
    return jnp.sum(x.reshape(-1, 8, x.shape[-1]), 0)


MID = 256
FF = 1536
FC = 768
GROUP = 48
BLOCKS = FF // GROUP


def middle_kernel(
    att_ref, conv_ref, inp_ref, cot_ref, mid_ref, vec_ref,
    out_ref, dctx_ref, dfirst_ref, dvec_ref, packed_ref,
    acc_out, acc_up, acc_down, acc_vec, act_ref, slope_ref, flip_ref,
    w_out_ref, w_rows, w_up_blocks, w_down_blocks, sems,
):
    step = pl.program_id(0)
    last = pl.num_programs(0) - 1

    @pl.when(step == 0)
    def _():
        targets = [w_rows] + [w.at[g] for w in (w_up_blocks, w_down_blocks) for g in (0, 1)]
        copies = [
            pltpu.make_async_copy(mid_ref.at[:, n * GROUP : (n + 1) * GROUP, :], to, sems.at[n])
            for n, to in enumerate(targets)
        ]
        for copy in copies:
            copy.start()
        acc_up[...] = jnp.zeros_like(acc_up)
        acc_down[...] = jnp.zeros_like(acc_down)
        acc_vec[...] = jnp.zeros_like(acc_vec)
        copies[0].wait()
        half = GROUP // 2

        def unfold(i, carry):
            both = w_rows[i].astype(F32)
            rows = pl.ds(pl.multiple_of(i * half, 8), half)
            acc_out[rows, :] = jnp.concatenate([both[:half], both[half:]], 1)
            return carry

        lax.fori_loop(0, BLOCKS, unfold, 0)
        w_out_ref[...] = acc_out[...].astype(BF)
        acc_out[...] = jnp.zeros_like(acc_out)
        for copy in copies[1:]:
            copy.wait()

    def w_up(g, f):
        return w_up_blocks[g, f * FC // GROUP : (f + 1) * FC // GROUP].reshape(FC, ATT)

    def w_down(g, f):
        return w_down_blocks[g, f * FC // GROUP : (f + 1) * FC // GROUP].reshape(FC, ATT)

    ctx = jnp.concatenate([att_ref[...], conv_ref[...]], -1)
    g_one, s_one = vec_ref[0:1, :], vec_ref[1:2, :]
    g_two, s_two = vec_ref[2:3, :], vec_ref[3:4, :]
    first_in = mm(ctx, w_out_ref[...]) + inp_ref[...].astype(F32)
    xh_one, r_one = norm_parts(first_in)
    first = xh_one * g_one + s_one
    first_low = first.astype(BF)
    outs = []
    for g in (0, 1):
        cols = slice(g * ATT, (g + 1) * ATT)
        total = None
        for f in range(FF // FC):
            hid = slice(f * FC, (f + 1) * FC)
            inner = mm_nt(first_low[:, cols], w_up(g, f))
            act, slope = gelu_both(inner)
            act = act.astype(BF)
            act_ref[g, :, hid] = act
            slope_ref[g, :, hid] = slope.astype(slope_ref.dtype)
            part = mm(act, w_down(g, f))
            total = part if total is None else total + part
        outs.append(total)
    xh_two, r_two = norm_parts(jnp.concatenate(outs, -1) + first)
    out_ref[...] = (xh_two * g_two + s_two).astype(BF)
    c = cot_ref[...].astype(F32)
    acc_vec[2] += fold_rows(c * xh_two)
    acc_vec[3] += fold_rows(c)
    d_second = norm_back(c, xh_two, r_two, g_two)
    d_outer = d_second.astype(BF)
    d_outer_t = d_second.T.astype(BF)
    first_t = first.T.astype(BF)
    backs = []
    for g in (0, 1):
        cols = slice(g * ATT, (g + 1) * ATT)
        total = None
        for f in range(FF // FC):
            hid = slice(f * FC, (f + 1) * FC)
            d_act = mm_nt(d_outer[:, cols], w_down(g, f))
            d_inner = (d_act * slope_ref[g, :, hid].astype(F32)).astype(BF)
            acc_down[g, :, hid] += mm(d_outer_t[cols, :], act_ref[g, :, hid])
            acc_up[g, :, hid] += mm(first_t[cols, :], d_inner)
            part = mm(d_inner, w_up(g, f))
            total = part if total is None else total + part
        backs.append(total)
    d_first = jnp.concatenate(backs, -1) + d_second
    acc_vec[0] += fold_rows(d_first * xh_one)
    acc_vec[1] += fold_rows(d_first)
    d_first_in = norm_back(d_first, xh_one, r_one, g_one)
    dfirst_ref[...] = d_first_in
    d_dense = d_first_in.astype(BF)
    acc_out[...] += mm_tn(ctx, d_dense)
    dctx_ref[...] = mm_nt(d_dense, w_out_ref[...]).astype(BF)

    @pl.when(step == last)
    def _():
        dvec_ref[...] = jnp.sum(acc_vec[...], 1)
        for g in (0, 1):
            flip_ref[0, g] = acc_up[g].T.astype(BF)
            flip_ref[1, g] = acc_down[g].T.astype(BF)

        def emit(i, carry):
            o = acc_out[pl.ds(pl.multiple_of(i * 24, 8), 24), :]
            packed_ref[i, 0:48, :] = jnp.concatenate([o[:, :ATT], o[:, ATT:]], 0).astype(BF)
            hidden = pl.ds(pl.multiple_of(i * 48, 16), 48)
            for n in range(4):
                packed_ref[i, 48 * n + 48 : 48 * n + 96, :] = flip_ref[n // 2, n % 2, hidden, :]
            return carry

        lax.fori_loop(0, BLOCKS, emit, 0)


def middle(att, conv, inputs, cot, mid, vecs):
    rows = att.shape[0]
    block = lambda n: pl.BlockSpec((MID, n), lambda s: (s, 0))
    packed = (BLOCKS, 5 * GROUP, LANES)
    return pl.pallas_call(
        middle_kernel,
        grid=(rows // MID,),
        in_specs=[
            block(ATT), block(ATT), block(WIDTH), block(WIDTH),
            pl.BlockSpec(memory_space=pl.ANY), whole((4, WIDTH)),
        ],
        out_specs=[block(WIDTH), block(WIDTH), block(WIDTH), whole_out((4, WIDTH)), whole_out(packed)],
        out_shape=[
            jax.ShapeDtypeStruct((rows, WIDTH), BF),
            jax.ShapeDtypeStruct((rows, WIDTH), BF),
            jax.ShapeDtypeStruct((rows, WIDTH), F32),
            jax.ShapeDtypeStruct((4, WIDTH), F32),
            jax.ShapeDtypeStruct(packed, BF),
        ],
        scratch_shapes=[
            pltpu.VMEM((WIDTH, WIDTH), F32),
            pltpu.VMEM((2, ATT, FF), F32),
            pltpu.VMEM((2, ATT, FF), F32),
            pltpu.VMEM((4, 8, WIDTH), F32),
            pltpu.VMEM((2, MID, FF), BF),
            pltpu.VMEM((2, MID, FF), F32),
            pltpu.VMEM((2, 2, FF, ATT), BF),
            pltpu.VMEM((WIDTH, WIDTH), BF),
            pltpu.VMEM((BLOCKS, GROUP, LANES), BF),
            pltpu.VMEM((2, BLOCKS, GROUP, ATT), BF),
            pltpu.VMEM((2, BLOCKS, GROUP, ATT), BF),
            pltpu.SemaphoreType.DMA((5,)),
        ],
        compiler_params=params(1),
        cost_estimate=cost(60e9, 40e6),
        name="middle",
    )(att, conv, inputs, cot, mid, vecs)


def conv_back_kernel(
    dconv_ref, kern_ref, q_ref, cv_ref, ck_ref, spread_ref, inp_ref, first_ref, w_depth_ref, w_point_ref, w_kern_ref,
    dq_ref, dcv_ref, din_ref, dpoint_ref, dkern_ref, ddepth_ref,
    x_pad, cv_pad, dc_pad, kl_pad, ds_pad, acc_point, acc_kern, acc_depth,
):
    step = pl.program_id(0)
    last = pl.num_programs(0) - 1
    zero = lambda n: jnp.zeros((8, n), F32)
    for ref, n in ((x_pad, WIDTH), (cv_pad, ATT), (dc_pad, ATT), (kl_pad, 128), (ds_pad, WIDTH)):
        ref[0:8, :] = zero(n)
        ref[SEQ + 8 : SEQ + 16, :] = zero(n)

    @pl.when(step == 0)
    def _():
        acc_point[...] = jnp.zeros_like(acc_point)
        acc_kern[...] = jnp.zeros_like(acc_kern)
        acc_depth[...] = jnp.zeros_like(acc_depth)

    def fill(i, carry):
        r = pl.multiple_of(i * FB, FB)
        rows = pl.ds(r, FB)
        there = pl.ds(r + 8, FB)
        x_pad[there, :] = inp_ref[rows, :].astype(F32)
        cv_pad[there, :] = cv_ref[rows, :].astype(F32)
        dc_pad[there, :] = dconv_ref[rows, :].astype(F32)
        kl_pad[there, :] = kern_ref[rows, :]
        return carry

    lax.fori_loop(0, SEQ // FB, fill, 0)

    def back(i, carry):
        r = pl.multiple_of(i * BB, BB)
        rows = pl.ds(r, BB)
        d_kern = jnp.zeros((BB, 128), F32)
        kl = kl_pad[pl.ds(r, (BB + 16)), :].astype(BF)
        for b in range(ATT // 128):
            lanes = slice(b * 128, (b + 1) * 128)
            spreader = tap_spread(b)
            cs = cv_pad[pl.ds(r, (BB + 16)), lanes]
            dc = dc_pad[pl.ds(r + 8, BB), lanes]
            prods = []
            for j in range(KER):
                moved = cs if j == 4 else pltpu.roll(cs, ((BB + 16) - (j - 4)) % (BB + 16), 0)
                prods.append((dc * moved[8 : 8 + BB]).astype(BF))
            d_kern = d_kern + mm_nt(jnp.concatenate(prods, -1), spreader)
            wide = mm(kl, spreader)
            dch = dc_pad[pl.ds(r, (BB + 16)), lanes]
            total = jnp.zeros((BB, 128), F32)
            for j in range(KER):
                term = wide[:, j * 128 : (j + 1) * 128] * dch
                moved = term if j == 4 else pltpu.roll(term, ((BB + 16) + (j - 4)) % (BB + 16), 0)
                total = total + moved[8 : 8 + BB]
            dcv_ref[rows, lanes] = total.astype(BF)
        kern = kern_ref[rows, :]
        dot_rows = lane_groups(kern * d_kern, jnp.add)
        d_logits = (kern * (d_kern - dot_rows)).astype(BF)
        q = q_ref[rows, :].astype(F32)
        ck = ck_ref[rows, :].astype(F32)
        mixed = (ck * q).astype(BF)
        acc_kern[...] += mm_tn(mixed, d_logits)
        d_mixed = mm_nt(d_logits, w_kern_ref[...])
        dq_ref[rows, :] = d_mixed * ck
        d_ck = (d_mixed * q).astype(BF)
        acc_point[...] += mm_tn(spread_ref[rows, :], d_ck)
        ds_pad[pl.ds(r + 8, BB), :] = mm_nt(d_ck, w_point_ref[...])
        return carry

    lax.fori_loop(0, SEQ // BB, back, 0)

    def depth(i, carry):
        r = pl.multiple_of(i * DB, DB)
        rows = pl.ds(r, DB)
        for b in range(WIDTH // 128):
            lanes = slice(b * 128, (b + 1) * 128)
            dsh = ds_pad[pl.ds(r, (DB + 16)), lanes]
            tap = lambda j: w_depth_ref[j : j + 1, lanes]
            shifted = [dsh] + [pltpu.roll(dsh, s, 0) for s in (1, 2, 3)]
            low_part = sum(tap(s) * shifted[s] for s in range(4))
            mid_part = sum(tap(4 + s) * shifted[s] for s in range(4))
            high_part = tap(8) * dsh
            low_part = pltpu.roll(low_part, (DB + 16) - 4, 0)
            high_part = pltpu.roll(high_part, 4, 0)
            taps = (low_part + mid_part + high_part)[8 : 8 + DB]
            din_ref[rows, lanes] = (taps + first_ref[rows, lanes]).astype(BF)
            xs = x_pad[pl.ds(r + 8, DB), lanes]
            far_low = [pltpu.roll(shifted[s], (DB + 16) - 4, 0) for s in range(4)]
            far_high = pltpu.roll(dsh, 4, 0)
            for j in range(KER):
                src = far_low[j] if j < 4 else (shifted[j - 4] if j < 8 else far_high)
                acc_depth[j, :, lanes] += fold_rows(src[8 : 8 + DB] * xs)
        return carry

    lax.fori_loop(0, SEQ // DB, depth, 0)

    @pl.when(step == last)
    def _():
        dpoint_ref[...] = acc_point[...]
        dkern_ref[...] = acc_kern[...]
        ddepth_ref[...] = jnp.sum(acc_depth[...], 1)


def conv_back(dctx, kern, proj, ck, spread, inputs, d_first_in, w_depth, w_point, w_kern):
    rows = inputs.shape[0]
    block = lambda n: pl.BlockSpec((SEQ, n), lambda s: (s, 0))
    at = lambda c: pl.BlockSpec((SEQ, ATT), lambda s: (s, c))
    return pl.pallas_call(
        conv_back_kernel,
        grid=(rows // SEQ,),
        in_specs=[
            at(1), block(128), at(0), at(3), block(ATT), block(WIDTH), block(WIDTH), block(WIDTH),
            whole((KER, WIDTH)), whole((WIDTH, ATT)), whole((ATT, 128)),
        ],
        out_specs=[
            block(ATT), block(ATT), block(WIDTH), whole_out((WIDTH, ATT)), whole_out((ATT, 128)),
            whole_out((KER, WIDTH)),
        ],
        out_shape=[
            jax.ShapeDtypeStruct((rows, ATT), F32),
            jax.ShapeDtypeStruct((rows, ATT), BF),
            jax.ShapeDtypeStruct((rows, WIDTH), BF),
            jax.ShapeDtypeStruct((WIDTH, ATT), F32),
            jax.ShapeDtypeStruct((ATT, 128), F32),
            jax.ShapeDtypeStruct((KER, WIDTH), F32),
        ],
        scratch_shapes=[
            pltpu.VMEM((SEQ + 16, WIDTH), F32),
            pltpu.VMEM((SEQ + 16, ATT), F32),
            pltpu.VMEM((SEQ + 16, ATT), F32),
            pltpu.VMEM((SEQ + 16, 128), F32),
            pltpu.VMEM((SEQ + 16, WIDTH), F32),
            pltpu.VMEM((WIDTH, ATT), F32),
            pltpu.VMEM((ATT, 128), F32),
            pltpu.VMEM((KER, 8, WIDTH), F32),
        ],
        compiler_params=params(1),
        cost_estimate=cost(25e9, 30e6),
        name="conv_back",
    )(dctx, kern, proj, proj, ck, spread, inputs, d_first_in, w_depth, w_point, w_kern)


def attend_back_kernel(
    q_ref, k_ref, v_ref, p_ref, o_ref, inv_ref, datt_ref, dqc_ref, dq_ref, dk_ref, dv_ref
):
    scale = HEAD**-0.5
    v = v_ref[...]
    d_att = datt_ref[...].astype(F32) * inv_ref[...]
    o = o_ref[...].astype(F32)
    q_all = q_ref[...].astype(F32) * scale
    k_all = k_ref[...].astype(F32) * scale
    dq, dk_t, dv_t = dqc_ref[...], 0.0, 0.0
    for head in (0, 1):
        mine = own_lanes(SEQ, head)
        da = jnp.where(mine, d_att, 0.0)
        dot_rows = jnp.sum(da * o, -1, keepdims=True)
        p = p_ref[0, head]
        ds = mm_nt(da.astype(BF), v)
        ds = (p.astype(F32) * (ds - dot_rows)).astype(BF)
        dq = dq + mm(ds, jnp.where(mine, k_all, 0.0).astype(BF))
        dk_t = dk_t + mm(jnp.where(mine, q_all, 0.0).T.astype(BF), ds)
        dv_t = dv_t + mm(da.T.astype(BF), p)
    dq_ref[...] = dq.astype(BF)
    dk_ref[...] = dk_t.T.astype(BF)
    dv_ref[...] = dv_t.T.astype(BF)


def attend_back(proj, probs, att, inv, dctx, dq_conv):
    rows = proj.shape[0]
    pairs = HEADS // 2
    col = lambda base: pl.BlockSpec((SEQ, 128), lambda s, p: (s, base + p))
    return pl.pallas_call(
        attend_back_kernel,
        grid=(rows // SEQ, pairs),
        in_specs=[
            col(0), col(pairs), col(2 * pairs),
            pl.BlockSpec((1, 2, SEQ, SEQ), lambda s, p: (s, p, 0, 0)),
            col(0), col(0), col(0), col(0),
        ],
        out_specs=[col(0)] * 3,
        out_shape=[jax.ShapeDtypeStruct((rows, ATT), BF)] * 3,
        compiler_params=params(2),
        cost_estimate=cost(30e9, 40e6),
        name="attend_back",
    )(proj, proj, proj, probs, att, inv, dctx, dq_conv)


WB = 512


def weight_kernel(core_ref, inp_ref, dq_ref, dk_ref, dv_ref, dcv_ref, point_ref, extra_ref, *refs):
    grad_refs, acc = refs[:-1], refs[-1]
    step = pl.program_id(0)
    last = pl.num_programs(0) - 1
    inp = inp_ref[...]

    @pl.when(step == 0)
    def _():
        acc[...] = jnp.zeros_like(acc)

    for n, ref in enumerate((dq_ref, dk_ref, dv_ref, dcv_ref)):
        acc[:, n * ATT : (n + 1) * ATT] += mm_tn(inp, ref[...])

    @pl.when(step == last)
    def _():
        for c, grad in enumerate(grad_refs):

            def emit(i, carry):
                owner = i
                if len(grad_refs) == 2:
                    owner = (i // 8) * 16 + (core_ref[0] ^ c) * 8 + i % 8
                rows = pl.ds(pl.multiple_of(owner * 24, 8), 24)
                o = acc[rows, :]
                cols = [o[:, n * ATT : (n + 1) * ATT] for n in range(4)]
                grad[i] = jnp.concatenate(cols + [point_ref[rows, :], extra_ref[owner]], 0).astype(BF)
                return carry

            lax.fori_loop(0, grad.shape[0], emit, 0)


def weight_grad(inputs, dq, dk, dv, dcv, d_point, extra, core=None):
    rows = inputs.shape[0]
    block = lambda n: pl.BlockSpec((WB, n), lambda s: (s, 0))
    shapes = [(32, 128, LANES)] if core is None else [(16, 128, LANES)] * 2
    core = jnp.zeros((1,), jnp.int32) if core is None else core
    return pl.pallas_call(
        weight_kernel,
        grid=(rows // WB,),
        in_specs=[pl.BlockSpec(memory_space=pltpu.SMEM), block(WIDTH)]
        + [block(ATT)] * 4
        + [whole(d_point.shape), whole(extra.shape)],
        out_specs=[whole_out(s) for s in shapes],
        out_shape=[jax.ShapeDtypeStruct(s, BF) for s in shapes],
        scratch_shapes=[pltpu.VMEM((WIDTH, 4 * ATT), F32)],
        compiler_params=params(1),
        cost_estimate=cost(12e9, 12e6),
        name="weight_grad",
    )(core, inputs, dq, dk, dv, dcv, d_point, extra)


LC = 512
STEPS = SEQ // LC


def leave_kernel(
    dq_ref, dk_ref, dv_ref, dcv_ref, rest_ref, mask_ref, to_ref, w_in_ref, out_ref, moved, kept
):
    step = pl.program_id(1)
    rows = pl.ds(pl.multiple_of((step % STEPS) * LC, LC), LC)

    @pl.when(step < STEPS)
    def _():
        d_proj = jnp.concatenate([dq_ref[...], dk_ref[...], dv_ref[...], dcv_ref[...]], 1)
        total = mm_nt(d_proj, w_in_ref[...]) + rest_ref[...].astype(F32)
        moved[rows, :] = total.astype(BF)
        kept[rows, :] = jnp.where(mask_ref[...] == 1, 0.0, total)

    @pl.when(step >= STEPS)
    def _():
        target = lax.broadcasted_iota(jnp.int32, (LC, SEQ), 0) + (step - STEPS) * LC
        hot = (target == to_ref[0]).astype(F32).astype(BF)
        out_ref[...] = kept[rows, :] + mm(hot, moved[...])


def leave(dq, dk, dv, dcv, d_rest, mask_col, to_row, w_in):
    rows = dq.shape[0]
    block = lambda n: pl.BlockSpec((LC, n), lambda s, i: (s * STEPS + jnp.minimum(i, STEPS - 1), 0))
    return pl.pallas_call(
        leave_kernel,
        grid=(rows // SEQ, 2 * STEPS),
        in_specs=[block(ATT)] * 4
        + [block(WIDTH), block(1), pl.BlockSpec((1, 1, SEQ), lambda s, i: (s, 0, 0)), whole((WIDTH, 4 * ATT))],
        out_specs=pl.BlockSpec((LC, WIDTH), lambda s, i: (s * STEPS + jnp.maximum(i - STEPS, 0), 0)),
        out_shape=jax.ShapeDtypeStruct((rows, WIDTH), F32),
        scratch_shapes=[pltpu.VMEM((SEQ, WIDTH), BF), pltpu.VMEM((SEQ, WIDTH), F32)],
        compiler_params=params(2),
        cost_estimate=cost(15e9, 30e6),
        name="leave",
    )(dq, dk, dv, dcv, d_rest, mask_col, to_row, w_in)


def pack_taps(kernel_full):
    by_tap = kernel_full.reshape(ATT, HEADS, KER).transpose(0, 2, 1)
    return jnp.pad(by_tap, ((0, 0), (0, 16 - KER), (0, 8 - HEADS))).reshape(ATT, 128)


def unpack_taps(packed):
    return packed.reshape(ATT, 16, 8)[:, :KER, :HEADS].transpose(0, 2, 1).reshape(ATT, HEADS * KER)


def per_device(
    tokens,
    masked,
    replace_ids,
    in_weight,
    depth_weight,
    point_weight,
    kernel_weight,
    out_weight,
    gain_one,
    shift_one,
    ffn_in,
    feedforward_output,
    gain_two,
    shift_two,
    cotangent,
):
    rows = tokens.shape[0]
    seqs = rows // SEQ
    dp, fsdp = lax.axis_size("dp"), lax.axis_size("fsdp")
    devices = dp * fsdp
    near = dp == NEAR["dp"] and fsdp == NEAR["fsdp"]
    own, hid = in_weight.shape[0], ffn_in.shape[2]
    n_depth, n_kern, n_vec = KER * own, kernel_weight.size, 4 * own
    hit = masked == 1
    here = jnp.arange(rows, dtype=jnp.int32) % SEQ
    pick = jnp.where(hit, replace_ids, here)[:, None]
    to_row = jnp.where(hit, replace_ids, -1).reshape(seqs, 1, SEQ)
    scale = 1.0 / math.sqrt(rows * devices)

    vec_own = jnp.stack([gain_one, shift_one, gain_two, shift_two])
    small_own = as_rows(
        jnp.concatenate([depth_weight.reshape(-1), kernel_weight.reshape(-1), vec_own.reshape(-1)])
    )
    head_own = jnp.concatenate([in_weight.reshape(own, 4, ATT).transpose(1, 0, 2), point_weight[None]])
    mid_own = jnp.concatenate(
        [
            out_weight.reshape(own, 2, ATT).transpose(1, 0, 2).reshape(-1, LANES),
            ffn_in.transpose(0, 2, 1).reshape(-1, LANES),
            feedforward_output.reshape(-1, LANES),
        ]
    )
    if near:
        me = place().astype(jnp.int32).reshape(1)
        pair, core = me // 2, me // CORE_BIT % 2
        slab, pick = tie(pair_slab(head_own, small_own), pick)
        slabs = [slab] + [hop(slab, k * Z_BIT) for k in (1, 2, 3)]
        across = [hop(slab, X_BIT)]
        inputs, (across, slabs[1:]) = tie(pick_rows(pick, tokens), (across, slabs[1:]))
        slabs[1:], mid_own = tie(slabs[1:], mid_own)
        mid = lax.all_gather(mid_own, AXES, axis=0)
        slabs = slabs + across + [hop(slab, X_BIT) for slab in slabs[1:]]
        slabs = slabs + [hop(slab, CORE_BIT) for slab in slabs]
        small_all = small_rows(slabs, pair)
    else:
        small_all = lax.all_gather(small_own, AXES, axis=0).reshape(devices, -1)
        w_all = lax.all_gather(head_own, AXES, axis=1, tiled=True).reshape(5, 16, 48, LANES)
        slabs = [w_all[:, bits].reshape(-1, LANES) for bits in SLAB_BITS]
        mid = lax.all_gather(mid_own, AXES, axis=0)
        w_out = mid[:, : 2 * own].reshape(devices, 2, own, ATT).transpose(1, 0, 2, 3)
        w_out = w_out.reshape(2, BLOCKS, 24, ATT).transpose(1, 0, 2, 3).reshape(BLOCKS, 48, ATT)
        w_ffn = mid[:, 2 * own :].reshape(devices, 4, hid, ATT).transpose(1, 0, 2, 3)
        w_ffn = w_ffn.reshape(4, BLOCKS, 48, ATT).transpose(1, 0, 2, 3).reshape(BLOCKS, 192, ATT)
        mid = jnp.concatenate([w_out, w_ffn], 1)
        pair, core = jnp.zeros((1,), jnp.int32), None
        inputs = pick_rows(pick, tokens)
    w_depth = small_all[:, :n_depth].reshape(devices, KER, own).transpose(1, 0, 2).reshape(KER, WIDTH)
    w_depth = w_depth.astype(F32)
    w_kern = pack_taps(small_all[:fsdp, n_depth : n_depth + n_kern].reshape(ATT, HEADS * KER))
    vecs = small_all[:, n_depth + n_kern :][:, :n_vec].reshape(devices, 4, own)
    vecs = vecs.transpose(1, 0, 2).reshape(4, WIDTH).astype(F32)

    proj, spread, ck, kern, conv, w_in, w_point = enter(inputs, pair, w_depth, w_kern, slabs)
    probs, att, inv = attend(proj)
    out, dctx, d_first_in, d_vecs, mid_grad = middle(att, conv, inputs, cotangent, mid, vecs)
    if near:
        mid_sum = lax.psum_scatter(mid_grad, AXES, scatter_dimension=0, tiled=True)[0]
    dq_conv, dcv, d_rest, d_point, d_kern, d_depth = conv_back(
        dctx, kern, proj, ck, spread, inputs, d_first_in, w_depth, w_point, w_kern
    )
    by_owner = lambda g: g.reshape(-1, devices, own).transpose(1, 0, 2).reshape(devices, -1)
    kern_by = jnp.tile(unpack_taps(d_kern).reshape(fsdp, -1), (dp, 1))
    small_grad = jnp.concatenate([by_owner(d_depth), kern_by, by_owner(d_vecs)], 1)
    small_grad = jnp.pad(small_grad, ((0, 0), (0, -small_grad.shape[1] % LANES)))
    small_grad = small_grad.reshape(devices, -1, LANES)
    dq, dk, dv = attend_back(proj, probs, att, inv, dctx, dq_conv)
    mask_col = masked[:, None]
    if near:
        mine, other = weight_grad(inputs, dq, dk, dv, dcv, d_point, small_grad, core)
        parts = fold_xy(me, mine, hop(other, CORE_BIT))
        parts = [parts[0]] + [hop(part, bit) for part, bit in zip(parts[1:], (Y_BIT, X_BIT, X_BIT + Y_BIT))]
        parts[0], dq = tie(parts[0], dq)
        d_tokens = leave(dq, dk, dv, dcv, d_rest, mask_col, to_row, w_in)
        d_tokens, parts = tie(d_tokens, parts)
        parts = fold_z(me, parts)
        parts = [parts[0]] + [hop(parts[k], k * Z_BIT) for k in (1, 2, 3)]
        parts[0], mid_sum = tie(parts[0], mid_sum)
        d_out, d_up, d_down = finish_mid(scale, mid_sum)
        d_up = d_up.transpose(0, 2, 1)
        parts[3], d_out = tie(parts[3], d_out)
        small_shapes = [(KER, own), kernel_weight.shape, (4, own)]
        d_in, d_point, depth_sum, kern_sum, vec_sum = finish(scale, parts, small_shapes)
    else:
        (grads,) = weight_grad(inputs, dq, dk, dv, dcv, d_point, jnp.zeros((32, 8, LANES), F32))
        d_in = grads[:, :96].reshape(32, 4, 24, ATT).transpose(0, 2, 1, 3).reshape(devices, -1, LANES)
        d_point = grads[:, 96:120].reshape(devices, -1, LANES)
        w_out = mid_grad[:, :48].reshape(BLOCKS, 2, 24, ATT).transpose(0, 2, 1, 3).reshape(devices, -1, LANES)
        w_ffn = mid_grad[:, 48:].reshape(BLOCKS, 4, 48, ATT).transpose(1, 0, 2, 3)
        w_ffn = w_ffn.reshape(4, devices, hid, ATT).transpose(1, 0, 2, 3).reshape(devices, -1, LANES)
        packed = jnp.concatenate([w_out, w_ffn, d_in, d_point, small_grad.astype(BF)], 1)
        total = lax.psum_scatter(packed, AXES, scatter_dimension=0, tiled=True)[0].astype(F32) * scale
        cuts = [2 * own, 2 * own + 2 * hid, 2 * own + 4 * hid, 6 * own + 4 * hid, 7 * own + 4 * hid]
        d_out, d_up, d_down, d_in, d_point, small_sum = jnp.split(total, cuts)
        d_out, d_in, small_sum = d_out.reshape(own, WIDTH), d_in.reshape(own, 4 * ATT), small_sum.reshape(-1)
        d_up, d_down = d_up.reshape(2, hid, ATT).transpose(0, 2, 1), d_down.reshape(2, hid, ATT)
        d_tokens = leave(dq, dk, dv, dcv, d_rest, mask_col, to_row, w_in)
        depth_sum = small_sum[:n_depth].reshape(KER, own)
        kern_sum = small_sum[n_depth : n_depth + n_kern].reshape(kernel_weight.shape)
        vec_sum = small_sum[n_depth + n_kern :][:n_vec].reshape(4, own)
    return (
        out,
        d_tokens,
        d_in,
        depth_sum,
        d_point,
        kern_sum,
        d_out,
        vec_sum[0],
        vec_sum[1],
        d_up,
        d_down,
        vec_sum[2],
        vec_sum[3],
    )


def solution(mesh):
    return jax.shard_map(
        per_device,
        mesh=mesh,
        in_specs=(
            P(("dp", "fsdp"), None),
            P(("dp", "fsdp")),
            P(("dp", "fsdp")),
            P(("dp", "fsdp"), None),
            P(None, ("dp", "fsdp")),
            P(("dp", "fsdp"), None),
            P("fsdp", None),
            P(("dp", "fsdp"), None),
            P(("dp", "fsdp")),
            P(("dp", "fsdp")),
            P(None, None, ("dp", "fsdp")),
            P(None, ("dp", "fsdp"), None),
            P(("dp", "fsdp")),
            P(("dp", "fsdp")),
            P(("dp", "fsdp"), None),
        ),
        out_specs=(
            P(("dp", "fsdp"), None),
            P(("dp", "fsdp"), None),
            P(("dp", "fsdp"), None),
            P(None, ("dp", "fsdp")),
            P(("dp", "fsdp"), None),
            P("fsdp", None),
            P(("dp", "fsdp"), None),
            P(("dp", "fsdp")),
            P(("dp", "fsdp")),
            P(None, None, ("dp", "fsdp")),
            P(None, ("dp", "fsdp"), None),
            P(("dp", "fsdp")),
            P(("dp", "fsdp")),
        ),
        check_vma=False,
    )
```
